32 devices in a mesh: rep: 8 (over y, x, core), shard: 4 (over z).
Axes of the slice: x: 2, y: 2, z: 4, core: 2. Of those that a mesh axis runs over, the one named last changes fastest.
Arguments:
- tokens: bfloat16 [16384, 1024], P(('rep', 'shard')), may hold values from -6 to 6
- doc_ids: int32 [16384], P(('rep', 'shard')), may hold values from 0 to 511, as said below
- routes: int32 [16384, 8], P(('rep', 'shard')), may hold values from 0 to 15, all different within a row; in each aligned block of 512 rows (0 to 511, 512 to 1023, ...) at most 288 rows name the same one
- norm_in_gain: bfloat16 [1024], P('shard'), may hold values from 0.5 to 1.5
- w_query: bfloat16 [1024, 1024], P('shard'), may hold values from -0.1875 to 0.1875
- w_key: bfloat16 [1024, 512], P('shard'), may hold values from -0.1875 to 0.1875
- w_value: bfloat16 [1024, 512], P('shard'), may hold values from -0.1875 to 0.1875
- w_out: bfloat16 [1024, 1024], P('shard'), may hold values from -0.75 to 0.75
- norm_mid_gain: bfloat16 [1024], P('shard'), may hold values from 0.5 to 1.5
- w_router: bfloat16 [1024, 16], P('shard'), may hold values from -0.09375 to 0.09375
- w_expert_in: bfloat16 [16, 1024, 1024], P('shard'), may hold values from -0.1875 to 0.1875
- w_expert_down: bfloat16 [16, 512, 1024], P('shard'), may hold values from -0.75 to 0.75
- cotangent: bfloat16 [16384, 1024], P(('rep', 'shard')), may hold values from -6 to 6
Outputs:
- mixed: bfloat16 [16384, 1024], P(('rep', 'shard'))
- grad_tokens: float32 [16384, 1024], P(('rep', 'shard'))
- grad_norm_in_gain: float32 [1024], P('shard')
- grad_w_query: float32 [1024, 1024], P('shard')
- grad_w_key: float32 [1024, 512], P('shard')
- grad_w_value: float32 [1024, 512], P('shard')
- grad_w_out: float32 [1024, 1024], P('shard')
- grad_norm_mid_gain: float32 [1024], P('shard')
- grad_w_router: float32 [1024, 16], P('shard')
- grad_w_expert_in: float32 [16, 1024, 1024], P('shard')
- grad_w_expert_down: float32 [16, 512, 1024], P('shard')
The draws below stay inside these ranges and needn't reach their ends.
Inputs may be any that keep to these rules, and one draw needn't show every extreme that they name: `doc_ids`: in every aligned block of 512 tokens the numbers start at 0 and rise by 0 or 1 from token to token. Among the 512 tokens of one device, no expert is named by more than 288 routes.
All inputs are finite; a program needn't handle non-finite values.
Results may differ from the reference program's by a relative error of at most 0.019.
Values may be sent and summed in bfloat16 or wider, within the bound.
A program may use at most 320 MiB of HBM per device.

```python
import math
import jax
import jax.numpy as jnp
import numpy as np
from jax import lax

D = 1024
HEADS = 16
KV_HEADS = 8
HEAD_DIM = 64
FF = 512
EXPERTS = 16
TOP_K = 8
TOK_DEV = 512
CAP = 288
TOKENS = 16384


def draw_doc_ids(key, part):
    block_count = TOKENS // TOK_DEV
    key_rate, key_single, key_many, key_bits = jax.random.split(key, 4)
    divisors = jnp.array([2, 8, 32, 128], dtype=jnp.int32)
    row_divisor = divisors[jax.random.randint(key_rate, (block_count,), 0, 4)]
    single_row = jax.random.randint(key_single, (), 0, block_count)
    many_row = (single_row + 1 + jax.random.randint(key_many, (), 0, block_count - 1)) % block_count
    row_index = jnp.arange(block_count, dtype=jnp.int32)
    row_divisor = jnp.where(row_index == many_row, 1, row_divisor)
    random_bits = jax.random.randint(key_bits, (block_count, TOK_DEV), 0, 1 << 20)
    place_row = jnp.arange(TOK_DEV, dtype=jnp.int32)[None, :]
    opening = (random_bits % row_divisor[:, None] == 0) | (place_row == 0)
    opening = jnp.where(row_index[:, None] == single_row, place_row == 0, opening)
    return (jnp.cumsum(opening.astype(jnp.int32), axis=1) - 1).astype(jnp.int32).reshape(-1)


def block_scale(own_key, dims, pieces, smallest, high):
    gain = 1.0
    for axis_at, parts in pieces:
        draws = jax.random.uniform(jax.random.fold_in(jax.random.fold_in(own_key, 6), axis_at), (parts,), jnp.float32, smallest / len(pieces), high / len(pieces))
        gain = gain * jnp.repeat(jnp.exp(draws), dims[axis_at] // parts).reshape((-1,) + (1,) * (len(dims) - 1 - axis_at))
    return gain


def routed_block(rng, own, number, rows, amount, top, reach, lean):
    order = jax.random.permutation(rng, amount)
    packed, usual = portions_of(amount, rows * top, reach, lean, True), portions_of(amount, rows * top, reach, lean, False)
    places = jnp.arange(amount)

    def named(tallies, turn):
        used = int((tallies > 0).sum())
        fixed = max(1, used // 4)
        shifted = fixed + (places - fixed + turn * (used - fixed)) % max(1, amount - fixed)
        return jnp.zeros((amount,), jnp.int32).at[order[jnp.where(places < fixed, places, shifted)]].set(jnp.asarray(tallies, jnp.int32))

    tallies = jnp.where(number % 4 == 0, named(packed, number // 4), named(usual, number - number // 4 - 1))
    mixed = jax.random.permutation(jax.random.fold_in(own, 3), amount)
    giver, sink = mixed[0:amount // 2 * 2:2], mixed[1:amount // 2 * 2:2]
    slack = jnp.minimum(tallies[giver] - 1, reach - tallies[sink]) // 2
    slack = jnp.where((giver == order[0]) | (sink == order[0]) | (tallies[sink] == 0), 0, jnp.maximum(slack, 0))
    shifted = jax.random.randint(jax.random.fold_in(own, 4), (amount // 2,), 0, 1 << 20) % (slack + 1)
    tallies = tallies.at[giver].add(-shifted).at[sink].add(shifted)
    items = jnp.searchsorted(jnp.cumsum(tallies), jnp.arange(rows * top), side="right").astype(jnp.int32)
    table = items.reshape(top, rows).T
    table = table[jax.random.permutation(jax.random.fold_in(own, 1), rows)]
    turn = jax.random.randint(jax.random.fold_in(own, 2), (rows, 1), 0, top)
    return jnp.take_along_axis(table, (jnp.arange(top)[None, :] + turn) % top, axis=1)


def portions_of(number_of, total, reach, skew, full):
    loads = [(1 << 20) // math.isqrt(rank ** skew) + 1 for rank in range(1, number_of + 1)]
    largest = reach if full else min(reach, max(-(-total // number_of), total * loads[0] // sum(loads)))
    least = 1 if total - largest >= number_of - 1 else 0
    counts, surplus = [largest] + [least] * (number_of - 1), total - largest - least * (number_of - 1)
    while surplus > 0:
        movable = [i for i in range(1, number_of) if counts[i] < largest] or [i for i in range(1, number_of) if counts[i] < reach]
        pool, budget = sum([loads[i] for i in movable]), surplus
        for i in movable:
            more = min(reach - counts[i], max(1, budget * loads[i] // pool), surplus)
            counts[i] = counts[i] + more
            surplus = surplus - more
    return np.array(counts)


def normal_values(rng, shape, deviation, bound, cuts=(), kind=jnp.bfloat16):
    level = block_scale(rng, shape, cuts, -0.22, 0.18) if cuts else 1.0
    result = jax.random.normal(rng, shape, jnp.float32) * deviation * level
    return jnp.minimum(jnp.maximum(result, -bound), bound).astype(kind)


def setup_inputs(seed: int = 0) -> dict:
    streams_of = jax.random.split(jax.random.key(seed), 14)
    tokens = normal_values(streams_of[0], (TOKENS, D), 1.0, 6.0, ((0, 32),))
    doc_ids = draw_doc_ids(jax.random.fold_in(streams_of[13], 71), 0)
    routes_keys = jax.random.split(jax.random.fold_in(streams_of[2], 1), TOKENS // TOK_DEV)
    routes_turns = jax.random.permutation(jax.random.fold_in(streams_of[2], 3), TOKENS // TOK_DEV)
    routes = jax.vmap(lambda own, number: routed_block(jax.random.fold_in(streams_of[2], 2), own, number, TOK_DEV, EXPERTS, TOP_K, CAP, 0))(routes_keys, routes_turns).reshape((TOKENS, TOP_K))
    norm_in_gain = jnp.clip(1.0 + 0.1 * jax.random.normal(streams_of[3], (D,), jnp.float32), 0.5, 1.5).astype(jnp.bfloat16)
    w_query = normal_values(streams_of[4], (D, HEADS * HEAD_DIM), D ** -0.5, 0.1875, ((0, 4),))
    w_key = normal_values(streams_of[5], (D, KV_HEADS * HEAD_DIM), D ** -0.5, 0.1875, ((0, 4),))
    w_value = normal_values(streams_of[6], (D, KV_HEADS * HEAD_DIM), D ** -0.5, 0.1875, ((0, 4),))
    w_out = normal_values(streams_of[7], (HEADS * HEAD_DIM, D), (D // 16) ** -0.5, 0.75, ((0, 4),))
    norm_mid_gain = jnp.clip(1.0 + 0.1 * jax.random.normal(streams_of[8], (D,), jnp.float32), 0.5, 1.5).astype(jnp.bfloat16)
    w_router = normal_values(streams_of[9], (D, EXPERTS), (4 * D) ** -0.5, 0.09375, ((0, 4),))
    w_expert_in = normal_values(streams_of[10], (EXPERTS, D, 2 * FF), D ** -0.5, 0.1875, ((0, 4),))
    w_expert_down = normal_values(streams_of[11], (EXPERTS, FF, D), (FF // 8) ** -0.5, 0.75, ((0, 4),))
    cotangent = normal_values(streams_of[12], (TOKENS, D), 1.0, 6.0, ((0, 32),))
    return {"tokens": tokens, "doc_ids": doc_ids, "routes": routes, "norm_in_gain": norm_in_gain, "w_query": w_query, "w_key": w_key, "w_value": w_value, "w_out": w_out, "norm_mid_gain": norm_mid_gain, "w_router": w_router, "w_expert_in": w_expert_in, "w_expert_down": w_expert_down, "cotangent": cotangent}


highest = lax.Precision.HIGHEST
epsilon = 1e-06
rope_base = 10000.0
masked_score = -1e+30

@jax.custom_vjp
def low(v):
    return lax.optimization_barrier(v.astype(jnp.bfloat16)).astype(jnp.float32)

@jax.custom_vjp
def low_back(v):
    return v

def low_keep(v):
    return (low(v), None)

def low_pass(kept, grad):
    return (grad,)

def back_keep(v):
    return (v, None)

def back_low(kept, grad):
    return (low(grad),)
low.defvjp(low_keep, low_pass)
low_back.defvjp(back_keep, back_low)

def positions(doc_rows):
    row_count = doc_rows.shape[0]
    places = jnp.arange(row_count, dtype=jnp.int32)
    opening = jnp.concatenate([jnp.ones((1,), dtype=jnp.bool_), doc_rows[1:] != doc_rows[:-1]])
    begins = lax.cummax(jnp.where(opening, places, 0), axis=0)
    return (places - begins).astype(jnp.int32)

def rotary_tables(places, head_width):
    half_width = head_width // 2
    frequencies = jnp.power(rope_base, -2.0 * jnp.arange(half_width, dtype=jnp.float32) / head_width)
    angles = places.astype(jnp.float32)[:, None] * frequencies[None, :]
    return (jnp.cos(angles)[:, None, :], jnp.sin(angles)[:, None, :])

def rotate(values, cosine, sine_table):
    half_width = values.shape[-1] // 2
    former, latter = (values[..., :half_width], values[..., half_width:])
    return jnp.concatenate([former * cosine - latter * sine_table, latter * cosine + former * sine_table], axis=-1)

def rms_scale(values):
    return lax.rsqrt(lax.optimization_barrier(jnp.mean(values * values, axis=-1, keepdims=True)) + epsilon)

def dispatch(route_rows):
    flat_routes = route_rows.reshape(-1)
    route_count = flat_routes.shape[0]
    onehot = (flat_routes[:, None] == jnp.arange(EXPERTS, dtype=jnp.int32)[None, :]).astype(jnp.int32)
    expert_rank = lax.optimization_barrier(jnp.sum((jnp.cumsum(onehot, axis=0) - 1) * onehot, axis=1))
    slot_index = (flat_routes * CAP + expert_rank).astype(jnp.int32)
    source = jnp.full((EXPERTS * CAP,), route_count, dtype=jnp.int32).at[slot_index].set(jnp.arange(route_count, dtype=jnp.int32))
    filled = source < route_count
    token_of = jnp.where(filled, source // TOP_K, 0).astype(jnp.int32)
    route_of = jnp.where(filled, source, 0).astype(jnp.int32)
    return (token_of, route_of, filled)

def layer_block(params, inputs, doc_rows, route_rows):
    gain_in, query_w, key_w, value_w, out_w, gain_mid, router_w, expert_in_w, expert_down_w = params
    row_count = inputs.shape[0]
    groups = HEADS // KV_HEADS
    cosine, sine_table = rotary_tables(positions(doc_rows), HEAD_DIM)
    first = low(inputs * rms_scale(inputs) * gain_in)
    query_pre = low_back(jnp.dot(first, query_w, precision=highest))
    key_pre = low_back(jnp.dot(first, key_w, precision=highest))
    value_rows = low(low_back(jnp.dot(first, value_w, precision=highest))).reshape(row_count, KV_HEADS, HEAD_DIM)
    query_rows = low(rotate(query_pre.reshape(row_count, HEADS, HEAD_DIM), cosine, sine_table)).reshape(row_count, KV_HEADS, groups, HEAD_DIM)
    key_rows = low(rotate(key_pre.reshape(row_count, KV_HEADS, HEAD_DIM), cosine, sine_table))
    scores = jnp.einsum('qgrd,kgd->grqk', query_rows, key_rows, precision=highest) * HEAD_DIM ** (-0.5)
    places = jnp.arange(row_count, dtype=jnp.int32)
    allowed = (doc_rows[:, None] == doc_rows[None, :]) & (places[:, None] >= places[None, :])
    scores = low_back(jnp.where(allowed, scores, masked_score))
    row_max = lax.optimization_barrier(jnp.max(scores, axis=-1, keepdims=True))
    exponent = jnp.exp(scores - row_max)
    probs = exponent / lax.optimization_barrier(jnp.sum(exponent, axis=-1, keepdims=True))
    attended = jnp.einsum('grqk,kgd->qgrd', low(probs), value_rows, precision=highest).reshape(row_count, HEADS * HEAD_DIM)
    attended = low_back(low(attended))
    middle = inputs + low_back(jnp.dot(attended, out_w, precision=highest))
    second = low(middle * rms_scale(middle) * gain_mid)
    logits = low_back(jnp.dot(second, router_w, precision=highest))
    chosen = jnp.take_along_axis(logits, route_rows, axis=1)
    chosen_max = lax.optimization_barrier(jnp.max(chosen, axis=1, keepdims=True))
    gate_exp = jnp.exp(chosen - chosen_max)
    gates = gate_exp / lax.optimization_barrier(jnp.sum(gate_exp, axis=1, keepdims=True))
    token_of, route_of, filled = dispatch(route_rows)
    fill_mask = filled.astype(jnp.float32)
    expert_rows = (second[token_of] * fill_mask[:, None]).reshape(EXPERTS, CAP, D)
    both_parts = low_back(jnp.einsum('ecd,edf->ecf', expert_rows, expert_in_w, precision=highest))
    hidden = low(jax.nn.silu(both_parts[..., :FF]) * both_parts[..., FF:])
    expert_out = low_back(jnp.einsum('ecf,efd->ecd', hidden, expert_down_w, precision=highest)).reshape(EXPERTS * CAP, D)
    slot_gates = gates.reshape(-1)[route_of] * fill_mask
    combined = jax.ops.segment_sum(expert_out * slot_gates[:, None], token_of, num_segments=row_count)
    return middle + combined

def reference(tokens, doc_ids, routes, norm_in_gain, w_query, w_key, w_value, w_out, norm_mid_gain, w_router, w_expert_in, w_expert_down, cotangent):
    block_count = tokens.shape[0] // TOK_DEV
    params = (norm_in_gain.astype(jnp.float32), w_query.astype(jnp.float32), w_key.astype(jnp.float32), w_value.astype(jnp.float32), w_out.astype(jnp.float32), norm_mid_gain.astype(jnp.float32), w_router.astype(jnp.float32), w_expert_in.astype(jnp.float32), w_expert_down.astype(jnp.float32))
    inputs = tokens.astype(jnp.float32).reshape(block_count, TOK_DEV, D)
    doc_blocks = doc_ids.reshape(block_count, TOK_DEV)
    route_blocks = routes.reshape(block_count, TOK_DEV, TOP_K)

    def forward(weights_all, inputs_all):

        def one_block(block_items):
            return layer_block(weights_all, block_items[0], block_items[1], block_items[2])
        return lax.map(jax.checkpoint(one_block), (inputs_all, doc_blocks, route_blocks))
    outputs, pullback = jax.vjp(forward, params, inputs)
    grad_params, grad_inputs = pullback(cotangent.astype(jnp.float32).reshape(block_count, TOK_DEV, D))
    return (outputs.reshape(-1, D).astype(jnp.bfloat16), grad_inputs.reshape(-1, D), grad_params[0], grad_params[1], grad_params[2], grad_params[3], grad_params[4], grad_params[5], grad_params[6], grad_params[7], grad_params[8])
```

```python
import jax
import jax.numpy as jnp
from jax import lax
from jax.experimental import pallas as pl
from jax.experimental.pallas import tpu as pltpu
from jax.sharding import PartitionSpec as P

HEADS = 16
KV_HEADS = 8
HEAD_DIM = 64
EXPERTS = 16
PAD = 128
VMEM_BYTES = 54 * 2**20


epsilon = 1e-06
rope_base = 10000.0
masked_score = -1e30


def positions(doc_rows):
    row_count = doc_rows.shape[0]
    places = jnp.arange(row_count, dtype=jnp.int32)
    begins = jnp.sum((doc_rows[None, :] < doc_rows[:, None]).astype(jnp.int32), axis=1)
    return places - begins


def rotary_tables(places, head_width):
    half_width = head_width // 2
    frequencies = jnp.power(
        rope_base, -2.0 * jnp.arange(half_width, dtype=jnp.float32) / head_width
    )
    angles = places.astype(jnp.float32)[:, None] * frequencies[None, :]
    return (jnp.cos(angles)[:, None, :], jnp.sin(angles)[:, None, :])


def rotate(values, cosine, sine_table):
    half_width = values.shape[-1] // 2
    former, latter = (values[..., :half_width], values[..., half_width:])
    return jnp.concatenate(
        [former * cosine - latter * sine_table, latter * cosine + former * sine_table], axis=-1
    )


def unrotate(values, cosine, sine_table):
    half_width = values.shape[-1] // 2
    former, latter = (values[..., :half_width], values[..., half_width:])
    return jnp.concatenate(
        [former * cosine + latter * sine_table, latter * cosine - former * sine_table], axis=-1
    )


def normalize(values):
    row_scale = lax.rsqrt(jnp.mean(values * values, axis=-1, keepdims=True) + epsilon)
    return (values * row_scale, row_scale)


def norm_back(grad_scaled, normed, row_scale, gain_full):
    grad_normed = grad_scaled * gain_full
    inner = jnp.mean(grad_normed * normed, axis=-1, keepdims=True)
    return (row_scale * (grad_normed - normed * inner), jnp.sum(grad_scaled * normed, axis=0))


def score_block(query_blk, key_part, doc_query, doc_key):
    scores = jnp.einsum(
        "qgrd,kgd->grqk", query_blk, key_part, preferred_element_type=jnp.float32
    ) * query_blk.shape[-1] ** (-0.5)
    query_place = jnp.arange(query_blk.shape[0], dtype=jnp.int32)
    key_place = jnp.arange(key_part.shape[0], dtype=jnp.int32)
    allowed = (doc_query[:, None] == doc_key[None, :]) & (
        query_place[:, None] >= key_place[None, :]
    )
    return jnp.where(allowed, scores, masked_score)


def attend(query_rows, key_rows, value_rows, doc_rows):
    scores = score_block(query_rows, key_rows, doc_rows, doc_rows)
    row_max = jnp.max(scores, axis=-1, keepdims=True)
    exponent = jnp.exp(scores - row_max)
    row_total = jnp.sum(exponent, axis=-1, keepdims=True)
    probs_low = (exponent / row_total).astype(jnp.bfloat16)
    outputs = jnp.einsum(
        "grqk,kgd->qgrd", probs_low, value_rows, preferred_element_type=jnp.float32
    ).astype(jnp.bfloat16)
    lse_parts = row_max + jnp.log(row_total)
    return (outputs, lse_parts)


def attend_back(query_rows, key_rows, value_rows, doc_rows, log_sums, grad_att):
    row_count = query_rows.shape[0]
    block_rows = min(512, row_count)
    scale_factor = query_rows.shape[-1] ** (-0.5)
    grad_key = jnp.zeros(key_rows.shape, jnp.float32)
    grad_value = jnp.zeros(value_rows.shape, jnp.float32)
    scores = score_block(query_rows, key_rows, doc_rows, doc_rows)
    probs = jnp.exp(scores - log_sums)
    grad_probs = jnp.einsum(
        "qgrd,kgd->grqk", grad_att, value_rows, preferred_element_type=jnp.float32
    )
    inner = jnp.sum(probs * grad_probs, axis=-1, keepdims=True)
    grad_scores = (probs * (grad_probs - inner)).astype(jnp.bfloat16)
    query_parts = (
        jnp.einsum("grqk,kgd->qgrd", grad_scores, key_rows, preferred_element_type=jnp.float32)
        * scale_factor
    )
    grad_key = grad_key.at[:block_rows].add(
        jnp.einsum("grqk,qgrd->kgd", grad_scores, query_rows, preferred_element_type=jnp.float32)
        * scale_factor
    )
    grad_value = grad_value.at[:block_rows].add(
        jnp.einsum(
            "grqk,qgrd->kgd",
            probs.astype(jnp.bfloat16),
            grad_att,
            preferred_element_type=jnp.float32,
        )
    )
    return (query_parts, grad_key, grad_value)


MESH = pl.DeviceIdType.MESH
HALVES = 2


def bit_orders(reps):
    bits = reps.bit_length() - 1
    first = list(range(bits))
    return (first, first[:1] + first[1:][::-1])


def rep_place(rep_at, order):
    place = 0
    for bit in order:
        place = place * 2 + rep_at // 2**bit % 2
    return place


def partner(rep_at, bit):
    return rep_at + 2**bit * (1 - 2 * (rep_at // 2**bit % 2))


def halves_of(columns):
    tiles = columns // 128
    left = (tiles + 1) // 2 * 128
    return (pl.ds(0, left), pl.ds(left, columns - left))


def meet(rep_at, shard_at, reps, shard_count):
    barrier = pltpu.get_barrier_semaphore()
    bits = reps.bit_length() - 1
    for bit in range(bits):
        pl.semaphore_signal(
            barrier, inc=1, device_id=(partner(rep_at, bit), shard_at), device_id_type=MESH
        )
    for step in range(1, shard_count):
        pl.semaphore_signal(
            barrier,
            inc=1,
            device_id=(rep_at, (shard_at + step) % shard_count),
            device_id_type=MESH,
        )
    pl.semaphore_wait(barrier, bits + shard_count - 1)


def spread(out, orders, columns, rep_at, shard_at, sends, recvs):
    bits = len(orders[0])
    flying = [None] * HALVES
    for at in reversed(range(bits)):
        window = 2 ** (bits - 1 - at)
        for half in range(HALVES):
            order = orders[half]
            place = rep_place(rep_at, order)
            begin = place // window * window
            if flying[half] is not None:
                flying[half].wait()
            block = out.at[:, pl.ds(begin, window), :, columns[half]]
            flying[half] = pltpu.make_async_remote_copy(
                src_ref=block,
                dst_ref=block,
                send_sem=sends.at[half, at],
                recv_sem=recvs.at[half, at],
                device_id=(partner(rep_at, order[at]), shard_at),
                device_id_type=MESH,
            )
            flying[half].start()
    for half in range(HALVES):
        flying[half].wait()


def gather_kernel(reps, shard_count, piece, out, z_send, z_recv, sends, recvs):
    rep_at, shard_at = (lax.axis_index("rep"), lax.axis_index("shard"))
    orders = bit_orders(reps)
    columns = halves_of(piece.shape[-1])
    meet(rep_at, shard_at, reps, shard_count)
    flying = []
    for half in range(HALVES):
        place = rep_place(rep_at, orders[half])
        for step in range(1, shard_count):
            copy = pltpu.make_async_remote_copy(
                src_ref=piece.at[place, :, columns[half]],
                dst_ref=out.at[shard_at, place, :, columns[half]],
                send_sem=z_send.at[half, step - 1],
                recv_sem=z_recv.at[half, step - 1],
                device_id=(rep_at, (shard_at + step) % shard_count),
                device_id_type=MESH,
            )
            copy.start()
            flying.append(copy)
        out[shard_at, place, :, columns[half]] = piece[place, :, columns[half]]
    for copy in flying:
        copy.wait()
    spread(out, orders, columns, rep_at, shard_at, sends, recvs)


def gather_all(piece, reps, shard_count, number):
    own, width = piece.shape
    rows = own // reps
    bits = reps.bit_length() - 1
    out = pl.pallas_call(
        lambda *refs: gather_kernel(reps, shard_count, *refs),
        out_shape=jax.ShapeDtypeStruct((shard_count, reps, rows, width), piece.dtype),
        in_specs=[pl.BlockSpec(memory_space=pltpu.VMEM)],
        out_specs=pl.BlockSpec(memory_space=pltpu.VMEM),
        scratch_shapes=[
            pltpu.SemaphoreType.DMA((HALVES, shard_count)),
            pltpu.SemaphoreType.DMA((HALVES, shard_count)),
            pltpu.SemaphoreType.DMA((HALVES, bits)),
            pltpu.SemaphoreType.DMA((HALVES, bits)),
        ],
        compiler_params=pltpu.CompilerParams(
            collective_id=number, has_side_effects=True, vmem_limit_bytes=VMEM_BYTES
        ),
        cost_estimate=pl.CostEstimate(
            flops=0, bytes_accessed=16 * shard_count * own * width, transcendentals=0
        ),
    )(piece.reshape(reps, rows, width))
    return out.reshape(shard_count * own, width)


def reduce_kernel(reps, shard_count, parts, out, *scratch):
    bits = reps.bit_length() - 1
    f32 = jnp.float32
    landed = [scratch[half * bits : (half + 1) * bits] for half in range(HALVES)]
    rest = scratch[HALVES * bits :]
    if shard_count > 1:
        z_land, (z_send, z_recv) = (rest[:HALVES], rest[HALVES : HALVES + 2])
        rest = rest[HALVES + 2 :]
    r_send, r_recv, sends, recvs = rest
    rep_at, shard_at = (lax.axis_index("rep"), lax.axis_index("shard"))
    orders = bit_orders(reps)
    columns = halves_of(parts.shape[-1])
    meet(rep_at, shard_at, reps, shard_count)
    flying = [None] * HALVES

    def source(half, at):
        return parts.at[:, :, :, columns[half]] if at == 0 else landed[half][at - 1]

    def begin(half, at):
        bit = orders[half][at]
        many = reps // 2 ** (at + 1)
        away = (1 - rep_at // 2**bit % 2) * many
        flying[half] = pltpu.make_async_remote_copy(
            src_ref=source(half, at).at[:, pl.ds(away, many)],
            dst_ref=landed[half][at],
            send_sem=r_send.at[half, at],
            recv_sem=r_recv.at[half, at],
            device_id=(partner(rep_at, bit), shard_at),
            device_id_type=MESH,
        )
        flying[half].start()

    for half in range(HALVES):
        begin(half, 0)
    for at in range(bits):
        many = reps // 2 ** (at + 1)
        for half in range(HALVES):
            flying[half].wait()
            keep = rep_at // 2 ** orders[half][at] % 2 * many
            mine, came = (source(half, at), landed[half][at])

            @pl.loop(0, parts.shape[0] * many)
            def _(index):
                outer, inner = (index // many, index % many)
                came[outer, inner] = (
                    came[outer, inner].astype(f32) + mine[outer, keep + inner].astype(f32)
                ).astype(came.dtype)

            if at + 1 < bits:
                begin(half, at + 1)
    copies = []
    if shard_count > 1:
        for half in range(HALVES):
            for step in range(1, shard_count):
                to = (shard_at + step) % shard_count
                copy = pltpu.make_async_remote_copy(
                    src_ref=landed[half][-1].at[to, 0],
                    dst_ref=z_land[half].at[step - 1],
                    send_sem=z_send.at[half, step - 1],
                    recv_sem=z_recv.at[half, step - 1],
                    device_id=(rep_at, to),
                    device_id_type=MESH,
                )
                copy.start()
                copies.append(copy)
    for copy in copies:
        copy.wait()
    for half in range(HALVES):
        place = rep_place(rep_at, orders[half])
        if shard_count > 1:
            total = landed[half][-1][shard_at, 0].astype(f32)
            for step in range(1, shard_count):
                total = total + z_land[half][step - 1].astype(f32)
            out[0, place, :, columns[half]] = total.astype(out.dtype)
        else:
            out[0, place, :, columns[half]] = landed[half][-1][0, 0]
    spread(out, orders, columns, rep_at, shard_at, sends, recvs)


def reduce_all(parts, reps, shard_count, number):
    total, width = parts.shape
    rows = total // (reps * shard_count)
    bits = reps.bit_length() - 1
    widths = (halves_of(width)[0].size, halves_of(width)[1].size)
    scratch = []
    for wide in widths:
        for at in range(bits):
            scratch.append(
                pltpu.VMEM((shard_count, reps // 2 ** (at + 1), rows, wide), parts.dtype)
            )
    if shard_count > 1:
        scratch += [pltpu.VMEM((shard_count - 1, rows, wide), parts.dtype) for wide in widths]
        scratch += [pltpu.SemaphoreType.DMA((HALVES, shard_count)) for _ in range(2)]
    scratch += [pltpu.SemaphoreType.DMA((HALVES, bits)) for _ in range(4)]
    out = pl.pallas_call(
        lambda *refs: reduce_kernel(reps, shard_count, *refs),
        out_shape=jax.ShapeDtypeStruct((1, reps, rows, width), parts.dtype),
        in_specs=[pl.BlockSpec(memory_space=pltpu.VMEM)],
        out_specs=pl.BlockSpec(memory_space=pltpu.VMEM),
        scratch_shapes=scratch,
        compiler_params=pltpu.CompilerParams(
            collective_id=number, has_side_effects=True, vmem_limit_bytes=VMEM_BYTES
        ),
        cost_estimate=pl.CostEstimate(
            flops=0, bytes_accessed=32 * total * width, transcendentals=0
        ),
    )(parts.reshape(shard_count, reps, rows, width))
    return out.reshape(reps * rows, width)


def gather_shard(piece):
    return lax.all_gather(piece, "shard", axis=0, tiled=True)


def shards(
    tokens,
    doc_ids,
    routes,
    norm_in_gain,
    w_query,
    w_key,
    w_value,
    w_out,
    norm_mid_gain,
    w_router,
    w_expert_in,
    w_expert_down,
    cotangent,
):
    bf16, f32 = jnp.bfloat16, jnp.float32
    row_count, model_width = tokens.shape
    groups = HEADS // KV_HEADS
    query_cols = w_query.shape[1]
    kv_cols = w_key.shape[1]
    own_rows = w_query.shape[0]
    own_experts, ff = w_expert_down.shape[:2]
    shard_at = lax.axis_index("shard")

    small = jnp.concatenate(
        [
            w_router,
            norm_in_gain[:, None],
            norm_mid_gain[:, None],
            jnp.zeros((own_rows, PAD - EXPERTS - 2), bf16),
        ],
        axis=1,
    )
    reps, shard_count = (lax.axis_size("rep"), lax.axis_size("shard"))
    all_w = gather_all(
        jnp.concatenate([w_query, w_key, w_value, w_out, small], axis=1), reps, shard_count, 1
    )
    qkv_cols = query_cols + 2 * kv_cols
    qkv_w = all_w[:, :qkv_cols]
    out_w = all_w[:, qkv_cols : qkv_cols + w_out.shape[1]]
    small_full = all_w[:, qkv_cols + w_out.shape[1] :]
    router_full = small_full[:, :EXPERTS]
    gain_in = small_full[:, EXPERTS].astype(f32)
    gain_mid = small_full[:, EXPERTS + 1].astype(f32)
    mask_own = jnp.any(
        routes[:, :, None] == jnp.arange(EXPERTS, dtype=jnp.int32)[None, None, :], axis=1
    )
    side = jnp.concatenate(
        [cotangent, mask_own.astype(bf16), jnp.zeros((row_count, PAD - EXPERTS), bf16)], axis=1
    )
    side_all = gather_shard(side)

    inputs = tokens.astype(f32)
    grad_final = cotangent.astype(f32)
    cosine, sine_table = rotary_tables(positions(doc_ids), HEAD_DIM)
    normed_in, scale_in = normalize(inputs)
    first_low = (normed_in * gain_in).astype(bf16)
    qkv_pre = jnp.dot(first_low, qkv_w, preferred_element_type=f32)
    query_pre = qkv_pre[:, :query_cols]
    key_pre = qkv_pre[:, query_cols : query_cols + kv_cols]
    value_pre = qkv_pre[:, query_cols + kv_cols :]
    query_rows = (
        rotate(query_pre.reshape(row_count, HEADS, HEAD_DIM), cosine, sine_table)
        .astype(bf16)
        .reshape(row_count, KV_HEADS, groups, HEAD_DIM)
    )
    key_rows = rotate(key_pre.reshape(row_count, KV_HEADS, HEAD_DIM), cosine, sine_table).astype(
        bf16
    )
    value_rows = value_pre.astype(bf16).reshape(row_count, KV_HEADS, HEAD_DIM)
    att_rows, log_sums = attend(query_rows, key_rows, value_rows, doc_ids)
    att_low = att_rows.reshape(row_count, query_cols)
    middle = inputs + jnp.dot(att_low, out_w, preferred_element_type=f32)
    normed_mid, scale_mid = normalize(middle)
    second_low = (normed_mid * gain_mid).astype(bf16)

    second_low, side_all = lax.optimization_barrier((second_low, side_all))
    dy_all = side_all[:, :model_width]
    mask_all = side_all[:, model_width : model_width + EXPERTS] > 0
    second_all = gather_shard(second_low)
    logits = jnp.dot(second_all, router_full, preferred_element_type=f32)
    chosen = jnp.where(mask_all, logits, masked_score)
    gate_exp = jnp.where(mask_all, jnp.exp(chosen - jnp.max(chosen, axis=1, keepdims=True)), 0.0)
    gates_all = gate_exp / jnp.sum(gate_exp, axis=1, keepdims=True)
    gates_here = lax.dynamic_slice_in_dim(gates_all, shard_at * own_experts, own_experts, axis=1)
    gates_own = lax.dynamic_slice_in_dim(gates_all, shard_at * row_count, row_count, axis=0)

    gated, grad_both, grad_gates_here = experts(
        second_all, dy_all, gates_here, w_expert_in, w_expert_down
    )
    combined = jnp.einsum("etf,efd->td", gated, w_expert_down, preferred_element_type=f32)
    combined_own = lax.psum_scatter(
        combined.astype(bf16), "shard", scatter_dimension=0, tiled=True
    )
    grad_second_here = jnp.einsum("etf,edf->td", grad_both, w_expert_in, preferred_element_type=f32)
    gate_cols = lax.dynamic_update_slice_in_dim(
        jnp.zeros((grad_gates_here.shape[0], EXPERTS), f32),
        grad_gates_here,
        shard_at * own_experts,
        axis=1,
    )
    gate_high = gate_cols.astype(bf16)
    gate_low = (gate_cols - gate_high.astype(f32)).astype(bf16)
    back_rows = jnp.concatenate(
        [
            grad_second_here.astype(bf16),
            gate_high,
            gate_low,
            jnp.zeros((gate_cols.shape[0], PAD - 2 * EXPERTS), bf16),
        ],
        axis=1,
    )
    back_own = lax.psum_scatter(back_rows, "shard", scatter_dimension=0, tiled=True)
    grad_in_here = jnp.einsum("td,etf->edf", second_all, grad_both, preferred_element_type=f32)
    grad_down_here = jnp.einsum("etf,td->efd", gated, dy_all, preferred_element_type=f32)
    grad_in_own, grad_down_own = lax.optimization_barrier(
        lax.psum((grad_in_here.astype(bf16), grad_down_here.astype(bf16)), "rep")
    )
    grad_in_own = grad_in_own.astype(f32)
    grad_down_own = grad_down_own.astype(f32)

    mixed = (middle + combined_own.astype(f32)).astype(bf16)
    gate_back = back_own[:, model_width : model_width + 2 * EXPERTS].astype(f32)
    grad_gates = gate_back[:, :EXPERTS] + gate_back[:, EXPERTS:]
    grad_logits = (
        gates_own * (grad_gates - jnp.sum(gates_own * grad_gates, axis=1, keepdims=True))
    ).astype(bf16)
    grad_router = jnp.einsum("td,te->de", second_low, grad_logits, preferred_element_type=f32)
    grad_second = back_own[:, :model_width].astype(f32) + jnp.einsum(
        "te,de->td", grad_logits, router_full, preferred_element_type=f32
    )
    grad_mid_norm, grad_gain_mid = norm_back(grad_second, normed_mid, scale_mid, gain_mid)
    grad_middle = grad_final + grad_mid_norm
    grad_branch = grad_middle.astype(bf16)
    grad_out_w = jnp.einsum("ta,td->ad", att_low, grad_branch, preferred_element_type=f32)
    grad_att = jnp.einsum("td,ad->ta", grad_branch, out_w, preferred_element_type=f32).astype(bf16)
    grad_query_rot, grad_key_rot, grad_value_rows = attend_back(
        query_rows,
        key_rows,
        value_rows,
        doc_ids,
        log_sums,
        grad_att.reshape(row_count, KV_HEADS, groups, HEAD_DIM),
    )
    grad_query_pre = (
        unrotate(grad_query_rot.reshape(row_count, HEADS, HEAD_DIM), cosine, sine_table)
        .astype(bf16)
        .reshape(row_count, query_cols)
    )
    grad_key_pre = unrotate(grad_key_rot, cosine, sine_table).astype(bf16)
    grad_pre = jnp.concatenate(
        [
            grad_query_pre,
            grad_key_pre.reshape(row_count, kv_cols),
            grad_value_rows.astype(bf16).reshape(row_count, kv_cols),
        ],
        axis=1,
    )
    grad_qkv = jnp.einsum("td,tc->dc", first_low, grad_pre, preferred_element_type=f32)
    columns = jnp.einsum("tc,dc->td", grad_pre, qkv_w, preferred_element_type=f32)
    grad_in_norm, grad_gain_in = norm_back(columns, normed_in, scale_in, gain_in)
    grad_tokens = grad_middle + grad_in_norm

    joint = jnp.concatenate(
        [
            grad_qkv.astype(bf16),
            grad_out_w.astype(bf16),
            grad_router.astype(bf16),
            grad_gain_in.astype(bf16)[:, None],
            grad_gain_mid.astype(bf16)[:, None],
            jnp.zeros((model_width, PAD - EXPERTS - 2), bf16),
        ],
        axis=1,
    )
    joint_own = reduce_all(joint, reps, shard_count, 3).astype(f32)
    edges = [0]
    for width in (query_cols, kv_cols, kv_cols, w_out.shape[1], EXPERTS, 1, 1):
        edges.append(edges[-1] + width)
    pieces = [joint_own[:, a:b] for a, b in zip(edges[:-1], edges[1:])]
    query_own, key_own, value_own, out_own, router_own, gain_in_own, gain_mid_own = pieces
    return (
        mixed,
        grad_tokens,
        gain_in_own[:, 0],
        query_own,
        key_own,
        value_own,
        out_own,
        gain_mid_own[:, 0],
        router_own,
        grad_in_own,
        grad_down_own,
    )


def experts(rows, dy_rows, gates, in_w, down_w):
    f32, bf16 = jnp.float32, jnp.bfloat16
    both = jnp.einsum("td,edf->etf", rows, in_w, preferred_element_type=f32)
    half_width = both.shape[-1] // 2
    gate_part, up_part = (both[..., :half_width], both[..., half_width:])
    sigmoid_gate = jax.nn.sigmoid(gate_part)
    silu_gate = gate_part * sigmoid_gate
    hidden = (silu_gate * up_part).astype(bf16).astype(f32)
    back = jnp.einsum("td,efd->etf", dy_rows, down_w, preferred_element_type=f32)
    gate_cols = gates.T[:, :, None]
    grad_gates = jnp.sum(hidden * back, axis=-1).T
    gated = (hidden * gate_cols).astype(bf16)
    grad_hidden = back * gate_cols
    grad_gate = grad_hidden * up_part * sigmoid_gate * (1.0 + gate_part * (1.0 - sigmoid_gate))
    grad_both = jnp.concatenate([grad_gate, grad_hidden * silu_gate], axis=-1).astype(bf16)
    return (gated, grad_both, grad_gates)


def solution(mesh):
    in_specs = (
        P(("rep", "shard"), None),
        P(("rep", "shard")),
        P(("rep", "shard"), None),
        P("shard"),
        P("shard", None),
        P("shard", None),
        P("shard", None),
        P("shard", None),
        P("shard"),
        P("shard", None),
        P("shard", None, None),
        P("shard", None, None),
        P(("rep", "shard"), None),
    )
    out_specs = (
        P(("rep", "shard"), None),
        P(("rep", "shard"), None),
        P("shard"),
        P("shard", None),
        P("shard", None),
        P("shard", None),
        P("shard", None),
        P("shard"),
        P("shard", None),
        P("shard", None, None),
        P("shard", None, None),
    )
    return jax.shard_map(shards, mesh=mesh, in_specs=in_specs, out_specs=out_specs, check_vma=False)
```

```python
import jax
import jax.numpy as jnp
from jax import lax
from jax.experimental import pallas as pl
from jax.experimental.pallas import tpu as pltpu
from jax.sharding import PartitionSpec as P

HEADS = 16
KV_HEADS = 8
HEAD_DIM = 64
EXPERTS = 16
PAD = 128
VMEM_BYTES = 54 * 2**20


epsilon = 1e-06
rope_base = 10000.0
masked_score = -1e30


def positions(doc_rows):
    row_count = doc_rows.shape[0]
    places = jnp.arange(row_count, dtype=jnp.int32)
    begins = jnp.sum((doc_rows[None, :] < doc_rows[:, None]).astype(jnp.int32), axis=1)
    return places - begins


def rotary_tables(places, head_width):
    half_width = head_width // 2
    frequencies = jnp.power(
        rope_base, -2.0 * jnp.arange(half_width, dtype=jnp.float32) / head_width
    )
    angles = places.astype(jnp.float32)[:, None] * frequencies[None, :]
    return (jnp.cos(angles)[:, None, :], jnp.sin(angles)[:, None, :])


MESH = pl.DeviceIdType.MESH
HALVES = 2


def bit_orders(reps):
    bits = reps.bit_length() - 1
    first = list(range(bits))
    return (first, first[:1] + first[1:][::-1])


def rep_place(rep_at, order):
    place = 0
    for bit in order:
        place = place * 2 + rep_at // 2**bit % 2
    return place


def partner(rep_at, bit):
    return rep_at + 2**bit * (1 - 2 * (rep_at // 2**bit % 2))


def halves_of(columns):
    tiles = columns // 128
    left = (tiles + 1) // 2 * 128
    return (pl.ds(0, left), pl.ds(left, columns - left))


def meet(rep_at, shard_at, reps, shard_count):
    barrier = pltpu.get_barrier_semaphore()
    bits = reps.bit_length() - 1
    for bit in range(bits):
        pl.semaphore_signal(
            barrier, inc=1, device_id=(partner(rep_at, bit), shard_at), device_id_type=MESH
        )
    for step in range(1, shard_count):
        pl.semaphore_signal(
            barrier,
            inc=1,
            device_id=(rep_at, (shard_at + step) % shard_count),
            device_id_type=MESH,
        )
    pl.semaphore_wait(barrier, bits + shard_count - 1)


def spread(out, orders, columns, rep_at, shard_at, sends, recvs):
    bits = len(orders[0])
    flying = [None] * HALVES
    for at in reversed(range(bits)):
        window = 2 ** (bits - 1 - at)
        for half in range(HALVES):
            order = orders[half]
            place = rep_place(rep_at, order)
            begin = place // window * window
            if flying[half] is not None:
                flying[half].wait()
            block = out.at[:, pl.ds(begin, window), :, columns[half]]
            flying[half] = pltpu.make_async_remote_copy(
                src_ref=block,
                dst_ref=block,
                send_sem=sends.at[half, at],
                recv_sem=recvs.at[half, at],
                device_id=(partner(rep_at, order[at]), shard_at),
                device_id_type=MESH,
            )
            flying[half].start()
    for half in range(HALVES):
        flying[half].wait()


def gather_kernel(reps, shard_count, piece, out, z_send, z_recv, sends, recvs):
    rep_at, shard_at = (lax.axis_index("rep"), lax.axis_index("shard"))
    orders = bit_orders(reps)
    columns = halves_of(piece.shape[-1])
    meet(rep_at, shard_at, reps, shard_count)
    flying = []
    for half in range(HALVES):
        place = rep_place(rep_at, orders[half])
        for step in range(1, shard_count):
            copy = pltpu.make_async_remote_copy(
                src_ref=piece.at[place, :, columns[half]],
                dst_ref=out.at[shard_at, place, :, columns[half]],
                send_sem=z_send.at[half, step - 1],
                recv_sem=z_recv.at[half, step - 1],
                device_id=(rep_at, (shard_at + step) % shard_count),
                device_id_type=MESH,
            )
            copy.start()
            flying.append(copy)
        out[shard_at, place, :, columns[half]] = piece[place, :, columns[half]]
    for copy in flying:
        copy.wait()
    spread(out, orders, columns, rep_at, shard_at, sends, recvs)


def gather_all(piece, reps, shard_count, number):
    own, width = piece.shape
    rows = own // reps
    bits = reps.bit_length() - 1
    out = pl.pallas_call(
        lambda *refs: gather_kernel(reps, shard_count, *refs),
        out_shape=jax.ShapeDtypeStruct((shard_count, reps, rows, width), piece.dtype),
        in_specs=[pl.BlockSpec(memory_space=pltpu.VMEM)],
        out_specs=pl.BlockSpec(memory_space=pltpu.VMEM),
        scratch_shapes=[
            pltpu.SemaphoreType.DMA((HALVES, shard_count)),
            pltpu.SemaphoreType.DMA((HALVES, shard_count)),
            pltpu.SemaphoreType.DMA((HALVES, bits)),
            pltpu.SemaphoreType.DMA((HALVES, bits)),
        ],
        compiler_params=pltpu.CompilerParams(
            collective_id=number, has_side_effects=True, vmem_limit_bytes=VMEM_BYTES
        ),
        cost_estimate=pl.CostEstimate(
            flops=0, bytes_accessed=shard_count * own * width, transcendentals=0
        ),
    )(piece.reshape(reps, rows, width))
    return out.reshape(shard_count * own, width)


def reduce_kernel(reps, shard_count, parts, out, *scratch):
    bits = reps.bit_length() - 1
    f32 = jnp.float32
    landed = [scratch[half * bits : (half + 1) * bits] for half in range(HALVES)]
    rest = scratch[HALVES * bits :]
    if shard_count > 1:
        z_land, (z_send, z_recv) = (rest[:HALVES], rest[HALVES : HALVES + 2])
        rest = rest[HALVES + 2 :]
    r_send, r_recv, sends, recvs = rest
    rep_at, shard_at = (lax.axis_index("rep"), lax.axis_index("shard"))
    orders = bit_orders(reps)
    columns = halves_of(parts.shape[-1])
    meet(rep_at, shard_at, reps, shard_count)
    flying = [None] * HALVES

    def source(half, at):
        return parts.at[:, :, :, columns[half]] if at == 0 else landed[half][at - 1]

    def begin(half, at):
        bit = orders[half][at]
        many = reps // 2 ** (at + 1)
        away = (1 - rep_at // 2**bit % 2) * many
        flying[half] = pltpu.make_async_remote_copy(
            src_ref=source(half, at).at[:, pl.ds(away, many)],
            dst_ref=landed[half][at],
            send_sem=r_send.at[half, at],
            recv_sem=r_recv.at[half, at],
            device_id=(partner(rep_at, bit), shard_at),
            device_id_type=MESH,
        )
        flying[half].start()

    for half in range(HALVES):
        begin(half, 0)
    for at in range(bits):
        many = reps // 2 ** (at + 1)
        for half in range(HALVES):
            flying[half].wait()
            keep = rep_at // 2 ** orders[half][at] % 2 * many
            mine, came = (source(half, at), landed[half][at])

            @pl.loop(0, parts.shape[0] * many)
            def _(index):
                outer, inner = (index // many, index % many)
                came[outer, inner] = (
                    came[outer, inner].astype(f32) + mine[outer, keep + inner].astype(f32)
                ).astype(came.dtype)

            if at + 1 < bits:
                begin(half, at + 1)
    copies = []
    if shard_count > 1:
        for half in range(HALVES):
            for step in range(1, shard_count):
                to = (shard_at + step) % shard_count
                copy = pltpu.make_async_remote_copy(
                    src_ref=landed[half][-1].at[to, 0],
                    dst_ref=z_land[half].at[step - 1],
                    send_sem=z_send.at[half, step - 1],
                    recv_sem=z_recv.at[half, step - 1],
                    device_id=(rep_at, to),
                    device_id_type=MESH,
                )
                copy.start()
                copies.append(copy)
    for copy in copies:
        copy.wait()
    for half in range(HALVES):
        place = rep_place(rep_at, orders[half])
        if shard_count > 1:
            total = landed[half][-1][shard_at, 0].astype(f32)
            for step in range(1, shard_count):
                total = total + z_land[half][step - 1].astype(f32)
            out[0, place, :, columns[half]] = total.astype(out.dtype)
        else:
            out[0, place, :, columns[half]] = landed[half][-1][0, 0]
    spread(out, orders, columns, rep_at, shard_at, sends, recvs)


def reduce_all(parts, reps, shard_count, number):
    total, width = parts.shape
    rows = total // (reps * shard_count)
    bits = reps.bit_length() - 1
    widths = (halves_of(width)[0].size, halves_of(width)[1].size)
    scratch = []
    for wide in widths:
        for at in range(bits):
            scratch.append(
                pltpu.VMEM((shard_count, reps // 2 ** (at + 1), rows, wide), parts.dtype)
            )
    if shard_count > 1:
        scratch += [pltpu.VMEM((shard_count - 1, rows, wide), parts.dtype) for wide in widths]
        scratch += [pltpu.SemaphoreType.DMA((HALVES, shard_count)) for _ in range(2)]
    scratch += [pltpu.SemaphoreType.DMA((HALVES, bits)) for _ in range(4)]
    out = pl.pallas_call(
        lambda *refs: reduce_kernel(reps, shard_count, *refs),
        out_shape=jax.ShapeDtypeStruct((1, reps, rows, width), parts.dtype),
        in_specs=[pl.BlockSpec(memory_space=pltpu.VMEM)],
        out_specs=pl.BlockSpec(memory_space=pltpu.VMEM),
        scratch_shapes=scratch,
        compiler_params=pltpu.CompilerParams(
            collective_id=number, has_side_effects=True, vmem_limit_bytes=VMEM_BYTES
        ),
        cost_estimate=pl.CostEstimate(
            flops=0, bytes_accessed=total * width, transcendentals=0
        ),
    )(parts.reshape(shard_count, reps, rows, width))
    return out.reshape(reps * rows, width)


F32, BF16 = jnp.float32, jnp.bfloat16
LANES = 128
TILE = 256
LIGHT = pl.CostEstimate(flops=10**6, bytes_accessed=10**5, transcendentals=0)
GROUP = HEADS // KV_HEADS


def dot(a, b):
    return lax.dot_general(a, b, (((1,), (0,)), ((), ())), preferred_element_type=F32)


def dot_nt(a, b):
    return lax.dot_general(a, b, (((1,), (1,)), ((), ())), preferred_element_type=F32)


def lane_of(shape):
    return lax.broadcasted_iota(jnp.int32, shape, len(shape) - 1)


def swap_halves(values):
    near = lane_of(values.shape) % HEAD_DIM < HEAD_DIM // 2
    up = pltpu.roll(values, LANES - HEAD_DIM // 2, 1)
    down = pltpu.roll(values, HEAD_DIM // 2, 1)
    return jnp.where(near, up, down)


def rope_block(values, ct, st):
    return values * ct + swap_halves(values) * st


def unrope_block(values, ct, st):
    return values * ct - swap_halves(values) * st


def low_high(block, side):
    lane = lane_of(block.shape)
    wide = block.astype(F32)
    kept = jnp.where((lane < HEAD_DIM) if side == 0 else (lane >= HEAD_DIM), wide, 0.0)
    moved = pltpu.roll(kept, HEAD_DIM, 1)
    pair = (kept, moved) if side == 0 else (moved, kept)
    return [item.astype(BF16) for item in pair]


def fill_bias(bias, doc_col, doc_row):
    rows = bias.shape[0]
    keys = lax.broadcasted_iota(jnp.int32, (TILE, rows), 0)
    queries = lax.broadcasted_iota(jnp.int32, (TILE, rows), 1)
    for start in range(0, rows, TILE):
        allowed = (doc_col[start : start + TILE, :] == doc_row[...]) & (keys + start <= queries)
        bias[start : start + TILE, :] = jnp.where(allowed, 0.0, masked_score)


def tile_at(index, width=TILE):
    return pl.ds(pl.multiple_of(index * width, width), width)


def gate_softmax(second, small, mask):
    logits = dot(second, small)
    chosen = jnp.where(mask, logits, masked_score)
    gate_exp = jnp.where(mask, jnp.exp(chosen - jnp.max(chosen, axis=1, keepdims=True)), 0.0)
    return gate_exp / jnp.sum(gate_exp, axis=1, keepdims=True)


def forward_kernel(
    tokens, w, ct, st, doc_col, doc_row,
    second, middle, first_t, q8, keys, values, att_t, lse,
    first, att, bias,
):
    rows, width = tokens.shape
    q_cols, kv_cols = q8.shape[1], keys.shape[1]
    small_at = w.shape[1] - PAD
    gains = w[:, small_at:].astype(F32).T
    gain_in, gain_mid = gains[EXPERTS : EXPERTS + 1], gains[EXPERTS + 1 : EXPERTS + 2]
    for at in range(0, rows, LANES):
        x = tokens[at : at + LANES, :].astype(F32)
        scale = lax.rsqrt(jnp.mean(x * x, axis=-1, keepdims=True) + epsilon)
        low = (x * scale * gain_in).astype(BF16)
        first[at : at + LANES, :] = low
        first_t[:, at : at + LANES] = low.T

    def project(index):
        return dot(first[...], w[:, tile_at(index)])

    def roped(index):
        part = project(index)
        return jnp.concatenate(
            [
                rope_block(part[:, at : at + LANES], ct[...], st[...])
                for at in range(0, TILE, LANES)
            ],
            axis=1,
        )

    @pl.loop(0, q_cols // TILE)
    def _(j):
        q8[:, tile_at(j)] = (roped(j) * HEAD_DIM**-0.5).astype(BF16)

    @pl.loop(0, kv_cols // TILE)
    def _(j):
        keys[:, tile_at(j)] = roped(q_cols // TILE + j).astype(BF16)

    @pl.loop(0, kv_cols // TILE)
    def _(j):
        values[:, tile_at(j)] = project((q_cols + kv_cols) // TILE + j).astype(BF16)

    fill_bias(bias, doc_col, doc_row)

    @pl.loop(0, kv_cols // LANES)
    def _(pair):
        k128, v128 = keys[:, tile_at(pair, LANES)], values[:, tile_at(pair, LANES)]
        v_t = v128.astype(F32).T.astype(BF16)
        for side in range(2):
            low_k = low_high(k128, side)
            q = q8[:, tile_at(pair * 2 + side, LANES)]
            v_s = v_t[side * HEAD_DIM : (side + 1) * HEAD_DIM]
            for h in range(GROUP):
                head = pair * 2 * GROUP + side * GROUP + h
                for begin in range(0, rows, TILE):
                    kr = begin + TILE
                    s = dot_nt(low_k[h][:kr], q[begin:kr]) + bias[:kr, begin:kr]
                    top = jnp.max(s, axis=0, keepdims=True)
                    p = jnp.exp(s - top)
                    total = jnp.sum(p, axis=0, keepdims=True)
                    probs = (p * (1.0 / total)).astype(BF16)
                    lse[head, :, begin:kr] = top + jnp.log(total)
                    att_t[tile_at(head, HEAD_DIM), begin:kr] = dot(v_s[:, :kr], probs).astype(BF16)

    @pl.loop(0, width // TILE)
    def _(j):
        att[:, tile_at(j)] = att_t[tile_at(j), :].astype(F32).T.astype(BF16)

    @pl.loop(0, width // TILE)
    def _(j):
        out_w = w[:, pl.ds(pl.multiple_of(q_cols + 2 * kv_cols + j * TILE, TILE), TILE)]
        middle[:, tile_at(j)] = tokens[:, tile_at(j)].astype(F32) + dot(att[...], out_w)

    for at in range(0, rows, LANES):
        x = middle[at : at + LANES, :]
        scale = lax.rsqrt(jnp.mean(x * x, axis=-1, keepdims=True) + epsilon)
        second[at : at + LANES, :] = (x * scale * gain_mid).astype(BF16)


def split_kernel(joint, *outs):
    begin = 0
    for out in outs:
        out[...] = joint[:, begin : begin + out.shape[1]].astype(F32)
        begin += out.shape[1]


def shape_of(shape, kind):
    return jax.ShapeDtypeStruct(shape, kind)


def local_call(kernel, outs, scratch, *args):
    return pl.pallas_call(
        kernel,
        out_shape=outs,
        in_specs=[pl.BlockSpec(memory_space=pltpu.VMEM)] * len(args),
        out_specs=[pl.BlockSpec(memory_space=pltpu.VMEM)] * len(outs),
        scratch_shapes=scratch,
        compiler_params=pltpu.CompilerParams(vmem_limit_bytes=VMEM_BYTES),
        cost_estimate=LIGHT,
    )(*args)


def forward_block(tokens, w, ct, st, doc_ids, q_cols, kv_cols):
    rows, width = tokens.shape
    outs = [
        shape_of((rows, width), BF16),
        shape_of((rows, width), F32),
        shape_of((width, rows), BF16),
        shape_of((rows, q_cols), BF16),
        shape_of((rows, kv_cols), BF16),
        shape_of((rows, kv_cols), BF16),
        shape_of((q_cols, rows), BF16),
        shape_of((HEADS, 1, rows), F32),
    ]
    scratch = [
        pltpu.VMEM((rows, width), BF16),
        pltpu.VMEM((rows, q_cols), BF16),
        pltpu.VMEM((rows, rows), F32),
    ]
    return local_call(
        forward_kernel, outs, scratch, tokens, w, ct, st, doc_ids[:, None], doc_ids[None, :]
    )


def backward_kernel(
    tokens, side, middle, second, back_own, back_left, back_right, w, ct, st, doc_col, doc_row,
    first_t, q8, keys, values, att_t, lse,
    joint, grad_tokens,
    bias, grad_middle, grad_branch, grad_att, grad_pre, grad_first, dq_t, dk, dv, rows_t,
):
    rows, width = tokens.shape
    q_cols, kv_cols = q8.shape[1], keys.shape[1]
    qkv_cols = q_cols + 2 * kv_cols
    small_at = w.shape[1] - PAD
    small = w[:, small_at:]
    gains = small.astype(F32).T
    gain_in, gain_mid = gains[EXPERTS : EXPERTS + 1], gains[EXPERTS + 1 : EXPERTS + 2]
    tall = back_own.shape[1]
    gain_sum = jnp.zeros((1, width), F32)
    router_t = jnp.zeros((PAD, width), F32)
    for at in range(0, rows, LANES):
        here = slice(at, at + LANES)
        mask = side[here, width:] > 0
        gates = gate_softmax(second[here, :], small, mask)
        came = (
            back_own[here, width:].astype(F32)
            + back_left[here, width:].astype(F32)
            + back_right[here, width:].astype(F32)
        )
        gate_back = jnp.where(
            lane_of(came.shape) < EXPERTS, came + pltpu.roll(came, tall - width - EXPERTS, 1), 0.0
        )
        grad_logits = gates * (gate_back - jnp.sum(gates * gate_back, axis=1, keepdims=True))
        low_logits = grad_logits.astype(BF16)
        router_t += dot(grad_logits.T.astype(BF16), second[here, :])
        grad_second = (
            back_own[here, :width].astype(F32)
            + back_left[here, :width].astype(F32)
            + back_right[here, :width].astype(F32)
            + dot_nt(low_logits, small)
        )
        x = middle[here, :]
        scale = lax.rsqrt(jnp.mean(x * x, axis=-1, keepdims=True) + epsilon)
        normed = x * scale
        gain_sum += jnp.sum(grad_second * normed, axis=0, keepdims=True)
        u = grad_second * gain_mid
        inner = jnp.mean(u * normed, axis=-1, keepdims=True)
        total = side[here, :width].astype(F32) + scale * (u - normed * inner)
        grad_middle[here, :] = total
        grad_branch[here, :] = total.astype(BF16)
    rows_t[...] = router_t
    rows_t[EXPERTS + 1 : EXPERTS + 2, :] = gain_sum

    @pl.loop(0, width // TILE)
    def _(j):
        joint[:, pl.ds(pl.multiple_of(qkv_cols + j * TILE, TILE), TILE)] = dot(
            att_t[...], grad_branch[:, tile_at(j)]
        ).astype(BF16)
        out_rows = w[tile_at(j), pl.ds(qkv_cols, width)]
        grad_att[:, tile_at(j)] = dot_nt(grad_branch[...], out_rows).astype(BF16)

    fill_bias(bias, doc_col, doc_row)

    @pl.loop(0, kv_cols // LANES)
    def _(pair):
        k128, v128 = keys[:, tile_at(pair, LANES)], values[:, tile_at(pair, LANES)]
        k_t = k128.astype(F32).T.astype(BF16)
        sums = []
        for side_at in range(2):
            low_k, low_v = low_high(k128, side_at), low_high(v128, side_at)
            q = q8[:, tile_at(pair * 2 + side_at, LANES)]
            grad_o = grad_att[:, tile_at(pair * 2 + side_at, LANES)]
            k_s = k_t[side_at * HEAD_DIM : (side_at + 1) * HEAD_DIM]
            for h in range(GROUP):
                head = pair * 2 * GROUP + side_at * GROUP + h
                for begin in reversed(range(0, rows, TILE)):
                    kr = begin + TILE
                    s = dot_nt(low_k[h][:kr], q[begin:kr]) + bias[:kr, begin:kr]
                    p = jnp.exp(s - lse[head, :, begin:kr])
                    dp = dot_nt(low_v[h][:kr], grad_o[begin:kr])
                    inner = jnp.sum(p * dp, axis=0, keepdims=True)
                    ds = (p * (dp - inner)).astype(BF16)
                    dq_t[h * HEAD_DIM : (h + 1) * HEAD_DIM, begin:kr] = dot(k_s[:, :kr], ds)
                    more_k, more_v = dot(ds, q[begin:kr]), dot(p.astype(BF16), grad_o[begin:kr])
                    if kr == rows:
                        dk[h, :, :], dv[h, :, :] = more_k, more_v
                    else:
                        dk[h, :kr, :] += more_k
                        dv[h, :kr, :] += more_v
            grad_q = unrope_block(dq_t[...].T * HEAD_DIM**-0.5, ct[...], st[...])
            grad_pre[:, tile_at(pair * 2 + side_at, LANES)] = grad_q.astype(BF16)
            left = lane_of((rows, LANES)) < HEAD_DIM
            mixed_k = jnp.where(left, dk[0], dk[1])
            mixed_v = jnp.where(left, dv[0], dv[1])
            sums.append(
                (mixed_k + pltpu.roll(mixed_k, HEAD_DIM, 1), mixed_v + pltpu.roll(mixed_v, HEAD_DIM, 1))
            )
        left = lane_of((rows, LANES)) < HEAD_DIM
        grad_k = unrope_block(jnp.where(left, sums[0][0], sums[1][0]), ct[...], st[...])
        grad_v = jnp.where(left, sums[0][1], sums[1][1])
        k_at = pl.multiple_of(q_cols + pair * LANES, LANES)
        v_at = pl.multiple_of(q_cols + kv_cols + pair * LANES, LANES)
        grad_pre[:, pl.ds(k_at, LANES)] = grad_k.astype(BF16)
        grad_pre[:, pl.ds(v_at, LANES)] = grad_v.astype(BF16)

    @pl.loop(0, qkv_cols // TILE)
    def _(j):
        joint[:, tile_at(j)] = dot(first_t[...], grad_pre[:, tile_at(j)]).astype(BF16)

    @pl.loop(0, width // TILE)
    def _(j):
        grad_first[:, tile_at(j)] = dot_nt(grad_pre[...], w[tile_at(j), pl.ds(0, qkv_cols)])

    gain_sum = jnp.zeros((1, width), F32)
    for at in range(0, rows, LANES):
        here = slice(at, at + LANES)
        x = tokens[here, :].astype(F32)
        scale = lax.rsqrt(jnp.mean(x * x, axis=-1, keepdims=True) + epsilon)
        normed = x * scale
        columns = grad_first[here, :]
        gain_sum += jnp.sum(columns * normed, axis=0, keepdims=True)
        u = columns * gain_in
        inner = jnp.mean(u * normed, axis=-1, keepdims=True)
        grad_tokens[here, :] = grad_middle[here, :] + scale * (u - normed * inner)
    rows_t[EXPERTS : EXPERTS + 1, :] = gain_sum
    joint[:, pl.ds(small_at, PAD)] = rows_t[...].T.astype(BF16)


def backward_block(tokens, side, middle, second, backs, w, ct, st, doc_ids, kept):
    rows, width = tokens.shape
    q_cols, kv_cols = kept[1].shape[1], kept[2].shape[1]
    outs = [shape_of((width, w.shape[1]), BF16), shape_of((rows, width), F32)]
    scratch = [
        pltpu.VMEM((rows, rows), F32),
        pltpu.VMEM((rows, width), F32),
        pltpu.VMEM((rows, width), BF16),
        pltpu.VMEM((rows, q_cols), BF16),
        pltpu.VMEM((rows, q_cols + 2 * kv_cols), BF16),
        pltpu.VMEM((rows, width), F32),
        pltpu.VMEM((LANES, rows), F32),
        pltpu.VMEM((GROUP, rows, LANES), F32),
        pltpu.VMEM((GROUP, rows, LANES), F32),
        pltpu.VMEM((PAD, width), F32),
    ]
    return local_call(
        backward_kernel, outs, scratch,
        tokens, side, middle, second, *backs, w, ct, st, doc_ids[:, None], doc_ids[None, :], *kept,
    )


def expert_kernel(
    aliased, first_expert, second, side, small, in_w, down_w, *refs
):
    gated, grad_both, comb, back, gates, grad_gates, comb_sum, back_sum = refs[2 * aliased :]
    rows, width = second.shape
    ff = down_w.shape[1]
    at = pl.program_id(0)
    lane = lane_of((rows, PAD))

    @pl.when(at == 0)
    def _():
        gates[...] = gate_softmax(second[...], small[...], side[:, width:] > 0)
        grad_gates[...] = jnp.zeros_like(grad_gates)
        comb_sum[...] = jnp.zeros_like(comb_sum)
        back_sum[...] = jnp.zeros_like(back_sum)

    mine = lane == first_expert[0] + at
    gate = jnp.sum(jnp.where(mine, gates[...], 0.0), axis=1, keepdims=True)
    grad_col = jnp.zeros((rows, 1), F32)
    for start in range(0, ff, TILE):
        tile = slice(start, start + TILE)
        up_tile = slice(ff + start, ff + start + TILE)
        gate_part = dot(second[...], in_w[0, :, tile])
        up_part = dot(second[...], in_w[0, :, up_tile])
        came = dot_nt(side[:, :width], down_w[0, tile, :])
        sigmoid_gate = 0.5 * jnp.tanh(0.5 * gate_part) + 0.5
        silu_gate = gate_part * sigmoid_gate
        hidden = (silu_gate * up_part).astype(BF16).astype(F32)
        grad_col += jnp.sum(hidden * came, axis=1, keepdims=True)
        gated[0, 0, :, tile] = (hidden * gate).astype(BF16)
        grad_hidden = came * gate
        slope = sigmoid_gate + silu_gate * (1.0 - sigmoid_gate)
        grad_both[0, 0, :, tile] = (grad_hidden * up_part * slope).astype(BF16)
        grad_both[0, 0, :, up_tile] = (grad_hidden * silu_gate).astype(BF16)
    grad_gates[...] += jnp.where(mine, grad_col, 0.0)
    for start in range(0, width, TILE):
        tile = slice(start, start + TILE)
        comb_sum[:, tile] += dot(gated[0, 0], down_w[0, :, tile])
        back_sum[:, tile] += dot_nt(grad_both[0, 0], in_w[0, tile, :])

    @pl.when(at == pl.num_programs(0) - 1)
    def _():
        comb[...] = comb_sum[...].astype(BF16)
        back[:, :width] = back_sum[...].astype(BF16)
        high = grad_gates[...].astype(BF16).astype(F32)
        back[:, width:] = (high + pltpu.roll(grad_gates[...] - high, EXPERTS, 1)).astype(BF16)


def expert_block(first_expert, second, side, small, in_w, down_w, place, count, before):
    rows, width = second.shape
    experts, ff = down_w.shape[:2]
    whole = lambda *shape: pl.BlockSpec(shape, lambda e: (0,) * len(shape))
    in_specs = [
        pl.BlockSpec(memory_space=pltpu.SMEM),
        whole(rows, width),
        whole(*side.shape),
        whole(*small.shape),
        pl.BlockSpec((1, width, 2 * ff), lambda e: (e, 0, 0)),
        pl.BlockSpec((1, ff, width), lambda e: (e, 0, 0)),
    ] + [pl.BlockSpec(memory_space=pl.ANY)] * len(before)
    out_specs = [
        pl.BlockSpec((1, 1, rows, ff), lambda e: (e, place, 0, 0)),
        pl.BlockSpec((1, 1, rows, 2 * ff), lambda e: (e, place, 0, 0)),
        whole(rows, width),
        whole(*side.shape),
    ]
    outs = [
        shape_of((experts, count, rows, ff), BF16),
        shape_of((experts, count, rows, 2 * ff), BF16),
        shape_of((rows, width), BF16),
        shape_of(side.shape, BF16),
    ]
    return pl.pallas_call(
        lambda *refs: expert_kernel(bool(before), *refs),
        grid=(experts,),
        out_shape=outs,
        in_specs=in_specs,
        out_specs=out_specs,
        scratch_shapes=[
            pltpu.VMEM((rows, PAD), F32),
            pltpu.VMEM((rows, PAD), F32),
            pltpu.VMEM((rows, width), F32),
            pltpu.VMEM((rows, width), F32),
        ],
        input_output_aliases={6: 0, 7: 1} if before else {},
        compiler_params=pltpu.CompilerParams(
            vmem_limit_bytes=VMEM_BYTES, dimension_semantics=("arbitrary",)
        ),
        cost_estimate=LIGHT,
    )(first_expert, second, side, small, in_w, down_w, *before)


def shift(block, count, step):
    return lax.ppermute(block, "shard", [(at, (at + step) % count) for at in range(count)])


def tie(*values):
    return lax.optimization_barrier(values)


def gather_near(piece, count):
    got = {0: piece}
    right = left = piece
    for step in range(1, (count - 1) // 2 + 1):
        right, left = shift(right, count, 1), shift(left, count, -1)
        got[step], got[count - step] = right, left
    return got, right, left


def gather_far(right, left, count):
    half = right.shape[0] // 2
    return shift(right[:half], count, 1), shift(left[half:], count, -1)


def far_first(parts, count):
    half = parts[0].shape[0] // 2
    far = parts[count // 2]
    return shift(far[:half], count, -1), shift(far[half:], count, 1)


def near_rest(parts, left, right, count):
    half = parts[0].shape[0] // 2
    if count == 2:
        return jnp.concatenate([left, right], axis=0), jnp.zeros_like(parts[0])
    for step in reversed(range(1, count // 2)):
        near, far = parts[step], parts[count - step]
        if step == count // 2 - 1:
            left = jnp.concatenate([add_low(near[:half], left), near[half:]], axis=0)
            right = jnp.concatenate([far[:half], add_low(far[half:], right)], axis=0)
        else:
            left, right = add_low(near, left), add_low(far, right)
        left, right = shift(left, count, -1), shift(right, count, 1)
    return left, right


def add_low(a, b):
    return (a.astype(F32) + b.astype(F32)).astype(BF16)


def across(block, reps, bit):
    return lax.ppermute(block, "rep", [(at, at ^ 2**bit) for at in range(reps)])


def part_of(block, index):
    half = block.shape[0] // 2
    return lax.dynamic_slice_in_dim(block, index * half, half, axis=0)


def both_halves(mine, other, index):
    first = jnp.where(index == 0, mine, other)
    last = jnp.where(index == 0, other, mine)
    return jnp.concatenate([first, last])


def orders_of(bits):
    return list(range(1, bits)), list(range(1, bits))[::-1]


def sent(block, reps, bit, bit_of):
    return across(part_of(block, 1 - bit_of[bit]), reps, bit)


def kept_sum(block, came, bit, bit_of):
    return add_low(part_of(block, bit_of[bit]), came)


def place_kernel(begin, cut, half, upper, lower, *refs):
    at = begin + pl.program_id(0)

    @pl.when(at < cut)
    def _():
        refs[-1][...] = upper[...].astype(F32)

    @pl.when(at >= cut)
    def _():
        refs[-1][...] = lower[...].astype(F32)


def place_half(upper, lower, begin, rows, target, index):
    cut, width = upper.shape[0] // TILE, upper.shape[1]
    first, blocks = begin // TILE, rows // TILE
    grid_spec = pltpu.PrefetchScalarGridSpec(
        num_scalar_prefetch=1,
        grid=(blocks,),
        in_specs=[
            pl.BlockSpec((TILE, width), lambda at, half: (jnp.minimum(first + at, cut - 1), 0)),
            pl.BlockSpec((TILE, width), lambda at, half: (jnp.maximum(first + at - cut, 0), 0)),
        ]
        + [pl.BlockSpec(memory_space=pl.ANY)] * (target is not None),
        out_specs=pl.BlockSpec((TILE, width), lambda at, half: (half[0] * blocks + at, 0)),
    )
    return pl.pallas_call(
        lambda *refs: place_kernel(first, cut, *refs),
        grid_spec=grid_spec,
        out_shape=shape_of((2 * rows, width), F32),
        input_output_aliases={} if target is None else {3: 0},
        compiler_params=pltpu.CompilerParams(
            vmem_limit_bytes=VMEM_BYTES, dimension_semantics=("arbitrary",)
        ),
        cost_estimate=LIGHT,
    )(index[None].astype(jnp.int32), upper, lower, *([] if target is None else [target]))


def shards(
    tokens,
    doc_ids,
    routes,
    norm_in_gain,
    w_query,
    w_key,
    w_value,
    w_out,
    norm_mid_gain,
    w_router,
    w_expert_in,
    w_expert_down,
    cotangent,
):
    bf16, f32 = BF16, F32
    row_count, model_width = tokens.shape
    query_cols = w_query.shape[1]
    kv_cols = w_key.shape[1]
    own_rows = w_query.shape[0]
    own_experts, ff = w_expert_down.shape[:2]
    shard_at = lax.axis_index("shard")
    reps, shard_count = (lax.axis_size("rep"), lax.axis_size("shard"))

    mask_own = jnp.any(
        routes[:, :, None] == jnp.arange(PAD, dtype=jnp.int32)[None, None, :], axis=1
    )
    side = jnp.concatenate([cotangent, mask_own.astype(bf16)], axis=1)
    side_parts, side_right, side_left = gather_near(side, shard_count)

    small = jnp.concatenate(
        [
            w_router,
            norm_in_gain[:, None],
            norm_mid_gain[:, None],
            jnp.zeros((own_rows, PAD - EXPERTS - 2), bf16),
        ],
        axis=1,
    )
    all_w = gather_all(
        jnp.concatenate([w_query, w_key, w_value, w_out, small], axis=1), reps, shard_count, 1
    )
    small_at = query_cols + 2 * kv_cols + w_out.shape[1]

    cosine, sine_table = rotary_tables(positions(doc_ids), HEAD_DIM)
    cosine, sine_table = cosine[:, 0, :], sine_table[:, 0, :]
    ct = jnp.concatenate([cosine] * 4, axis=1)
    st = jnp.concatenate([-sine_table, sine_table] * 2, axis=1)
    all_w, side_parts, side_right, side_left = tie(all_w, side_parts, side_right, side_left)
    side_far = gather_far(side_right, side_left, shard_count)
    second_low, middle, *kept = forward_block(
        tokens, all_w, ct, st, doc_ids, query_cols, kv_cols
    )
    second_low, side_far = tie(second_low, side_far)
    far_at = shard_count // 2
    side_parts[far_at] = jnp.concatenate(side_far)
    second_parts, *ends = gather_near(second_low, shard_count)
    first_expert = (shard_at * own_experts)[None].astype(jnp.int32)
    order = sorted(range(shard_count), key=lambda k: min(k, shard_count - k))
    order = order[:-2] + order[:-3:-1]
    small_full = all_w[:, small_at:]
    combs, backs, kept_parts = {}, {}, ()
    back_far = None
    for place, k in enumerate(order):
        gated, grad_both, combs[k], backs[k] = expert_block(
            first_expert,
            second_parts[k],
            side_parts[k],
            small_full,
            w_expert_in,
            w_expert_down,
            place,
            shard_count,
            kept_parts,
        )
        if k == 0:
            gated, grad_both, second_parts, ends = tie(gated, grad_both, second_parts, ends)
            second_parts[far_at] = jnp.concatenate(gather_far(*ends, shard_count))
        kept_parts = (gated, grad_both)
        if k == far_at:
            back_far = far_first(backs, shard_count)
        elif back_far is not None:
            gated, grad_both, back_far, backs = tie(gated, grad_both, back_far, backs)
            kept_parts = (gated, grad_both)
    back_near = near_rest(backs, *back_far, shard_count)
    group_rows = shard_count * row_count
    second_all = jnp.concatenate([second_parts[k] for k in order])
    dy_all = jnp.concatenate([side_parts[k][:, :model_width] for k in order])
    grad_in_here = jnp.einsum(
        "td,etf->edf",
        second_all,
        grad_both.reshape(own_experts, group_rows, 2 * ff),
        preferred_element_type=f32,
    ).astype(bf16)
    grad_down_here = jnp.einsum(
        "etf,td->efd",
        gated.reshape(own_experts, group_rows, ff),
        dy_all,
        preferred_element_type=f32,
    ).astype(bf16)

    rep_at = lax.axis_index("rep")
    bits = reps.bit_length() - 1
    bit_of = [rep_at // 2**bit % 2 for bit in range(bits)]
    grads = [g.reshape(-1, model_width) for g in (grad_in_here, grad_down_here)]
    away = jnp.concatenate([part_of(g, 1 - bit_of[0]) for g in grads])
    mine = jnp.concatenate([part_of(g, bit_of[0]) for g in grads])
    held = add_low(mine, across(away, reps, 0))
    back_near, held, combs = tie(back_near, held, combs)
    comb_far = far_first(combs, shard_count)
    cut = held.shape[0] // 2
    blocks, block_orders = [held[:cut], held[cut:]], orders_of(bits)
    steps = bits - 1
    came = [sent(b, reps, o[0], bit_of) for b, o in zip(blocks, block_orders)]
    joint, grad_tokens = backward_block(
        tokens, side, middle, second_low, (backs[0], *back_near), all_w, ct, st, doc_ids, kept
    )
    joint, came, comb_far, blocks, combs = tie(joint, came, comb_far, blocks, combs)
    comb_near = near_rest(combs, *comb_far, shard_count)
    blocks = [kept_sum(b, c, o[0], bit_of) for b, c, o in zip(blocks, came, block_orders)]
    joint, blocks = tie(joint, blocks)
    came = [sent(b, reps, o[1], bit_of) for b, o in zip(blocks, block_orders)]
    joint_own = reduce_all(joint, reps, shard_count, 3)
    joint_own, blocks, comb_near, came = tie(joint_own, blocks, comb_near, came)
    mixed = middle + combs[0].astype(f32) + sum(part.astype(f32) for part in comb_near)
    mixed = mixed.astype(bf16)
    blocks = [kept_sum(b, c, o[1], bit_of) for b, c, o in zip(blocks, came, block_orders)]
    for at in range(2, steps):
        blocks = [
            kept_sum(b, sent(b, reps, o[at], bit_of), o[at], bit_of)
            for b, o in zip(blocks, block_orders)
        ]
    for at in reversed(range(steps)):
        blocks = [
            both_halves(b, across(b, reps, o[at]), bit_of[o[at]])
            for b, o in zip(blocks, block_orders)
        ]
    others = [across(b, reps, 0) for b in blocks]
    in_rows, down_rows = [g.shape[0] // 2 for g in grads]
    grad_in_own = place_half(*blocks, 0, in_rows, None, bit_of[0])
    grad_down_own = place_half(*blocks, in_rows, down_rows, None, bit_of[0])
    grad_in_own = place_half(*others, 0, in_rows, grad_in_own, 1 - bit_of[0])
    grad_down_own = place_half(*others, in_rows, down_rows, grad_down_own, 1 - bit_of[0])
    widths = (query_cols, kv_cols, kv_cols, w_out.shape[1], PAD)
    query_own, key_own, value_own, out_own, small_own = local_call(
        split_kernel, [shape_of((own_rows, wide), f32) for wide in widths], [], joint_own
    )
    return (
        mixed,
        grad_tokens,
        small_own[:, EXPERTS],
        query_own,
        key_own,
        value_own,
        out_own,
        small_own[:, EXPERTS + 1],
        small_own[:, :EXPERTS],
        grad_in_own.reshape(own_experts, model_width, 2 * ff),
        grad_down_own.reshape(own_experts, ff, model_width),
    )


def solution(mesh):
    in_specs = (
        P(("rep", "shard"), None),
        P(("rep", "shard")),
        P(("rep", "shard"), None),
        P("shard"),
        P("shard", None),
        P("shard", None),
        P("shard", None),
        P("shard", None),
        P("shard"),
        P("shard", None),
        P("shard", None, None),
        P("shard", None, None),
        P(("rep", "shard"), None),
    )
    out_specs = (
        P(("rep", "shard"), None),
        P(("rep", "shard"), None),
        P("shard"),
        P("shard", None),
        P("shard", None),
        P("shard", None),
        P("shard", None),
        P("shard"),
        P("shard", None),
        P("shard", None, None),
        P("shard", None, None),
    )
    return jax.shard_map(shards, mesh=mesh, in_specs=in_specs, out_specs=out_specs, check_vma=False)
```

```python
import jax
import jax.numpy as jnp
from jax import lax
from jax.experimental import pallas as pl
from jax.experimental.pallas import tpu as pltpu
from jax.sharding import PartitionSpec as P

HEADS = 16
KV_HEADS = 8
HEAD_DIM = 64
EXPERTS = 16
PAD = 128
VMEM_BYTES = 54 * 2**20


epsilon = 1e-06
rope_base = 10000.0
masked_score = -1e30


def positions(doc_rows):
    row_count = doc_rows.shape[0]
    places = jnp.arange(row_count, dtype=jnp.int32)
    begins = jnp.sum((doc_rows[None, :] < doc_rows[:, None]).astype(jnp.int32), axis=1)
    return places - begins


def rotary_tables(places, head_width):
    half_width = head_width // 2
    frequencies = jnp.power(
        rope_base, -2.0 * jnp.arange(half_width, dtype=jnp.float32) / head_width
    )
    angles = places.astype(jnp.float32)[:, None] * frequencies[None, :]
    return (jnp.cos(angles)[:, None, :], jnp.sin(angles)[:, None, :])


MESH = pl.DeviceIdType.MESH
HALVES = 2


def bit_orders(reps):
    bits = reps.bit_length() - 1
    first = list(range(bits))
    return (first, first[:1] + first[1:][::-1])


def rep_place(rep_at, order):
    place = 0
    for bit in order:
        place = place * 2 + rep_at // 2**bit % 2
    return place


def partner(rep_at, bit):
    return rep_at + 2**bit * (1 - 2 * (rep_at // 2**bit % 2))


def halves_of(columns):
    tiles = columns // 128
    left = (tiles + 1) // 2 * 128
    return (pl.ds(0, left), pl.ds(left, columns - left))


def meet(rep_at, shard_at, reps, shard_count):
    barrier = pltpu.get_barrier_semaphore()
    bits = reps.bit_length() - 1
    for bit in range(bits):
        pl.semaphore_signal(
            barrier, inc=1, device_id=(partner(rep_at, bit), shard_at), device_id_type=MESH
        )
    for step in range(1, shard_count):
        pl.semaphore_signal(
            barrier,
            inc=1,
            device_id=(rep_at, (shard_at + step) % shard_count),
            device_id_type=MESH,
        )
    pl.semaphore_wait(barrier, bits + shard_count - 1)


def spread(out, orders, columns, rep_at, shard_at, sends, recvs):
    bits = len(orders[0])
    flying = [None] * HALVES
    for at in reversed(range(bits)):
        window = 2 ** (bits - 1 - at)
        for half in range(HALVES):
            order = orders[half]
            place = rep_place(rep_at, order)
            begin = place // window * window
            if flying[half] is not None:
                flying[half].wait()
            block = out.at[:, pl.ds(begin, window), :, columns[half]]
            flying[half] = pltpu.make_async_remote_copy(
                src_ref=block,
                dst_ref=block,
                send_sem=sends.at[half, at],
                recv_sem=recvs.at[half, at],
                device_id=(partner(rep_at, order[at]), shard_at),
                device_id_type=MESH,
            )
            flying[half].start()
    for half in range(HALVES):
        flying[half].wait()


def spread_others(out, orders, columns, rep_at, shard_at, shard_count, sends, recvs):
    bits = len(orders[0])
    flying = [[] for _ in range(HALVES)]
    for at in reversed(range(bits)):
        window = 2 ** (bits - 1 - at)
        for half in range(HALVES):
            order = orders[half]
            place = rep_place(rep_at, order)
            begin = place // window * window
            for copy in flying[half]:
                copy.wait()
            flying[half] = []
            for step in range(1, shard_count):
                block = out.at[
                    (shard_at + step) % shard_count, pl.ds(begin, window), :, columns[half]
                ]
                copy = pltpu.make_async_remote_copy(
                    src_ref=block,
                    dst_ref=block,
                    send_sem=sends.at[half, at, step],
                    recv_sem=recvs.at[half, at, step],
                    device_id=(partner(rep_at, order[at]), shard_at),
                    device_id_type=MESH,
                )
                copy.start()
                flying[half].append(copy)
    for half in range(HALVES):
        for copy in flying[half]:
            copy.wait()


def gather_kernel(reps, shard_count, *refs):
    weights, (dy, routes, out, side, right, left) = refs[:5], refs[5:11]
    piece, z_send, z_recv, sends, recvs, d_send, d_recv = refs[11:]
    rep_at, shard_at = (lax.axis_index("rep"), lax.axis_index("shard"))
    orders = bit_orders(reps)
    columns = halves_of(piece.shape[-1])
    begin = 0
    for ref in weights:
        piece[:, :, begin : begin + ref.shape[-1]] = ref[...]
        begin += ref.shape[-1]
    meet(rep_at, shard_at, reps, shard_count)
    flying = []
    for half in range(HALVES):
        place = rep_place(rep_at, orders[half])
        for step in range(1, shard_count):
            copy = pltpu.make_async_remote_copy(
                src_ref=piece.at[place, :, columns[half]],
                dst_ref=out.at[shard_at, place, :, columns[half]],
                send_sem=z_send.at[half, step - 1],
                recv_sem=z_recv.at[half, step - 1],
                device_id=(rep_at, (shard_at + step) % shard_count),
                device_id_type=MESH,
            )
            copy.start()
            flying.append(copy)

    @pl.loop(0, reps)
    def _(index):
        out[shard_at, index] = piece[index]

    rows, width = dy.shape
    for at in range(0, rows, LANES):
        here = slice(at, at + LANES)
        side[here, :width] = dy[here, :]
        named = routes[here, :]
        lane = lane_of((LANES, PAD))
        mask = lane == named[:, 0:1]
        for k in range(1, named.shape[1]):
            mask = mask | (lane == named[:, k : k + 1])
        side[here, width:] = jnp.where(mask, 1.0, 0.0).astype(side.dtype)
    for copy in flying:
        copy.wait()
    flying = []
    if shard_count > 1:
        for number, (step, target) in enumerate(((1, right), (shard_count - 1, left))):
            copy = pltpu.make_async_remote_copy(
                src_ref=side,
                dst_ref=target,
                send_sem=d_send.at[number],
                recv_sem=d_recv.at[number],
                device_id=(rep_at, (shard_at + step) % shard_count),
                device_id_type=MESH,
            )
            copy.start()
            flying.append(copy)
    spread_others(out, orders, columns, rep_at, shard_at, shard_count, sends, recvs)
    for copy in flying:
        copy.wait()


def gather_all(weights, dy, routes, reps, shard_count, number):
    own = weights[0].shape[0]
    width = sum(w.shape[1] for w in weights)
    rows = own // reps
    bits = reps.bit_length() - 1
    kind = weights[0].dtype
    wide = jax.ShapeDtypeStruct((dy.shape[0], dy.shape[1] + PAD), kind)
    out, side, right, left = pl.pallas_call(
        lambda *refs: gather_kernel(reps, shard_count, *refs),
        out_shape=[jax.ShapeDtypeStruct((shard_count, reps, rows, width), kind), wide, wide, wide],
        in_specs=[pl.BlockSpec(memory_space=pltpu.VMEM)] * (len(weights) + 2),
        out_specs=[pl.BlockSpec(memory_space=pltpu.VMEM)] * 4,
        scratch_shapes=[
            pltpu.VMEM((reps, rows, width), kind),
            pltpu.SemaphoreType.DMA((HALVES, shard_count)),
            pltpu.SemaphoreType.DMA((HALVES, shard_count)),
            pltpu.SemaphoreType.DMA((HALVES, bits, shard_count)),
            pltpu.SemaphoreType.DMA((HALVES, bits, shard_count)),
            pltpu.SemaphoreType.DMA((2,)),
            pltpu.SemaphoreType.DMA((2,)),
        ],
        compiler_params=pltpu.CompilerParams(
            collective_id=number, has_side_effects=True, vmem_limit_bytes=VMEM_BYTES
        ),
        cost_estimate=pl.CostEstimate(
            flops=0, bytes_accessed=shard_count * own * width, transcendentals=0
        ),
    )(*[w.reshape(reps, rows, w.shape[1]) for w in weights], dy, routes)
    return out.reshape(shard_count * own, width), side, right, left


def reduce_kernel(reps, shard_count, parts, out, *scratch):
    bits = reps.bit_length() - 1
    f32 = jnp.float32
    landed = [scratch[half * bits : (half + 1) * bits] for half in range(HALVES)]
    rest = scratch[HALVES * bits :]
    if shard_count > 1:
        z_land, (z_send, z_recv) = (rest[:HALVES], rest[HALVES : HALVES + 2])
        rest = rest[HALVES + 2 :]
    r_send, r_recv, sends, recvs = rest
    rep_at, shard_at = (lax.axis_index("rep"), lax.axis_index("shard"))
    orders = bit_orders(reps)
    columns = halves_of(parts.shape[-1])
    meet(rep_at, shard_at, reps, shard_count)
    flying = [None] * HALVES

    def source(half, at):
        return parts.at[:, :, :, columns[half]] if at == 0 else landed[half][at - 1]

    def begin(half, at):
        bit = orders[half][at]
        many = reps // 2 ** (at + 1)
        away = (1 - rep_at // 2**bit % 2) * many
        flying[half] = pltpu.make_async_remote_copy(
            src_ref=source(half, at).at[:, pl.ds(away, many)],
            dst_ref=landed[half][at],
            send_sem=r_send.at[half, at],
            recv_sem=r_recv.at[half, at],
            device_id=(partner(rep_at, bit), shard_at),
            device_id_type=MESH,
        )
        flying[half].start()

    for half in range(HALVES):
        begin(half, 0)
    for at in range(bits):
        many = reps // 2 ** (at + 1)
        for half in range(HALVES):
            flying[half].wait()
            keep = rep_at // 2 ** orders[half][at] % 2 * many
            mine, came = (source(half, at), landed[half][at])

            @pl.loop(0, parts.shape[0] * many)
            def _(index):
                outer, inner = (index // many, index % many)
                came[outer, inner] = (
                    came[outer, inner].astype(f32) + mine[outer, keep + inner].astype(f32)
                ).astype(came.dtype)

            if at + 1 < bits:
                begin(half, at + 1)
    copies = []
    if shard_count > 1:
        for half in range(HALVES):
            for step in range(1, shard_count):
                to = (shard_at + step) % shard_count
                copy = pltpu.make_async_remote_copy(
                    src_ref=landed[half][-1].at[to, 0],
                    dst_ref=z_land[half].at[step - 1],
                    send_sem=z_send.at[half, step - 1],
                    recv_sem=z_recv.at[half, step - 1],
                    device_id=(rep_at, to),
                    device_id_type=MESH,
                )
                copy.start()
                copies.append(copy)
    for copy in copies:
        copy.wait()
    for half in range(HALVES):
        place = rep_place(rep_at, orders[half])
        if shard_count > 1:
            total = landed[half][-1][shard_at, 0].astype(f32)
            for step in range(1, shard_count):
                total = total + z_land[half][step - 1].astype(f32)
            out[0, place, :, columns[half]] = total.astype(out.dtype)
        else:
            out[0, place, :, columns[half]] = landed[half][-1][0, 0]
    spread(out, orders, columns, rep_at, shard_at, sends, recvs)


def reduce_all(parts, reps, shard_count, number):
    total, width = parts.shape
    rows = total // (reps * shard_count)
    bits = reps.bit_length() - 1
    widths = (halves_of(width)[0].size, halves_of(width)[1].size)
    scratch = []
    for wide in widths:
        for at in range(bits):
            scratch.append(
                pltpu.VMEM((shard_count, reps // 2 ** (at + 1), rows, wide), parts.dtype)
            )
    if shard_count > 1:
        scratch += [pltpu.VMEM((shard_count - 1, rows, wide), parts.dtype) for wide in widths]
        scratch += [pltpu.SemaphoreType.DMA((HALVES, shard_count)) for _ in range(2)]
    scratch += [pltpu.SemaphoreType.DMA((HALVES, bits)) for _ in range(4)]
    out = pl.pallas_call(
        lambda *refs: reduce_kernel(reps, shard_count, *refs),
        out_shape=jax.ShapeDtypeStruct((1, reps, rows, width), parts.dtype),
        in_specs=[pl.BlockSpec(memory_space=pltpu.VMEM)],
        out_specs=pl.BlockSpec(memory_space=pltpu.VMEM),
        scratch_shapes=scratch,
        compiler_params=pltpu.CompilerParams(
            collective_id=number, has_side_effects=True, vmem_limit_bytes=VMEM_BYTES
        ),
        cost_estimate=pl.CostEstimate(
            flops=0, bytes_accessed=total * width, transcendentals=0
        ),
    )(parts.reshape(shard_count, reps, rows, width))
    return out.reshape(reps * rows, width)


F32, BF16 = jnp.float32, jnp.bfloat16
LANES = 128
TILE = 256
LIGHT = pl.CostEstimate(flops=10**6, bytes_accessed=10**5, transcendentals=0)
GROUP = HEADS // KV_HEADS


def dot(a, b):
    return lax.dot_general(a, b, (((1,), (0,)), ((), ())), preferred_element_type=F32)


def dot_nt(a, b):
    return lax.dot_general(a, b, (((1,), (1,)), ((), ())), preferred_element_type=F32)


def lane_of(shape):
    return lax.broadcasted_iota(jnp.int32, shape, len(shape) - 1)


def swap_halves(values):
    near = lane_of(values.shape) % HEAD_DIM < HEAD_DIM // 2
    up = pltpu.roll(values, LANES - HEAD_DIM // 2, 1)
    down = pltpu.roll(values, HEAD_DIM // 2, 1)
    return jnp.where(near, up, down)


def rope_block(values, ct, st):
    return values * ct + swap_halves(values) * st


def unrope_block(values, ct, st):
    return values * ct - swap_halves(values) * st


def low_high(block, side):
    lane = lane_of(block.shape)
    wide = block.astype(F32)
    kept = jnp.where((lane < HEAD_DIM) if side == 0 else (lane >= HEAD_DIM), wide, 0.0)
    moved = pltpu.roll(kept, HEAD_DIM, 1)
    pair = (kept, moved) if side == 0 else (moved, kept)
    return [item.astype(BF16) for item in pair]


def fill_bias(bias, doc_col, doc_row):
    rows = bias.shape[0]
    keys = lax.broadcasted_iota(jnp.int32, (TILE, rows), 0)
    queries = lax.broadcasted_iota(jnp.int32, (TILE, rows), 1)
    for start in range(0, rows, TILE):
        allowed = (doc_col[start : start + TILE, :] == doc_row[...]) & (keys + start <= queries)
        bias[start : start + TILE, :] = jnp.where(allowed, 0.0, masked_score)


def tile_at(index, width=TILE):
    return pl.ds(pl.multiple_of(index * width, width), width)


def gate_softmax(second, small, mask):
    logits = dot(second, small)
    chosen = jnp.where(mask, logits, masked_score)
    gate_exp = jnp.where(mask, jnp.exp(chosen - jnp.max(chosen, axis=1, keepdims=True)), 0.0)
    return gate_exp / jnp.sum(gate_exp, axis=1, keepdims=True)


def forward_kernel(
    tokens, w, ct, st, doc_col, doc_row,
    second, middle, first_t, q8, keys, values, att_t, lse,
    first, att, bias,
):
    rows, width = tokens.shape
    q_cols, kv_cols = q8.shape[1], keys.shape[1]
    small_at = w.shape[1] - PAD
    gains = w[:, small_at:].astype(F32).T
    gain_in, gain_mid = gains[EXPERTS : EXPERTS + 1], gains[EXPERTS + 1 : EXPERTS + 2]
    for at in range(0, rows, LANES):
        x = tokens[at : at + LANES, :].astype(F32)
        scale = lax.rsqrt(jnp.mean(x * x, axis=-1, keepdims=True) + epsilon)
        low = (x * scale * gain_in).astype(BF16)
        first[at : at + LANES, :] = low
        first_t[:, at : at + LANES] = low.T

    def project(index):
        return dot(first[...], w[:, tile_at(index)])

    def roped(index):
        part = project(index)
        return jnp.concatenate(
            [
                rope_block(part[:, at : at + LANES], ct[...], st[...])
                for at in range(0, TILE, LANES)
            ],
            axis=1,
        )

    @pl.loop(0, q_cols // TILE)
    def _(j):
        q8[:, tile_at(j)] = (roped(j) * HEAD_DIM**-0.5).astype(BF16)

    @pl.loop(0, kv_cols // TILE)
    def _(j):
        keys[:, tile_at(j)] = roped(q_cols // TILE + j).astype(BF16)

    @pl.loop(0, kv_cols // TILE)
    def _(j):
        values[:, tile_at(j)] = project((q_cols + kv_cols) // TILE + j).astype(BF16)

    fill_bias(bias, doc_col, doc_row)

    @pl.loop(0, kv_cols // LANES)
    def _(pair):
        k128, v128 = keys[:, tile_at(pair, LANES)], values[:, tile_at(pair, LANES)]
        v_t = v128.astype(F32).T.astype(BF16)
        for side in range(2):
            low_k = low_high(k128, side)
            q = q8[:, tile_at(pair * 2 + side, LANES)]
            v_s = v_t[side * HEAD_DIM : (side + 1) * HEAD_DIM]
            for h in range(GROUP):
                head = pair * 2 * GROUP + side * GROUP + h
                for begin in range(0, rows, TILE):
                    kr = begin + TILE
                    s = dot_nt(low_k[h][:kr], q[begin:kr]) + bias[:kr, begin:kr]
                    top = jnp.max(s, axis=0, keepdims=True)
                    p = jnp.exp(s - top)
                    total = jnp.sum(p, axis=0, keepdims=True)
                    probs = (p * (1.0 / total)).astype(BF16)
                    lse[head, :, begin:kr] = top + jnp.log(total)
                    att_t[tile_at(head, HEAD_DIM), begin:kr] = dot(v_s[:, :kr], probs).astype(BF16)

    @pl.loop(0, width // TILE)
    def _(j):
        att[:, tile_at(j)] = att_t[tile_at(j), :].astype(F32).T.astype(BF16)

    @pl.loop(0, width // TILE)
    def _(j):
        out_w = w[:, pl.ds(pl.multiple_of(q_cols + 2 * kv_cols + j * TILE, TILE), TILE)]
        middle[:, tile_at(j)] = tokens[:, tile_at(j)].astype(F32) + dot(att[...], out_w)

    for at in range(0, rows, LANES):
        x = middle[at : at + LANES, :]
        scale = lax.rsqrt(jnp.mean(x * x, axis=-1, keepdims=True) + epsilon)
        second[at : at + LANES, :] = (x * scale * gain_mid).astype(BF16)


def split_kernel(joint, *outs):
    begin = 0
    for out in outs:
        out[...] = joint[:, begin : begin + out.shape[1]].astype(F32)
        begin += out.shape[1]


def shape_of(shape, kind):
    return jax.ShapeDtypeStruct(shape, kind)


def local_call(kernel, outs, scratch, *args):
    return pl.pallas_call(
        kernel,
        out_shape=outs,
        in_specs=[pl.BlockSpec(memory_space=pltpu.VMEM)] * len(args),
        out_specs=[pl.BlockSpec(memory_space=pltpu.VMEM)] * len(outs),
        scratch_shapes=scratch,
        compiler_params=pltpu.CompilerParams(vmem_limit_bytes=VMEM_BYTES),
        cost_estimate=LIGHT,
    )(*args)


def forward_block(tokens, w, ct, st, doc_ids, q_cols, kv_cols):
    rows, width = tokens.shape
    outs = [
        shape_of((rows, width), BF16),
        shape_of((rows, width), F32),
        shape_of((width, rows), BF16),
        shape_of((rows, q_cols), BF16),
        shape_of((rows, kv_cols), BF16),
        shape_of((rows, kv_cols), BF16),
        shape_of((q_cols, rows), BF16),
        shape_of((HEADS, 1, rows), F32),
    ]
    scratch = [
        pltpu.VMEM((rows, width), BF16),
        pltpu.VMEM((rows, q_cols), BF16),
        pltpu.VMEM((rows, rows), F32),
    ]
    return local_call(
        forward_kernel, outs, scratch, tokens, w, ct, st, doc_ids[:, None], doc_ids[None, :]
    )


def backward_kernel(
    tokens, side, middle, second, back_own, back_left, back_right, w, ct, st, doc_col, doc_row,
    q8, keys, values, att_t, lse,
    grad_out, rows_t, grad_middle, grad_pre,
    bias, grad_branch, grad_att, dq_t, dk, dv,
):
    rows, width = tokens.shape
    q_cols, kv_cols = q8.shape[1], keys.shape[1]
    qkv_cols = q_cols + 2 * kv_cols
    small_at = w.shape[1] - PAD
    small = w[:, small_at:]
    gains = small.astype(F32).T
    gain_mid = gains[EXPERTS + 1 : EXPERTS + 2]
    tall = back_own.shape[1]
    gain_sum = jnp.zeros((1, width), F32)
    router_t = jnp.zeros((PAD, width), F32)
    for at in range(0, rows, LANES):
        here = slice(at, at + LANES)
        mask = side[here, width:] > 0
        gates = gate_softmax(second[here, :], small, mask)
        came = (
            back_own[here, width:].astype(F32)
            + back_left[here, width:].astype(F32)
            + back_right[here, width:].astype(F32)
        )
        gate_back = jnp.where(
            lane_of(came.shape) < EXPERTS, came + pltpu.roll(came, tall - width - EXPERTS, 1), 0.0
        )
        grad_logits = gates * (gate_back - jnp.sum(gates * gate_back, axis=1, keepdims=True))
        low_logits = grad_logits.astype(BF16)
        router_t += dot(grad_logits.T.astype(BF16), second[here, :])
        grad_second = (
            back_own[here, :width].astype(F32)
            + back_left[here, :width].astype(F32)
            + back_right[here, :width].astype(F32)
            + dot_nt(low_logits, small)
        )
        x = middle[here, :]
        scale = lax.rsqrt(jnp.mean(x * x, axis=-1, keepdims=True) + epsilon)
        normed = x * scale
        gain_sum += jnp.sum(grad_second * normed, axis=0, keepdims=True)
        u = grad_second * gain_mid
        inner = jnp.mean(u * normed, axis=-1, keepdims=True)
        total = side[here, :width].astype(F32) + scale * (u - normed * inner)
        grad_middle[here, :] = total
        grad_branch[here, :] = total.astype(BF16)
    rows_t[...] = router_t
    rows_t[EXPERTS + 1 : EXPERTS + 2, :] = gain_sum

    @pl.loop(0, width // TILE)
    def _(j):
        grad_out[:, tile_at(j)] = dot(att_t[...], grad_branch[:, tile_at(j)]).astype(BF16)
        out_rows = w[tile_at(j), pl.ds(qkv_cols, width)]
        grad_att[:, tile_at(j)] = dot_nt(grad_branch[...], out_rows).astype(BF16)

    fill_bias(bias, doc_col, doc_row)

    @pl.loop(0, kv_cols // LANES)
    def _(pair):
        k128, v128 = keys[:, tile_at(pair, LANES)], values[:, tile_at(pair, LANES)]
        k_t = k128.astype(F32).T.astype(BF16)
        sums = []
        for side_at in range(2):
            low_k, low_v = low_high(k128, side_at), low_high(v128, side_at)
            q = q8[:, tile_at(pair * 2 + side_at, LANES)]
            grad_o = grad_att[:, tile_at(pair * 2 + side_at, LANES)]
            k_s = k_t[side_at * HEAD_DIM : (side_at + 1) * HEAD_DIM]
            for h in range(GROUP):
                head = pair * 2 * GROUP + side_at * GROUP + h
                for begin in reversed(range(0, rows, TILE)):
                    kr = begin + TILE
                    s = dot_nt(low_k[h][:kr], q[begin:kr]) + bias[:kr, begin:kr]
                    p = jnp.exp(s - lse[head, :, begin:kr])
                    dp = dot_nt(low_v[h][:kr], grad_o[begin:kr])
                    inner = jnp.sum(p * dp, axis=0, keepdims=True)
                    ds = (p * (dp - inner)).astype(BF16)
                    dq_t[h * HEAD_DIM : (h + 1) * HEAD_DIM, begin:kr] = dot(k_s[:, :kr], ds)
                    more_k, more_v = dot(ds, q[begin:kr]), dot(p.astype(BF16), grad_o[begin:kr])
                    if kr == rows:
                        dk[h, :, :], dv[h, :, :] = more_k, more_v
                    else:
                        dk[h, :kr, :] += more_k
                        dv[h, :kr, :] += more_v
            grad_q = unrope_block(dq_t[...].T * HEAD_DIM**-0.5, ct[...], st[...])
            grad_pre[:, tile_at(pair * 2 + side_at, LANES)] = grad_q.astype(BF16)
            left = lane_of((rows, LANES)) < HEAD_DIM
            mixed_k = jnp.where(left, dk[0], dk[1])
            mixed_v = jnp.where(left, dv[0], dv[1])
            sums.append(
                (mixed_k + pltpu.roll(mixed_k, HEAD_DIM, 1), mixed_v + pltpu.roll(mixed_v, HEAD_DIM, 1))
            )
        left = lane_of((rows, LANES)) < HEAD_DIM
        grad_k = unrope_block(jnp.where(left, sums[0][0], sums[1][0]), ct[...], st[...])
        grad_v = jnp.where(left, sums[0][1], sums[1][1])
        k_at = pl.multiple_of(q_cols + pair * LANES, LANES)
        v_at = pl.multiple_of(q_cols + kv_cols + pair * LANES, LANES)
        grad_pre[:, pl.ds(k_at, LANES)] = grad_k.astype(BF16)
        grad_pre[:, pl.ds(v_at, LANES)] = grad_v.astype(BF16)


def finish_kernel(
    tokens, w, grad_middle, grad_pre, grad_out, rows_in, first_t,
    joint, grad_tokens,
    grad_first, rows_t,
):
    rows, width = tokens.shape
    qkv_cols = grad_pre.shape[1]
    small_at = w.shape[1] - PAD
    gain_in = w[:, small_at:].astype(F32).T[EXPERTS : EXPERTS + 1]
    joint[:, qkv_cols:small_at] = grad_out[...]
    rows_t[...] = rows_in[...]

    @pl.loop(0, qkv_cols // TILE)
    def _(j):
        joint[:, tile_at(j)] = dot(first_t[...], grad_pre[:, tile_at(j)]).astype(BF16)

    @pl.loop(0, width // TILE)
    def _(j):
        grad_first[:, tile_at(j)] = dot_nt(grad_pre[...], w[tile_at(j), pl.ds(0, qkv_cols)])

    gain_sum = jnp.zeros((1, width), F32)
    for at in range(0, rows, LANES):
        here = slice(at, at + LANES)
        x = tokens[here, :].astype(F32)
        scale = lax.rsqrt(jnp.mean(x * x, axis=-1, keepdims=True) + epsilon)
        normed = x * scale
        columns = grad_first[here, :]
        gain_sum += jnp.sum(columns * normed, axis=0, keepdims=True)
        u = columns * gain_in
        inner = jnp.mean(u * normed, axis=-1, keepdims=True)
        grad_tokens[here, :] = grad_middle[here, :] + scale * (u - normed * inner)
    rows_t[EXPERTS : EXPERTS + 1, :] = gain_sum
    joint[:, pl.ds(small_at, PAD)] = rows_t[...].T.astype(BF16)


def backward_block(tokens, side, middle, second, backs, w, ct, st, doc_ids, kept):
    rows, width = tokens.shape
    q_cols, kv_cols = kept[1].shape[1], kept[2].shape[1]
    outs = [
        shape_of((width, width), BF16),
        shape_of((PAD, width), F32),
        shape_of((rows, width), F32),
        shape_of((rows, q_cols + 2 * kv_cols), BF16),
    ]
    scratch = [
        pltpu.VMEM((rows, rows), F32),
        pltpu.VMEM((rows, width), BF16),
        pltpu.VMEM((rows, q_cols), BF16),
        pltpu.VMEM((LANES, rows), F32),
        pltpu.VMEM((GROUP, rows, LANES), F32),
        pltpu.VMEM((GROUP, rows, LANES), F32),
    ]
    return local_call(
        backward_kernel, outs, scratch,
        tokens, side, middle, second, *backs, w, ct, st, doc_ids[:, None], doc_ids[None, :], *kept[1:],
    )


def finish_block(tokens, w, grad_middle, grad_pre, grad_out, rows_t, first_t):
    rows, width = tokens.shape
    outs = [shape_of((width, w.shape[1]), BF16), shape_of((rows, width), F32)]
    scratch = [pltpu.VMEM((rows, width), F32), pltpu.VMEM((PAD, width), F32)]
    return local_call(
        finish_kernel, outs, scratch, tokens, w, grad_middle, grad_pre, grad_out, rows_t, first_t
    )


def expert_kernel(
    aliased, first_expert, second, side, small, in_w, down_w, *refs
):
    gated_t, grad_both, second_t, dy, comb, back = refs[4 * aliased : 4 * aliased + 6]
    gates, grad_gates, comb_sum, back_sum, gated = refs[4 * aliased + 6 :]
    rows, width = second.shape
    ff = down_w.shape[1]
    at = pl.program_id(0)
    lane = lane_of((rows, PAD))

    @pl.when(at == 0)
    def _():
        gates[...] = gate_softmax(second[...], small[...], side[:, width:] > 0)
        grad_gates[...] = jnp.zeros_like(grad_gates)
        comb_sum[...] = jnp.zeros_like(comb_sum)
        back_sum[...] = jnp.zeros_like(back_sum)
        dy[...] = side[:, :width]
        second_t[...] = second[...].T

    mine = lane == first_expert[0] + at
    gate = jnp.sum(jnp.where(mine, gates[...], 0.0), axis=1, keepdims=True)
    grad_col = jnp.zeros((rows, 1), F32)
    for start in range(0, ff, TILE):
        tile = slice(start, start + TILE)
        up_tile = slice(ff + start, ff + start + TILE)
        gate_part = dot(second[...], in_w[0, :, tile])
        up_part = dot(second[...], in_w[0, :, up_tile])
        came = dot_nt(side[:, :width], down_w[0, tile, :])
        sigmoid_gate = 0.5 * jnp.tanh(0.5 * gate_part) + 0.5
        silu_gate = gate_part * sigmoid_gate
        hidden = (silu_gate * up_part).astype(BF16).astype(F32)
        grad_col += jnp.sum(hidden * came, axis=1, keepdims=True)
        gated[:, tile] = (hidden * gate).astype(BF16)
        gated_t[0, tile, :] = gated[:, tile].T
        grad_hidden = came * gate
        slope = sigmoid_gate + silu_gate * (1.0 - sigmoid_gate)
        grad_both[0, :, tile] = (grad_hidden * up_part * slope).astype(BF16)
        grad_both[0, :, up_tile] = (grad_hidden * silu_gate).astype(BF16)
    grad_gates[...] += jnp.where(mine, grad_col, 0.0)
    for start in range(0, width, TILE):
        tile = slice(start, start + TILE)
        comb_sum[:, tile] += dot(gated[...], down_w[0, :, tile])
        back_sum[:, tile] += dot_nt(grad_both[0], in_w[0, tile, :])

    @pl.when(at == pl.num_programs(0) - 1)
    def _():
        comb[...] = comb_sum[...].astype(BF16)
        back[:, :width] = back_sum[...].astype(BF16)
        high = grad_gates[...].astype(BF16).astype(F32)
        back[:, width:] = (high + pltpu.roll(grad_gates[...] - high, EXPERTS, 1)).astype(BF16)


def expert_block(first_expert, second, side, small, in_w, down_w, place, count, before):
    rows, width = second.shape
    experts, ff = down_w.shape[:2]
    whole = lambda *shape: pl.BlockSpec(shape, lambda e: (0,) * len(shape))
    in_specs = [
        pl.BlockSpec(memory_space=pltpu.SMEM),
        whole(rows, width),
        whole(*side.shape),
        whole(*small.shape),
        pl.BlockSpec((1, width, 2 * ff), lambda e: (e, 0, 0)),
        pl.BlockSpec((1, ff, width), lambda e: (e, 0, 0)),
    ] + [pl.BlockSpec(memory_space=pl.ANY)] * len(before)
    out_specs = [
        pl.BlockSpec((1, ff, rows), lambda e: (e, 0, place)),
        pl.BlockSpec((1, rows, 2 * ff), lambda e: (e, place, 0)),
        pl.BlockSpec((width, rows), lambda e: (0, place)),
        pl.BlockSpec((rows, width), lambda e: (place, 0)),
        whole(rows, width),
        whole(*side.shape),
    ]
    outs = [
        shape_of((experts, ff, count * rows), BF16),
        shape_of((experts, count * rows, 2 * ff), BF16),
        shape_of((width, count * rows), BF16),
        shape_of((count * rows, width), BF16),
        shape_of((rows, width), BF16),
        shape_of(side.shape, BF16),
    ]
    return pl.pallas_call(
        lambda *refs: expert_kernel(bool(before), *refs),
        grid=(experts,),
        out_shape=outs,
        in_specs=in_specs,
        out_specs=out_specs,
        scratch_shapes=[
            pltpu.VMEM((rows, PAD), F32),
            pltpu.VMEM((rows, PAD), F32),
            pltpu.VMEM((rows, width), F32),
            pltpu.VMEM((rows, width), F32),
            pltpu.VMEM((rows, ff), BF16),
        ],
        input_output_aliases={6: 0, 7: 1, 8: 2, 9: 3} if before else {},
        compiler_params=pltpu.CompilerParams(
            vmem_limit_bytes=VMEM_BYTES, dimension_semantics=("arbitrary",)
        ),
        cost_estimate=LIGHT,
    )(first_expert, second, side, small, in_w, down_w, *before)


def weight_kernel(base, second_t, dy, gated_t, grad_both, grad_in, grad_down):
    @pl.loop(0, grad_in.shape[1] // TILE)
    def _(j):
        grad_in[:, tile_at(j)] = dot(second_t[...], grad_both[0, :, tile_at(j)]).astype(BF16)

    @pl.loop(0, grad_down.shape[1] // TILE)
    def _(j):
        grad_down[:, tile_at(j)] = dot(gated_t[0], dy[:, tile_at(j)]).astype(BF16)


def weight_block(base, second_t, dy, gated_t, grad_both, experts):
    width, rows = second_t.shape
    ff = gated_t.shape[1]
    grid_spec = pltpu.PrefetchScalarGridSpec(
        num_scalar_prefetch=1,
        grid=(experts,),
        in_specs=[
            pl.BlockSpec((width, rows), lambda e, at: (0, 0)),
            pl.BlockSpec((rows, width), lambda e, at: (0, 0)),
            pl.BlockSpec((1, ff, rows), lambda e, at: (at[0] + e, 0, 0)),
            pl.BlockSpec((1, rows, 2 * ff), lambda e, at: (at[0] + e, 0, 0)),
        ],
        out_specs=[
            pl.BlockSpec((width, 2 * ff), lambda e, at: (e, 0)),
            pl.BlockSpec((ff, width), lambda e, at: (e, 0)),
        ],
    )
    return pl.pallas_call(
        weight_kernel,
        grid_spec=grid_spec,
        out_shape=[shape_of((experts * width, 2 * ff), BF16), shape_of((experts * ff, width), BF16)],
        compiler_params=pltpu.CompilerParams(
            vmem_limit_bytes=VMEM_BYTES, dimension_semantics=("arbitrary",)
        ),
        cost_estimate=LIGHT,
    )(base[None].astype(jnp.int32), second_t, dy, gated_t, grad_both)


def shift(block, count, step):
    return lax.ppermute(block, "shard", [(at, (at + step) % count) for at in range(count)])


def tie(*values):
    return lax.optimization_barrier(values)


def gather_near(piece, count):
    got = {0: piece}
    right = left = piece
    for step in range(1, (count - 1) // 2 + 1):
        right, left = shift(right, count, 1), shift(left, count, -1)
        got[step], got[count - step] = right, left
    return got, right, left


def gather_far(right, left, count):
    half = right.shape[0] // 2
    return shift(right[:half], count, 1), shift(left[half:], count, -1)


def far_first(parts, count):
    half = parts[0].shape[0] // 2
    far = parts[count // 2]
    return shift(far[:half], count, -1), shift(far[half:], count, 1)


def near_rest(parts, left, right, count, after=()):
    half = parts[0].shape[0] // 2
    if count == 2:
        return jnp.concatenate([left, right], axis=0), jnp.zeros_like(parts[0]), after
    for step in reversed(range(1, count // 2)):
        near, far = parts[step], parts[count - step]
        if step == count // 2 - 1:
            left = jnp.concatenate([add_low(near[:half], left), near[half:]], axis=0)
            right = jnp.concatenate([far[:half], add_low(far[half:], right)], axis=0)
        else:
            left, right = add_low(near, left), add_low(far, right)
        if step == 1:
            left, right, after = tie(left, right, after)
        left, right = shift(left, count, -1), shift(right, count, 1)
    return left, right, after


def add_low(a, b):
    return (a.astype(F32) + b.astype(F32)).astype(BF16)


def across(block, reps, bit):
    return lax.ppermute(block, "rep", [(at, at ^ 2**bit) for at in range(reps)])


def part_of(block, index):
    half = block.shape[0] // 2
    return lax.dynamic_slice_in_dim(block, index * half, half, axis=0)


def both_halves(mine, other, index):
    first = jnp.where(index == 0, mine, other)
    last = jnp.where(index == 0, other, mine)
    return jnp.concatenate([first, last])


def orders_of(bits):
    return list(range(1, bits)), list(range(1, bits))[::-1]


def sent(block, reps, bit, bit_of):
    return across(part_of(block, 1 - bit_of[bit]), reps, bit)


def kept_sum(block, came, bit, bit_of):
    return add_low(part_of(block, bit_of[bit]), came)


def place_kernel(begin, cut, half, upper, lower, *refs):
    at = begin + pl.program_id(0)

    @pl.when(at < cut)
    def _():
        refs[-1][...] = upper[...].astype(F32)

    @pl.when(at >= cut)
    def _():
        refs[-1][...] = lower[...].astype(F32)


def place_half(upper, lower, begin, rows, target, index):
    cut, width = upper.shape[0] // TILE, upper.shape[1]
    first, blocks = begin // TILE, rows // TILE
    grid_spec = pltpu.PrefetchScalarGridSpec(
        num_scalar_prefetch=1,
        grid=(blocks,),
        in_specs=[
            pl.BlockSpec((TILE, width), lambda at, half: (jnp.minimum(first + at, cut - 1), 0)),
            pl.BlockSpec((TILE, width), lambda at, half: (jnp.maximum(first + at - cut, 0), 0)),
        ]
        + [pl.BlockSpec(memory_space=pl.ANY)] * (target is not None),
        out_specs=pl.BlockSpec((TILE, width), lambda at, half: (half[0] * blocks + at, 0)),
    )
    return pl.pallas_call(
        lambda *refs: place_kernel(first, cut, *refs),
        grid_spec=grid_spec,
        out_shape=shape_of((2 * rows, width), F32),
        input_output_aliases={} if target is None else {3: 0},
        compiler_params=pltpu.CompilerParams(
            vmem_limit_bytes=VMEM_BYTES, dimension_semantics=("arbitrary",)
        ),
        cost_estimate=LIGHT,
    )(index[None].astype(jnp.int32), upper, lower, *([] if target is None else [target]))


def shards(
    tokens,
    doc_ids,
    routes,
    norm_in_gain,
    w_query,
    w_key,
    w_value,
    w_out,
    norm_mid_gain,
    w_router,
    w_expert_in,
    w_expert_down,
    cotangent,
):
    bf16, f32 = BF16, F32
    row_count, model_width = tokens.shape
    query_cols = w_query.shape[1]
    kv_cols = w_key.shape[1]
    own_rows = w_query.shape[0]
    own_experts, ff = w_expert_down.shape[:2]
    shard_at = lax.axis_index("shard")
    reps, shard_count = (lax.axis_size("rep"), lax.axis_size("shard"))

    small = jnp.concatenate(
        [
            w_router,
            norm_in_gain[:, None],
            norm_mid_gain[:, None],
            jnp.zeros((own_rows, PAD - EXPERTS - 2), bf16),
        ],
        axis=1,
    )
    weights = [w_query, w_key, w_value, w_out, small]
    all_w, side, side_right, side_left = gather_all(
        weights, cotangent, routes, reps, shard_count, 1
    )
    small_at = query_cols + 2 * kv_cols + w_out.shape[1]

    cosine, sine_table = rotary_tables(positions(doc_ids), HEAD_DIM)
    cosine, sine_table = cosine[:, 0, :], sine_table[:, 0, :]
    ct = jnp.concatenate([cosine] * 4, axis=1)
    st = jnp.concatenate([-sine_table, sine_table] * 2, axis=1)
    side_parts = {0: side}
    for step in range(1, (shard_count - 1) // 2 + 1):
        if step > 1:
            side_right, side_left = shift(side_right, shard_count, 1), shift(side_left, shard_count, -1)
        side_parts[step], side_parts[shard_count - step] = side_right, side_left
    if shard_count > 2:
        side_far = gather_far(side_right, side_left, shard_count)
    else:
        side_far = (side_right,)
    second_low, middle, *kept = forward_block(
        tokens, all_w, ct, st, doc_ids, query_cols, kv_cols
    )
    second_low, side_far = tie(second_low, side_far)
    far_at = shard_count // 2
    side_parts[far_at] = jnp.concatenate(side_far)
    second_parts, *ends = gather_near(second_low, shard_count)
    first_expert = (shard_at * own_experts)[None].astype(jnp.int32)
    order = sorted(range(shard_count), key=lambda k: min(k, shard_count - k))
    order = order[:-2] + order[:-3:-1]
    small_full = all_w[:, small_at:]
    combs, backs, kept_parts = {}, {}, ()
    back_far = None
    for place, k in enumerate(order):
        *kept_parts, combs[k], backs[k] = expert_block(
            first_expert,
            second_parts[k],
            side_parts[k],
            small_full,
            w_expert_in,
            w_expert_down,
            place,
            shard_count,
            kept_parts,
        )
        if k == 0:
            kept_parts, second_parts, ends = tie(kept_parts, second_parts, ends)
            second_parts[far_at] = jnp.concatenate(gather_far(*ends, shard_count))
        if k == far_at:
            back_far = far_first(backs, shard_count)
        elif back_far is not None:
            kept_parts, back_far, backs = tie(kept_parts, back_far, backs)
    *back_near, kept_parts = near_rest(backs, *back_far, shard_count, kept_parts)
    gated_t, grad_both, second_t, dy_all = kept_parts

    rep_at = lax.axis_index("rep")
    bits = reps.bit_length() - 1
    bit_of = [rep_at // 2**bit % 2 for bit in range(bits)]
    half = own_experts // 2
    grads = (second_t, dy_all, gated_t, grad_both)
    away = weight_block((1 - bit_of[0]) * half, *grads, half)
    core = [across(part, reps, 0) for part in away]
    away, grads = tie(away, grads)
    mine = weight_block(bit_of[0] * half, *grads, half)
    in_rows, down_rows = [part.shape[0] for part in mine]
    cut = (in_rows + down_rows) // 2
    held_in, held_down = [add_low(a, b) for a, b in zip(mine, core)]
    blocks = [held_in[:cut], jnp.concatenate([held_in[cut:], held_down])]
    block_orders = orders_of(bits)
    steps = bits - 1
    turns = [("sum", at) for at in range(steps)] + [("copy", at) for at in reversed(range(steps))]

    def begin(turn, blocks):
        kind, at = turn
        send = sent if kind == "sum" else lambda b, n, bit, _: across(b, n, bit)
        return [send(b, reps, o[at], bit_of) for b, o in zip(blocks, block_orders)]

    def finish(turn, blocks, came):
        kind, at = turn
        if kind == "sum":
            return [kept_sum(b, c, o[at], bit_of) for b, c, o in zip(blocks, came, block_orders)]
        return [both_halves(b, c, bit_of[o[at]]) for b, c, o in zip(blocks, came, block_orders)]

    came = begin(turns[0], blocks)
    back_near, blocks, combs = tie(back_near, blocks, combs)
    comb_far = far_first(combs, shard_count)
    middle_back = backward_block(
        tokens, side, middle, second_low, (backs[0], *back_near), all_w, ct, st, doc_ids, kept
    )
    middle_back, came, comb_far, blocks, combs = tie(middle_back, came, comb_far, blocks, combs)
    *comb_near, _ = near_rest(combs, *comb_far, shard_count)
    blocks = finish(turns[0], blocks, came)
    middle_back, blocks = tie(middle_back, blocks)
    came = begin(turns[1], blocks)
    grad_out, rows_t, grad_middle, grad_pre = middle_back
    joint, grad_tokens = finish_block(
        tokens, all_w, grad_middle, grad_pre, grad_out, rows_t, kept[0]
    )
    joint, came, blocks = tie(joint, came, blocks)
    blocks = finish(turns[1], blocks, came)
    joint, blocks = tie(joint, blocks)
    came = begin(turns[2], blocks)
    joint_own = reduce_all(joint, reps, shard_count, 3)
    joint_own, blocks, comb_near, came = tie(joint_own, blocks, comb_near, came)
    mixed = middle + combs[0].astype(f32) + sum(part.astype(f32) for part in comb_near)
    mixed = mixed.astype(bf16)
    blocks = finish(turns[2], blocks, came)
    for turn in turns[3:]:
        blocks = finish(turn, blocks, begin(turn, blocks))
    others = [across(b, reps, 0) for b in blocks]
    grad_in_own = place_half(*blocks, 0, in_rows, None, bit_of[0])
    grad_down_own = place_half(*blocks, in_rows, down_rows, None, bit_of[0])
    grad_in_own = place_half(*others, 0, in_rows, grad_in_own, 1 - bit_of[0])
    grad_down_own = place_half(*others, in_rows, down_rows, grad_down_own, 1 - bit_of[0])
    widths = (query_cols, kv_cols, kv_cols, w_out.shape[1], PAD)
    query_own, key_own, value_own, out_own, small_own = local_call(
        split_kernel, [shape_of((own_rows, wide), f32) for wide in widths], [], joint_own
    )
    return (
        mixed,
        grad_tokens,
        small_own[:, EXPERTS],
        query_own,
        key_own,
        value_own,
        out_own,
        small_own[:, EXPERTS + 1],
        small_own[:, :EXPERTS],
        grad_in_own.reshape(own_experts, model_width, 2 * ff),
        grad_down_own.reshape(own_experts, ff, model_width),
    )


def solution(mesh):
    in_specs = (
        P(("rep", "shard"), None),
        P(("rep", "shard")),
        P(("rep", "shard"), None),
        P("shard"),
        P("shard", None),
        P("shard", None),
        P("shard", None),
        P("shard", None),
        P("shard"),
        P("shard", None),
        P("shard", None, None),
        P("shard", None, None),
        P(("rep", "shard"), None),
    )
    out_specs = (
        P(("rep", "shard"), None),
        P(("rep", "shard"), None),
        P("shard"),
        P("shard", None),
        P("shard", None),
        P("shard", None),
        P("shard", None),
        P("shard"),
        P("shard", None),
        P("shard", None, None),
        P("shard", None, None),
    )
    return jax.shard_map(shards, mesh=mesh, in_specs=in_specs, out_specs=out_specs, check_vma=False)
```

```python
import math

import jax
import jax.numpy as jnp
from jax import lax
from jax.experimental import pallas as pl
from jax.experimental.pallas import tpu as pltpu
from jax.sharding import PartitionSpec as P

HEADS = 16
KV_HEADS = 8
HEAD_DIM = 64
EXPERTS = 16
PAD = 128
VMEM_BYTES = 54 * 2**20


epsilon = 1e-06
rope_base = 10000.0
masked_score = -1e30


def positions(doc_rows):
    row_count = doc_rows.shape[0]
    places = jnp.arange(row_count, dtype=jnp.int32)
    begins = jnp.sum((doc_rows[None, :] < doc_rows[:, None]).astype(jnp.int32), axis=1)
    return places - begins


def rotary_tables(places, head_width):
    half_width = head_width // 2
    frequencies = jnp.power(
        rope_base, -2.0 * jnp.arange(half_width, dtype=jnp.float32) / head_width
    )
    angles = places.astype(jnp.float32)[:, None] * frequencies[None, :]
    return (jnp.cos(angles)[:, None, :], jnp.sin(angles)[:, None, :])


MESH = pl.DeviceIdType.MESH
HALVES = 2


def bit_orders(reps):
    bits = reps.bit_length() - 1
    first = list(range(bits))
    return (first, first[:1] + first[1:][::-1])


def rep_place(rep_at, order):
    place = 0
    for bit in order:
        place = place * 2 + rep_at // 2**bit % 2
    return place


def partner(rep_at, bit):
    return rep_at + 2**bit * (1 - 2 * (rep_at // 2**bit % 2))


def halves_of(columns):
    tiles = columns // 128
    left = (tiles + 1) // 2 * 128
    return (pl.ds(0, left), pl.ds(left, columns - left))


def meet(rep_at, shard_at, reps, shard_count):
    barrier = pltpu.get_barrier_semaphore()
    bits = reps.bit_length() - 1
    for bit in range(bits):
        pl.semaphore_signal(
            barrier, inc=1, device_id=(partner(rep_at, bit), shard_at), device_id_type=MESH
        )
    for step in range(1, shard_count):
        pl.semaphore_signal(
            barrier,
            inc=1,
            device_id=(rep_at, (shard_at + step) % shard_count),
            device_id_type=MESH,
        )
    pl.semaphore_wait(barrier, bits + shard_count - 1)


def spread(out, orders, columns, rep_at, shard_at, sends, recvs):
    bits = len(orders[0])
    flying = [None] * HALVES
    for at in reversed(range(bits)):
        window = 2 ** (bits - 1 - at)
        for half in range(HALVES):
            order = orders[half]
            place = rep_place(rep_at, order)
            begin = place // window * window
            if flying[half] is not None:
                flying[half].wait()
            block = out.at[:, pl.ds(begin, window), :, columns[half]]
            flying[half] = pltpu.make_async_remote_copy(
                src_ref=block,
                dst_ref=block,
                send_sem=sends.at[half, at],
                recv_sem=recvs.at[half, at],
                device_id=(partner(rep_at, order[at]), shard_at),
                device_id_type=MESH,
            )
            flying[half].start()
    for half in range(HALVES):
        flying[half].wait()


def spread_others(out, orders, columns, rep_at, shard_at, shard_count, sends, recvs):
    bits = len(orders[0])
    flying = [[] for _ in range(HALVES)]
    for at in reversed(range(bits)):
        window = 2 ** (bits - 1 - at)
        for half in range(HALVES):
            order = orders[half]
            place = rep_place(rep_at, order)
            begin = place // window * window
            for copy in flying[half]:
                copy.wait()
            flying[half] = []
            for step in range(1, shard_count):
                block = out.at[
                    (shard_at + step) % shard_count, pl.ds(begin, window), :, columns[half]
                ]
                copy = pltpu.make_async_remote_copy(
                    src_ref=block,
                    dst_ref=block,
                    send_sem=sends.at[half, at, step],
                    recv_sem=recvs.at[half, at, step],
                    device_id=(partner(rep_at, order[at]), shard_at),
                    device_id_type=MESH,
                )
                copy.start()
                flying[half].append(copy)
    for half in range(HALVES):
        for copy in flying[half]:
            copy.wait()


def gather_kernel(reps, shard_count, *refs):
    weights, (dy, routes, out, side, right, left) = refs[:5], refs[5:11]
    piece, z_send, z_recv, sends, recvs, d_send, d_recv = refs[11:]
    rep_at, shard_at = (lax.axis_index("rep"), lax.axis_index("shard"))
    orders = bit_orders(reps)
    columns = halves_of(piece.shape[-1])
    begin = 0
    for ref in weights:
        piece[:, :, begin : begin + ref.shape[-1]] = ref[...]
        begin += ref.shape[-1]
    meet(rep_at, shard_at, reps, shard_count)
    flying = []
    for half in range(HALVES):
        place = rep_place(rep_at, orders[half])
        for step in range(1, shard_count):
            copy = pltpu.make_async_remote_copy(
                src_ref=piece.at[place, :, columns[half]],
                dst_ref=out.at[shard_at, place, :, columns[half]],
                send_sem=z_send.at[half, step - 1],
                recv_sem=z_recv.at[half, step - 1],
                device_id=(rep_at, (shard_at + step) % shard_count),
                device_id_type=MESH,
            )
            copy.start()
            flying.append(copy)

    @pl.loop(0, reps)
    def _(index):
        out[shard_at, index] = piece[index]

    rows, width = dy.shape
    for at in range(0, rows, LANES):
        here = slice(at, at + LANES)
        side[here, :width] = dy[here, :]
        named = routes[here, :]
        lane = lane_of((LANES, PAD))
        mask = lane == named[:, 0:1]
        for k in range(1, named.shape[1]):
            mask = mask | (lane == named[:, k : k + 1])
        side[here, width:] = jnp.where(mask, 1.0, 0.0).astype(side.dtype)
    for copy in flying:
        copy.wait()
    flying = []
    if shard_count > 1:
        for number, (step, target) in enumerate(((1, right), (shard_count - 1, left))):
            copy = pltpu.make_async_remote_copy(
                src_ref=side,
                dst_ref=target,
                send_sem=d_send.at[number],
                recv_sem=d_recv.at[number],
                device_id=(rep_at, (shard_at + step) % shard_count),
                device_id_type=MESH,
            )
            copy.start()
            flying.append(copy)
    spread_others(out, orders, columns, rep_at, shard_at, shard_count, sends, recvs)
    for copy in flying:
        copy.wait()


def gather_all(weights, dy, routes, reps, shard_count, number):
    own = weights[0].shape[0]
    width = sum(w.shape[1] for w in weights)
    rows = own // reps
    bits = reps.bit_length() - 1
    kind = weights[0].dtype
    wide = jax.ShapeDtypeStruct((dy.shape[0], dy.shape[1] + PAD), kind)
    out, side, right, left = pl.pallas_call(
        lambda *refs: gather_kernel(reps, shard_count, *refs),
        out_shape=[jax.ShapeDtypeStruct((shard_count, reps, rows, width), kind), wide, wide, wide],
        in_specs=[pl.BlockSpec(memory_space=pltpu.VMEM)] * (len(weights) + 2),
        out_specs=[pl.BlockSpec(memory_space=pltpu.VMEM)] * 4,
        scratch_shapes=[
            pltpu.VMEM((reps, rows, width), kind),
            pltpu.SemaphoreType.DMA((HALVES, shard_count)),
            pltpu.SemaphoreType.DMA((HALVES, shard_count)),
            pltpu.SemaphoreType.DMA((HALVES, bits, shard_count)),
            pltpu.SemaphoreType.DMA((HALVES, bits, shard_count)),
            pltpu.SemaphoreType.DMA((2,)),
            pltpu.SemaphoreType.DMA((2,)),
        ],
        compiler_params=pltpu.CompilerParams(
            collective_id=number, has_side_effects=True, vmem_limit_bytes=VMEM_BYTES
        ),
        cost_estimate=pl.CostEstimate(
            flops=0, bytes_accessed=shard_count * own * width, transcendentals=0
        ),
    )(*[w.reshape(reps, rows, w.shape[1]) for w in weights], dy, routes)
    return out.reshape(shard_count * own, width), side, right, left


def spread_steps(pieces, outs, orders, rep_at, shard_at, sends, recvs):
    flying = []
    places = [rep_place(rep_at, order) for order in orders]
    for piece, out, place in zip(pieces, outs, places):
        out[place] = piece[...]
    for at in reversed(range(len(orders[0]))):
        window = 2 ** (len(orders[0]) - 1 - at)
        for copy in flying:
            copy.wait()
        flying = []
        for half, (out, place, order) in enumerate(zip(outs, places, orders)):
            block = out.at[pl.ds(place // window * window, window)]
            copy = pltpu.make_async_remote_copy(
                src_ref=block,
                dst_ref=block,
                send_sem=sends.at[half, at],
                recv_sem=recvs.at[half, at],
                device_id=(partner(rep_at, order[at]), shard_at),
                device_id_type=MESH,
            )
            copy.start()
            flying.append(copy)
        yield
    for copy in flying:
        copy.wait()


def reduce_kernel(reps, shard_count, parts, upper, lower, out, upper_out, lower_out, *scratch):
    bits = reps.bit_length() - 1
    f32 = jnp.float32
    landed = [scratch[half * bits : (half + 1) * bits] for half in range(HALVES)]
    rest = scratch[HALVES * bits :]
    if shard_count > 1:
        z_land, (z_send, z_recv) = (rest[:HALVES], rest[HALVES : HALVES + 2])
        rest = rest[HALVES + 2 :]
    r_send, r_recv, sends, recvs, s_send, s_recv = rest
    rep_at, shard_at = (lax.axis_index("rep"), lax.axis_index("shard"))
    orders = bit_orders(reps)
    columns = halves_of(parts.shape[-1])
    meet(rep_at, shard_at, reps, shard_count)
    flying = [None] * HALVES

    def source(half, at):
        return parts.at[:, :, :, columns[half]] if at == 0 else landed[half][at - 1]

    def begin(half, at):
        bit = orders[half][at]
        many = reps // 2 ** (at + 1)
        away = (1 - rep_at // 2**bit % 2) * many
        flying[half] = pltpu.make_async_remote_copy(
            src_ref=source(half, at).at[:, pl.ds(away, many)],
            dst_ref=landed[half][at],
            send_sem=r_send.at[half, at],
            recv_sem=r_recv.at[half, at],
            device_id=(partner(rep_at, bit), shard_at),
            device_id_type=MESH,
        )
        flying[half].start()

    for half in range(HALVES):
        begin(half, 0)
    steps = spread_steps(
        (upper, lower), (upper_out, lower_out), orders_of(bits), rep_at, shard_at, s_send, s_recv
    )
    next(steps, None)
    for at in range(bits):
        many = reps // 2 ** (at + 1)
        for half in range(HALVES):
            flying[half].wait()
            keep = rep_at // 2 ** orders[half][at] % 2 * many
            mine, came = (source(half, at), landed[half][at])

            @pl.loop(0, parts.shape[0] * many)
            def _(index):
                outer, inner = (index // many, index % many)
                came[outer, inner] = (
                    came[outer, inner].astype(f32) + mine[outer, keep + inner].astype(f32)
                ).astype(came.dtype)

            if at + 1 < bits:
                begin(half, at + 1)
        if at > 0 and at + 1 < bits:
            next(steps, None)
    copies = []
    if shard_count > 1:
        for half in range(HALVES):
            for step in range(1, shard_count):
                to = (shard_at + step) % shard_count
                copy = pltpu.make_async_remote_copy(
                    src_ref=landed[half][-1].at[to, 0],
                    dst_ref=z_land[half].at[step - 1],
                    send_sem=z_send.at[half, step - 1],
                    recv_sem=z_recv.at[half, step - 1],
                    device_id=(rep_at, to),
                    device_id_type=MESH,
                )
                copy.start()
                copies.append(copy)
    for copy in copies:
        copy.wait()
    for half in range(HALVES):
        place = rep_place(rep_at, orders[half])
        if shard_count > 1:
            total = landed[half][-1][shard_at, 0].astype(f32)
            for step in range(1, shard_count):
                total = total + z_land[half][step - 1].astype(f32)
            out[0, place, :, columns[half]] = total.astype(out.dtype)
        else:
            out[0, place, :, columns[half]] = landed[half][-1][0, 0]
    spread(out, orders, columns, rep_at, shard_at, sends, recvs)
    for _ in steps:
        pass


def reduce_all(parts, upper, lower, reps, shard_count, number):
    total, width = parts.shape
    rows = total // (reps * shard_count)
    bits = reps.bit_length() - 1
    widths = (halves_of(width)[0].size, halves_of(width)[1].size)
    scratch = []
    for wide in widths:
        for at in range(bits):
            scratch.append(
                pltpu.VMEM((shard_count, reps // 2 ** (at + 1), rows, wide), parts.dtype)
            )
    if shard_count > 1:
        scratch += [pltpu.VMEM((shard_count - 1, rows, wide), parts.dtype) for wide in widths]
        scratch += [pltpu.SemaphoreType.DMA((HALVES, shard_count)) for _ in range(2)]
    scratch += [pltpu.SemaphoreType.DMA((HALVES, bits)) for _ in range(6)]
    out, *wholes = pl.pallas_call(
        lambda *refs: reduce_kernel(reps, shard_count, *refs),
        out_shape=[jax.ShapeDtypeStruct((1, reps, rows, width), parts.dtype)]
        + [jax.ShapeDtypeStruct((reps // 2, *piece.shape), piece.dtype) for piece in (upper, lower)],
        in_specs=[pl.BlockSpec(memory_space=pltpu.VMEM)] * 3,
        out_specs=[pl.BlockSpec(memory_space=pltpu.VMEM)] * 3,
        scratch_shapes=scratch,
        compiler_params=pltpu.CompilerParams(
            collective_id=number, has_side_effects=True, vmem_limit_bytes=VMEM_BYTES
        ),
        cost_estimate=pl.CostEstimate(
            flops=0, bytes_accessed=total * width, transcendentals=0
        ),
    )(parts.reshape(shard_count, reps, rows, width), upper, lower)
    wholes = [whole.reshape(-1, whole.shape[-1]) for whole in wholes]
    return out.reshape(reps * rows, width), wholes


F32, BF16 = jnp.float32, jnp.bfloat16
LANES = 128
TILE = 256
LIGHT = pl.CostEstimate(flops=10**6, bytes_accessed=10**5, transcendentals=0)
GROUP = HEADS // KV_HEADS


def dot(a, b):
    return lax.dot_general(a, b, (((1,), (0,)), ((), ())), preferred_element_type=F32)


def dot_nt(a, b):
    return lax.dot_general(a, b, (((1,), (1,)), ((), ())), preferred_element_type=F32)


def lane_of(shape):
    return lax.broadcasted_iota(jnp.int32, shape, len(shape) - 1)


def swap_halves(values):
    near = lane_of(values.shape) % HEAD_DIM < HEAD_DIM // 2
    up = pltpu.roll(values, LANES - HEAD_DIM // 2, 1)
    down = pltpu.roll(values, HEAD_DIM // 2, 1)
    return jnp.where(near, up, down)


def rope_block(values, ct, st):
    return values * ct + swap_halves(values) * st


def unrope_block(values, ct, st):
    return values * ct - swap_halves(values) * st


def low_high(block, side):
    lane = lane_of(block.shape)
    wide = block.astype(F32)
    kept = jnp.where((lane < HEAD_DIM) if side == 0 else (lane >= HEAD_DIM), wide, 0.0)
    moved = pltpu.roll(kept, HEAD_DIM, 1)
    pair = (kept, moved) if side == 0 else (moved, kept)
    return [item.astype(BF16) for item in pair]


def fill_bias(bias, doc_col, doc_row):
    rows = bias.shape[0]
    keys = lax.broadcasted_iota(jnp.int32, (TILE, rows), 0)
    queries = lax.broadcasted_iota(jnp.int32, (TILE, rows), 1)
    for start in range(0, rows, TILE):
        allowed = (doc_col[start : start + TILE, :] == doc_row[...]) & (keys + start <= queries)
        bias[start : start + TILE, :] = jnp.where(allowed, 0.0, masked_score)


def tile_at(index, width=TILE):
    return pl.ds(pl.multiple_of(index * width, width), width)


def gate_softmax(second, small, mask):
    logits = dot(second, small)
    chosen = jnp.where(mask, logits, masked_score)
    gate_exp = jnp.where(mask, jnp.exp(chosen - jnp.max(chosen, axis=1, keepdims=True)), 0.0)
    return gate_exp / jnp.sum(gate_exp, axis=1, keepdims=True)


def forward_kernel(
    tokens, w, ct, st, doc_col, doc_row,
    second, middle, first_t, q8, keys, values, att_t, lse,
    first, att, bias,
):
    rows, width = tokens.shape
    q_cols, kv_cols = q8.shape[1], keys.shape[1]
    small_at = w.shape[1] - PAD
    gains = w[:, small_at:].astype(F32).T
    gain_in, gain_mid = gains[EXPERTS : EXPERTS + 1], gains[EXPERTS + 1 : EXPERTS + 2]
    for at in range(0, rows, LANES):
        x = tokens[at : at + LANES, :].astype(F32)
        scale = lax.rsqrt(jnp.mean(x * x, axis=-1, keepdims=True) + epsilon)
        low = (x * scale * gain_in).astype(BF16)
        first[at : at + LANES, :] = low
        first_t[:, at : at + LANES] = low.T

    def project(index):
        return dot(first[...], w[:, tile_at(index)])

    def roped(index):
        part = project(index)
        return jnp.concatenate(
            [
                rope_block(part[:, at : at + LANES], ct[...], st[...])
                for at in range(0, TILE, LANES)
            ],
            axis=1,
        )

    @pl.loop(0, q_cols // TILE)
    def _(j):
        q8[:, tile_at(j)] = (roped(j) * HEAD_DIM**-0.5).astype(BF16)

    @pl.loop(0, kv_cols // TILE)
    def _(j):
        keys[:, tile_at(j)] = roped(q_cols // TILE + j).astype(BF16)

    @pl.loop(0, kv_cols // TILE)
    def _(j):
        values[:, tile_at(j)] = project((q_cols + kv_cols) // TILE + j).astype(BF16)

    fill_bias(bias, doc_col, doc_row)

    @pl.loop(0, kv_cols // LANES)
    def _(pair):
        k128, v128 = keys[:, tile_at(pair, LANES)], values[:, tile_at(pair, LANES)]
        v_t = v128.astype(F32).T.astype(BF16)
        for side in range(2):
            low_k = low_high(k128, side)
            q = q8[:, tile_at(pair * 2 + side, LANES)]
            v_s = v_t[side * HEAD_DIM : (side + 1) * HEAD_DIM]
            for h in range(GROUP):
                head = pair * 2 * GROUP + side * GROUP + h
                for begin in range(0, rows, TILE):
                    kr = begin + TILE
                    s = dot_nt(low_k[h][:kr], q[begin:kr]) + bias[:kr, begin:kr]
                    top = jnp.max(s, axis=0, keepdims=True)
                    p = jnp.exp(s - top)
                    total = jnp.sum(p, axis=0, keepdims=True)
                    probs = (p * (1.0 / total)).astype(BF16)
                    lse[head, :, begin:kr] = top + jnp.log(total)
                    att_t[tile_at(head, HEAD_DIM), begin:kr] = dot(v_s[:, :kr], probs).astype(BF16)

    @pl.loop(0, width // TILE)
    def _(j):
        att[:, tile_at(j)] = att_t[tile_at(j), :].astype(F32).T.astype(BF16)

    @pl.loop(0, width // TILE)
    def _(j):
        out_w = w[:, pl.ds(pl.multiple_of(q_cols + 2 * kv_cols + j * TILE, TILE), TILE)]
        middle[:, tile_at(j)] = tokens[:, tile_at(j)].astype(F32) + dot(att[...], out_w)

    for at in range(0, rows, LANES):
        x = middle[at : at + LANES, :]
        scale = lax.rsqrt(jnp.mean(x * x, axis=-1, keepdims=True) + epsilon)
        second[at : at + LANES, :] = (x * scale * gain_mid).astype(BF16)


def split_kernel(joint, *outs):
    begin = 0
    for out in outs:
        out[...] = joint[:, begin : begin + out.shape[1]].astype(F32)
        begin += out.shape[1]


def shape_of(shape, kind):
    return jax.ShapeDtypeStruct(shape, kind)


def local_call(kernel, outs, scratch, *args):
    return pl.pallas_call(
        kernel,
        out_shape=outs,
        in_specs=[pl.BlockSpec(memory_space=pltpu.VMEM)] * len(args),
        out_specs=[pl.BlockSpec(memory_space=pltpu.VMEM)] * len(outs),
        scratch_shapes=scratch,
        compiler_params=pltpu.CompilerParams(vmem_limit_bytes=VMEM_BYTES),
        cost_estimate=LIGHT,
    )(*args)


def forward_block(tokens, w, ct, st, doc_ids, q_cols, kv_cols):
    rows, width = tokens.shape
    outs = [
        shape_of((rows, width), BF16),
        shape_of((rows, width), F32),
        shape_of((width, rows), BF16),
        shape_of((rows, q_cols), BF16),
        shape_of((rows, kv_cols), BF16),
        shape_of((rows, kv_cols), BF16),
        shape_of((q_cols, rows), BF16),
        shape_of((HEADS, 1, rows), F32),
    ]
    scratch = [
        pltpu.VMEM((rows, width), BF16),
        pltpu.VMEM((rows, q_cols), BF16),
        pltpu.VMEM((rows, rows), F32),
    ]
    return local_call(
        forward_kernel, outs, scratch, tokens, w, ct, st, doc_ids[:, None], doc_ids[None, :]
    )


def backward_kernel(
    tokens, side, middle, second, back_own, left_up, right_up, left_low, right_low, w, ct, st, doc_col, doc_row,
    q8, keys, values, att_t, lse,
    grad_out, rows_t, grad_middle, grad_pre,
    bias, grad_branch, grad_att, dq_t, dk, dv,
):
    rows, width = tokens.shape
    q_cols, kv_cols = q8.shape[1], keys.shape[1]
    qkv_cols = q_cols + 2 * kv_cols
    small_at = w.shape[1] - PAD
    small = w[:, small_at:]
    gains = small.astype(F32).T
    gain_mid = gains[EXPERTS + 1 : EXPERTS + 2]
    tall = back_own.shape[1]
    gain_sum = jnp.zeros((1, width), F32)
    router_t = jnp.zeros((PAD, width), F32)
    for at in range(0, rows, LANES):
        here = slice(at, at + LANES)
        cut = left_up.shape[0]
        back_left, back_right = (left_up, right_up) if at < cut else (left_low, right_low)
        there = slice(at - cut * (at >= cut), at - cut * (at >= cut) + LANES)
        mask = side[here, width:] > 0
        gates = gate_softmax(second[here, :], small, mask)
        came = (
            back_own[here, width:].astype(F32)
            + back_left[there, width:].astype(F32)
            + back_right[there, width:].astype(F32)
        )
        gate_back = jnp.where(
            lane_of(came.shape) < EXPERTS, came + pltpu.roll(came, tall - width - EXPERTS, 1), 0.0
        )
        grad_logits = gates * (gate_back - jnp.sum(gates * gate_back, axis=1, keepdims=True))
        low_logits = grad_logits.astype(BF16)
        router_t += dot(grad_logits.T.astype(BF16), second[here, :])
        grad_second = (
            back_own[here, :width].astype(F32)
            + back_left[there, :width].astype(F32)
            + back_right[there, :width].astype(F32)
            + dot_nt(low_logits, small)
        )
        x = middle[here, :]
        scale = lax.rsqrt(jnp.mean(x * x, axis=-1, keepdims=True) + epsilon)
        normed = x * scale
        gain_sum += jnp.sum(grad_second * normed, axis=0, keepdims=True)
        u = grad_second * gain_mid
        inner = jnp.mean(u * normed, axis=-1, keepdims=True)
        total = side[here, :width].astype(F32) + scale * (u - normed * inner)
        grad_middle[here, :] = total
        grad_branch[here, :] = total.astype(BF16)
    rows_t[...] = router_t
    rows_t[EXPERTS + 1 : EXPERTS + 2, :] = gain_sum

    @pl.loop(0, width // TILE)
    def _(j):
        grad_out[:, tile_at(j)] = dot(att_t[...], grad_branch[:, tile_at(j)]).astype(BF16)
        out_rows = w[tile_at(j), pl.ds(qkv_cols, width)]
        grad_att[:, tile_at(j)] = dot_nt(grad_branch[...], out_rows).astype(BF16)

    fill_bias(bias, doc_col, doc_row)

    @pl.loop(0, kv_cols // LANES)
    def _(pair):
        k128, v128 = keys[:, tile_at(pair, LANES)], values[:, tile_at(pair, LANES)]
        k_t = k128.astype(F32).T.astype(BF16)
        sums = []
        for side_at in range(2):
            low_k, low_v = low_high(k128, side_at), low_high(v128, side_at)
            q = q8[:, tile_at(pair * 2 + side_at, LANES)]
            grad_o = grad_att[:, tile_at(pair * 2 + side_at, LANES)]
            k_s = k_t[side_at * HEAD_DIM : (side_at + 1) * HEAD_DIM]
            for h in range(GROUP):
                head = pair * 2 * GROUP + side_at * GROUP + h
                for begin in reversed(range(0, rows, TILE)):
                    kr = begin + TILE
                    s = dot_nt(low_k[h][:kr], q[begin:kr]) + bias[:kr, begin:kr]
                    p = jnp.exp(s - lse[head, :, begin:kr])
                    dp = dot_nt(low_v[h][:kr], grad_o[begin:kr])
                    inner = jnp.sum(p * dp, axis=0, keepdims=True)
                    ds = (p * (dp - inner)).astype(BF16)
                    dq_t[h * HEAD_DIM : (h + 1) * HEAD_DIM, begin:kr] = dot(k_s[:, :kr], ds)
                    more_k, more_v = dot(ds, q[begin:kr]), dot(p.astype(BF16), grad_o[begin:kr])
                    if kr == rows:
                        dk[h, :, :], dv[h, :, :] = more_k, more_v
                    else:
                        dk[h, :kr, :] += more_k
                        dv[h, :kr, :] += more_v
            grad_q = unrope_block(dq_t[...].T * HEAD_DIM**-0.5, ct[...], st[...])
            grad_pre[:, tile_at(pair * 2 + side_at, LANES)] = grad_q.astype(BF16)
            left = lane_of((rows, LANES)) < HEAD_DIM
            mixed_k = jnp.where(left, dk[0], dk[1])
            mixed_v = jnp.where(left, dv[0], dv[1])
            sums.append(
                (mixed_k + pltpu.roll(mixed_k, HEAD_DIM, 1), mixed_v + pltpu.roll(mixed_v, HEAD_DIM, 1))
            )
        left = lane_of((rows, LANES)) < HEAD_DIM
        grad_k = unrope_block(jnp.where(left, sums[0][0], sums[1][0]), ct[...], st[...])
        grad_v = jnp.where(left, sums[0][1], sums[1][1])
        k_at = pl.multiple_of(q_cols + pair * LANES, LANES)
        v_at = pl.multiple_of(q_cols + kv_cols + pair * LANES, LANES)
        grad_pre[:, pl.ds(k_at, LANES)] = grad_k.astype(BF16)
        grad_pre[:, pl.ds(v_at, LANES)] = grad_v.astype(BF16)


def finish_kernel(
    tokens, w, grad_middle, grad_pre, grad_out, rows_in, first_t,
    joint, grad_tokens,
    grad_first, rows_t,
):
    rows, width = tokens.shape
    qkv_cols = grad_pre.shape[1]
    small_at = w.shape[1] - PAD
    gain_in = w[:, small_at:].astype(F32).T[EXPERTS : EXPERTS + 1]
    joint[:, qkv_cols:small_at] = grad_out[...]
    rows_t[...] = rows_in[...]

    @pl.loop(0, qkv_cols // TILE)
    def _(j):
        joint[:, tile_at(j)] = dot(first_t[...], grad_pre[:, tile_at(j)]).astype(BF16)

    @pl.loop(0, width // TILE)
    def _(j):
        grad_first[:, tile_at(j)] = dot_nt(grad_pre[...], w[tile_at(j), pl.ds(0, qkv_cols)])

    gain_sum = jnp.zeros((1, width), F32)
    for at in range(0, rows, LANES):
        here = slice(at, at + LANES)
        x = tokens[here, :].astype(F32)
        scale = lax.rsqrt(jnp.mean(x * x, axis=-1, keepdims=True) + epsilon)
        normed = x * scale
        columns = grad_first[here, :]
        gain_sum += jnp.sum(columns * normed, axis=0, keepdims=True)
        u = columns * gain_in
        inner = jnp.mean(u * normed, axis=-1, keepdims=True)
        grad_tokens[here, :] = grad_middle[here, :] + scale * (u - normed * inner)
    rows_t[EXPERTS : EXPERTS + 1, :] = gain_sum
    joint[:, pl.ds(small_at, PAD)] = rows_t[...].T.astype(BF16)


def backward_block(tokens, side, middle, second, backs, w, ct, st, doc_ids, kept):
    rows, width = tokens.shape
    q_cols, kv_cols = kept[1].shape[1], kept[2].shape[1]
    outs = [
        shape_of((width, width), BF16),
        shape_of((PAD, width), F32),
        shape_of((rows, width), F32),
        shape_of((rows, q_cols + 2 * kv_cols), BF16),
    ]
    scratch = [
        pltpu.VMEM((rows, rows), F32),
        pltpu.VMEM((rows, width), BF16),
        pltpu.VMEM((rows, q_cols), BF16),
        pltpu.VMEM((LANES, rows), F32),
        pltpu.VMEM((GROUP, rows, LANES), F32),
        pltpu.VMEM((GROUP, rows, LANES), F32),
    ]
    return local_call(
        backward_kernel, outs, scratch,
        tokens, side, middle, second, *backs, w, ct, st, doc_ids[:, None], doc_ids[None, :], *kept[1:],
    )


def finish_block(tokens, w, grad_middle, grad_pre, grad_out, rows_t, first_t):
    rows, width = tokens.shape
    outs = [shape_of((width, w.shape[1]), BF16), shape_of((rows, width), F32)]
    scratch = [pltpu.VMEM((rows, width), F32), pltpu.VMEM((PAD, width), F32)]
    return local_call(
        finish_kernel, outs, scratch, tokens, w, grad_middle, grad_pre, grad_out, rows_t, first_t
    )


def expert_kernel(
    aliased, first_expert, second, side, small, in_w, down_w, *refs
):
    gated_t, grad_both, second_t, dy, comb, back = refs[4 * aliased : 4 * aliased + 6]
    gates, grad_gates, comb_sum, back_sum, gated = refs[4 * aliased + 6 :]
    rows, width = second.shape
    ff = down_w.shape[1]
    at = pl.program_id(0)
    lane = lane_of((rows, PAD))

    @pl.when(at == 0)
    def _():
        gates[...] = gate_softmax(second[...], small[...], side[:, width:] > 0)
        grad_gates[...] = jnp.zeros_like(grad_gates)
        comb_sum[...] = jnp.zeros_like(comb_sum)
        back_sum[...] = jnp.zeros_like(back_sum)
        dy[...] = side[:, :width]
        second_t[...] = second[...].T

    mine = lane == first_expert[0] + at
    gate = jnp.sum(jnp.where(mine, gates[...], 0.0), axis=1, keepdims=True)
    grad_col = jnp.zeros((rows, 1), F32)
    for start in range(0, ff, TILE):
        tile = slice(start, start + TILE)
        up_tile = slice(ff + start, ff + start + TILE)
        gate_part = dot(second[...], in_w[0, :, tile])
        up_part = dot(second[...], in_w[0, :, up_tile])
        came = dot_nt(side[:, :width], down_w[0, tile, :])
        sigmoid_gate = 0.5 * jnp.tanh(0.5 * gate_part) + 0.5
        silu_gate = gate_part * sigmoid_gate
        hidden = (silu_gate * up_part).astype(BF16).astype(F32)
        grad_col += jnp.sum(hidden * came, axis=1, keepdims=True)
        gated[:, tile] = (hidden * gate).astype(BF16)
        gated_t[0, tile, :] = gated[:, tile].T
        grad_hidden = came * gate
        slope = sigmoid_gate + silu_gate * (1.0 - sigmoid_gate)
        grad_both[0, :, tile] = (grad_hidden * up_part * slope).astype(BF16)
        grad_both[0, :, up_tile] = (grad_hidden * silu_gate).astype(BF16)
    grad_gates[...] += jnp.where(mine, grad_col, 0.0)
    for start in range(0, width, TILE):
        tile = slice(start, start + TILE)
        comb_sum[:, tile] += dot(gated[...], down_w[0, :, tile])
        back_sum[:, tile] += dot_nt(grad_both[0], in_w[0, tile, :])

    @pl.when(at == pl.num_programs(0) - 1)
    def _():
        comb[...] = comb_sum[...].astype(BF16)
        back[:, :width] = back_sum[...].astype(BF16)
        high = grad_gates[...].astype(BF16).astype(F32)
        back[:, width:] = (high + pltpu.roll(grad_gates[...] - high, EXPERTS, 1)).astype(BF16)


def expert_block(first_expert, second, side, small, in_w, down_w, place, count, before):
    rows, width = second.shape
    experts, ff = down_w.shape[:2]
    whole = lambda *shape: pl.BlockSpec(shape, lambda e: (0,) * len(shape))
    in_specs = [
        pl.BlockSpec(memory_space=pltpu.SMEM),
        whole(rows, width),
        whole(*side.shape),
        whole(*small.shape),
        pl.BlockSpec((1, width, 2 * ff), lambda e: (e, 0, 0)),
        pl.BlockSpec((1, ff, width), lambda e: (e, 0, 0)),
    ] + [pl.BlockSpec(memory_space=pl.ANY)] * len(before)
    out_specs = [
        pl.BlockSpec((1, ff, rows), lambda e: (e, 0, place)),
        pl.BlockSpec((1, rows, 2 * ff), lambda e: (e, place, 0)),
        pl.BlockSpec((width, rows), lambda e: (0, place)),
        pl.BlockSpec((rows, width), lambda e: (place, 0)),
        whole(rows, width),
        whole(*side.shape),
    ]
    outs = [
        shape_of((experts, ff, count * rows), BF16),
        shape_of((experts, count * rows, 2 * ff), BF16),
        shape_of((width, count * rows), BF16),
        shape_of((count * rows, width), BF16),
        shape_of((rows, width), BF16),
        shape_of(side.shape, BF16),
    ]
    return pl.pallas_call(
        lambda *refs: expert_kernel(bool(before), *refs),
        grid=(experts,),
        out_shape=outs,
        in_specs=in_specs,
        out_specs=out_specs,
        scratch_shapes=[
            pltpu.VMEM((rows, PAD), F32),
            pltpu.VMEM((rows, PAD), F32),
            pltpu.VMEM((rows, width), F32),
            pltpu.VMEM((rows, width), F32),
            pltpu.VMEM((rows, ff), BF16),
        ],
        input_output_aliases={6: 0, 7: 1, 8: 2, 9: 3} if before else {},
        compiler_params=pltpu.CompilerParams(
            vmem_limit_bytes=VMEM_BYTES, dimension_semantics=("arbitrary",)
        ),
        cost_estimate=LIGHT,
    )(first_expert, second, side, small, in_w, down_w, *before)


def weight_kernel(base, second_t, dy, gated_t, grad_both, *outs):
    def fill(grad_in, grad_down):
        for start in range(0, grad_in.shape[1], 2 * TILE):
            tile = slice(start, start + 2 * TILE)
            grad_in[:, tile] = dot(second_t[...], grad_both[0, :, tile]).astype(BF16)
            grad_down[:, tile] = dot(gated_t[0], dy[:, tile]).astype(BF16)

    early = pl.program_id(0) < pl.num_programs(0) // 2
    pl.when(early)(lambda: fill(*outs[:2]))
    pl.when(jnp.logical_not(early))(lambda: fill(*outs[2:]))


def weight_block(base, second_t, dy, gated_t, grad_both):
    width, rows = second_t.shape
    experts, ff = gated_t.shape[:2]
    half = experts // 2
    first = lambda e, at: (jnp.minimum(e, half - 1), 0)
    last = lambda e, at: (jnp.maximum(e - half, 0), 0)
    grid_spec = pltpu.PrefetchScalarGridSpec(
        num_scalar_prefetch=1,
        grid=(experts,),
        in_specs=[
            pl.BlockSpec((width, rows), lambda e, at: (0, 0)),
            pl.BlockSpec((rows, width), lambda e, at: (0, 0)),
            pl.BlockSpec((1, ff, rows), lambda e, at: ((at[0] + e) % experts, 0, 0)),
            pl.BlockSpec((1, rows, 2 * ff), lambda e, at: ((at[0] + e) % experts, 0, 0)),
        ],
        out_specs=[
            pl.BlockSpec((width, 2 * ff), first),
            pl.BlockSpec((ff, width), first),
            pl.BlockSpec((width, 2 * ff), last),
            pl.BlockSpec((ff, width), last),
        ],
    )
    pair = [shape_of((half * width, 2 * ff), BF16), shape_of((half * ff, width), BF16)]
    return pl.pallas_call(
        weight_kernel,
        grid_spec=grid_spec,
        out_shape=pair * 2,
        compiler_params=pltpu.CompilerParams(
            vmem_limit_bytes=VMEM_BYTES, dimension_semantics=("arbitrary",)
        ),
        cost_estimate=LIGHT,
    )(base[None].astype(jnp.int32), second_t, dy, gated_t, grad_both)


def shift(block, count, step):
    return lax.ppermute(block, "shard", [(at, (at + step) % count) for at in range(count)])


def tie(*values):
    return lax.optimization_barrier(values)


def gather_near(piece, count):
    got = {0: piece}
    right = left = piece
    for step in range(1, (count - 1) // 2 + 1):
        right, left = shift(right, count, 1), shift(left, count, -1)
        got[step], got[count - step] = right, left
    return got, right, left


def gather_far(right, left, count):
    half = right.shape[0] // 2
    return shift(right[:half], count, 1), shift(left[half:], count, -1)


def far_first(parts, count):
    half = parts[0].shape[0] // 2
    far = parts[count // 2]
    return shift(far[:half], count, -1), shift(far[half:], count, 1)


def near_rest(parts, left, right, count, after=()):
    half = parts[0].shape[0] // 2
    if count == 2:
        return left, jnp.zeros_like(left), right, jnp.zeros_like(right), after
    for step in reversed(range(1, count // 2)):
        near, far = parts[step], parts[count - step]
        if step == count // 2 - 1:
            left = jnp.concatenate([add_low(near[:half], left), near[half:]], axis=0)
            right = jnp.concatenate([far[:half], add_low(far[half:], right)], axis=0)
        else:
            left, right = add_low(near, left), add_low(far, right)
        if step == 1:
            left, right, after = tie(left, right, after)
            rows = left.shape[0]
            split = rows // LANES * 3 // 4 * LANES
            ends = ((0, split), (split, rows))
            cuts = [part[start:stop] for start, stop in ends for part in (left, right)]
            shifted = [shift(part, count, (-1, 1)[at % 2]) for at, part in enumerate(cuts)]
            return *shifted, after
        left, right = shift(left, count, -1), shift(right, count, 1)


def add_low(a, b):
    return (a.astype(F32) + b.astype(F32)).astype(BF16)


def across(block, reps, bit):
    return lax.ppermute(block, "rep", [(at, at ^ 2**bit) for at in range(reps)])


def part_of(block, index):
    half = block.shape[0] // 2
    return lax.dynamic_slice_in_dim(block, index * half, half, axis=0)


def orders_of(bits):
    return list(range(1, bits)), list(range(1, bits))[::-1]


def sent(block, reps, bit, bit_of):
    return across(part_of(block, 1 - bit_of[bit]), reps, bit)


def kept_sum(block, came, bit, bit_of):
    return add_low(part_of(block, bit_of[bit]), came)


def place_kernel(begin, cut, half, upper, lower, *refs):
    at = begin + pl.program_id(0)

    @pl.when(at < cut)
    def _():
        refs[-1][...] = upper[...].astype(F32)

    @pl.when(at >= cut)
    def _():
        refs[-1][...] = lower[...].astype(F32)


def place_half(upper, lower, begin, rows, target, index):
    step = math.gcd(2 * TILE, upper.shape[0], begin, rows)
    cut, width = upper.shape[0] // step, upper.shape[1]
    first, blocks = begin // step, rows // step
    grid_spec = pltpu.PrefetchScalarGridSpec(
        num_scalar_prefetch=1,
        grid=(blocks,),
        in_specs=[
            pl.BlockSpec((step, width), lambda at, half: (jnp.minimum(first + at, cut - 1), 0)),
            pl.BlockSpec((step, width), lambda at, half: (jnp.maximum(first + at - cut, 0), 0)),
        ]
        + [pl.BlockSpec(memory_space=pl.ANY)] * (target is not None),
        out_specs=pl.BlockSpec((step, width), lambda at, half: (half[0] * blocks + at, 0)),
    )
    return pl.pallas_call(
        lambda *refs: place_kernel(first, cut, *refs),
        grid_spec=grid_spec,
        out_shape=shape_of((2 * rows, width), F32),
        input_output_aliases={} if target is None else {3: 0},
        compiler_params=pltpu.CompilerParams(
            vmem_limit_bytes=VMEM_BYTES, dimension_semantics=("arbitrary",)
        ),
        cost_estimate=LIGHT,
    )(index[None].astype(jnp.int32), upper, lower, *([] if target is None else [target]))


def shards(
    tokens,
    doc_ids,
    routes,
    norm_in_gain,
    w_query,
    w_key,
    w_value,
    w_out,
    norm_mid_gain,
    w_router,
    w_expert_in,
    w_expert_down,
    cotangent,
):
    bf16, f32 = BF16, F32
    row_count, model_width = tokens.shape
    query_cols = w_query.shape[1]
    kv_cols = w_key.shape[1]
    own_rows = w_query.shape[0]
    own_experts, ff = w_expert_down.shape[:2]
    shard_at = lax.axis_index("shard")
    reps, shard_count = (lax.axis_size("rep"), lax.axis_size("shard"))

    small = jnp.concatenate(
        [
            w_router,
            norm_in_gain[:, None],
            norm_mid_gain[:, None],
            jnp.zeros((own_rows, PAD - EXPERTS - 2), bf16),
        ],
        axis=1,
    )
    weights = [w_query, w_key, w_value, w_out, small]
    all_w, side, side_right, side_left = gather_all(
        weights, cotangent, routes, reps, shard_count, 1
    )
    small_at = query_cols + 2 * kv_cols + w_out.shape[1]

    cosine, sine_table = rotary_tables(positions(doc_ids), HEAD_DIM)
    cosine, sine_table = cosine[:, 0, :], sine_table[:, 0, :]
    ct = jnp.concatenate([cosine] * 4, axis=1)
    st = jnp.concatenate([-sine_table, sine_table] * 2, axis=1)
    side_parts = {0: side}
    for step in range(1, (shard_count - 1) // 2 + 1):
        if step > 1:
            side_right, side_left = shift(side_right, shard_count, 1), shift(side_left, shard_count, -1)
        side_parts[step], side_parts[shard_count - step] = side_right, side_left
    if shard_count > 2:
        side_far = gather_far(side_right, side_left, shard_count)
    else:
        side_far = (side_right,)
    second_low, middle, *kept = forward_block(
        tokens, all_w, ct, st, doc_ids, query_cols, kv_cols
    )
    second_low, side_far = tie(second_low, side_far)
    far_at = shard_count // 2
    side_parts[far_at] = jnp.concatenate(side_far)
    second_parts, *ends = gather_near(second_low, shard_count)
    first_expert = (shard_at * own_experts)[None].astype(jnp.int32)
    order = sorted(range(shard_count), key=lambda k: min(k, shard_count - k))
    order = order[:-2] + order[:-3:-1]
    small_full = all_w[:, small_at:]
    combs, backs, kept_parts = {}, {}, ()
    back_far = None
    for place, k in enumerate(order):
        *kept_parts, combs[k], backs[k] = expert_block(
            first_expert,
            second_parts[k],
            side_parts[k],
            small_full,
            w_expert_in,
            w_expert_down,
            place,
            shard_count,
            kept_parts,
        )
        if k == 0:
            kept_parts, second_parts, ends = tie(kept_parts, second_parts, ends)
            second_parts[far_at] = jnp.concatenate(gather_far(*ends, shard_count))
        if k == far_at:
            back_far = far_first(backs, shard_count)
        elif back_far is not None:
            kept_parts, back_far, backs = tie(kept_parts, back_far, backs)
    *back_near, kept_parts = near_rest(backs, *back_far, shard_count, kept_parts)
    gated_t, grad_both, second_t, dy_all = kept_parts

    rep_at = lax.axis_index("rep")
    bits = reps.bit_length() - 1
    bit_of = [rep_at // 2**bit % 2 for bit in range(bits)]
    half = own_experts // 2
    grads = (second_t, dy_all, gated_t, grad_both)
    *away, mine_in, mine_down = weight_block((1 - bit_of[0]) * half, *grads)
    mine = (mine_in, mine_down)
    away, back_early = tie(away, back_near[:2])
    core = [across(part, reps, 0) for part in away]
    in_rows, down_rows = [part.shape[0] for part in mine]
    cut = (in_rows + down_rows) // 2
    held_in, held_down = [add_low(a, b) for a, b in zip(mine, core)]
    held_in, held_down, back_late = tie(held_in, held_down, back_near[2:])
    blocks = [held_in[:cut], jnp.concatenate([held_in[cut:], held_down])]
    block_orders = orders_of(bits)
    steps = bits - 1

    def begin(at, blocks):
        return [sent(b, reps, o[at], bit_of) for b, o in zip(blocks, block_orders)]

    def finish(at, blocks, came):
        return [kept_sum(b, c, o[at], bit_of) for b, c, o in zip(blocks, came, block_orders)]

    came = begin(0, blocks)
    back_near, blocks, combs = tie([*back_early, *back_late], blocks, combs)
    comb_far = far_first(combs, shard_count)
    middle_back = backward_block(
        tokens, side, middle, second_low, (backs[0], *back_near), all_w, ct, st, doc_ids, kept
    )
    middle_back, came, comb_far, blocks, combs = tie(middle_back, came, comb_far, blocks, combs)
    *comb_near, _ = near_rest(combs, *comb_far, shard_count)
    blocks = finish(0, blocks, came)
    middle_back, blocks = tie(middle_back, blocks)
    came = begin(1, blocks)
    grad_out, rows_t, grad_middle, grad_pre = middle_back
    joint, grad_tokens = finish_block(
        tokens, all_w, grad_middle, grad_pre, grad_out, rows_t, kept[0]
    )
    joint, came, blocks = tie(joint, came, blocks)
    blocks = finish(1, blocks, came)
    for at in range(2, steps):
        blocks = finish(at, blocks, begin(at, blocks))
    joint_own, blocks = reduce_all(joint, *blocks, reps, shard_count, 3)
    joint_own, blocks, comb_near = tie(joint_own, blocks, comb_near)
    upper, lower = [
        comb_near[at].astype(f32) + comb_near[at + 1].astype(f32) for at in (0, 2)
    ]
    mixed = middle + combs[0].astype(f32) + jnp.concatenate([upper, lower])
    mixed = mixed.astype(bf16)
    others = [across(b, reps, 0) for b in blocks]
    grad_in_own = place_half(*blocks, 0, in_rows, None, bit_of[0])
    grad_down_own = place_half(*blocks, in_rows, down_rows, None, bit_of[0])
    grad_in_own = place_half(*others, 0, in_rows, grad_in_own, 1 - bit_of[0])
    grad_down_own = place_half(*others, in_rows, down_rows, grad_down_own, 1 - bit_of[0])
    widths = (query_cols, kv_cols, kv_cols, w_out.shape[1], PAD)
    query_own, key_own, value_own, out_own, small_own = local_call(
        split_kernel, [shape_of((own_rows, wide), f32) for wide in widths], [], joint_own
    )
    return (
        mixed,
        grad_tokens,
        small_own[:, EXPERTS],
        query_own,
        key_own,
        value_own,
        out_own,
        small_own[:, EXPERTS + 1],
        small_own[:, :EXPERTS],
        grad_in_own.reshape(own_experts, model_width, 2 * ff),
        grad_down_own.reshape(own_experts, ff, model_width),
    )


def solution(mesh):
    in_specs = (
        P(("rep", "shard"), None),
        P(("rep", "shard")),
        P(("rep", "shard"), None),
        P("shard"),
        P("shard", None),
        P("shard", None),
        P("shard", None),
        P("shard", None),
        P("shard"),
        P("shard", None),
        P("shard", None, None),
        P("shard", None, None),
        P(("rep", "shard"), None),
    )
    out_specs = (
        P(("rep", "shard"), None),
        P(("rep", "shard"), None),
        P("shard"),
        P("shard", None),
        P("shard", None),
        P("shard", None),
        P("shard", None),
        P("shard"),
        P("shard", None),
        P("shard", None, None),
        P("shard", None, None),
    )
    return jax.shard_map(shards, mesh=mesh, in_specs=in_specs, out_specs=out_specs, check_vma=False)
```

```python
import math

import jax
import jax.numpy as jnp
from jax import lax
from jax.experimental import pallas as pl
from jax.experimental.pallas import tpu as pltpu
from jax.sharding import PartitionSpec as P

HEADS = 16
KV_HEADS = 8
HEAD_DIM = 64
EXPERTS = 16
PAD = 128
VMEM_BYTES = 54 * 2**20


epsilon = 1e-06
rope_base = 10000.0
masked_score = -1e30


def positions(doc_rows):
    row_count = doc_rows.shape[0]
    places = jnp.arange(row_count, dtype=jnp.int32)
    begins = jnp.sum((doc_rows[None, :] < doc_rows[:, None]).astype(jnp.int32), axis=1)
    return places - begins


def rotary_tables(places, head_width):
    half_width = head_width // 2
    frequencies = jnp.power(
        rope_base, -2.0 * jnp.arange(half_width, dtype=jnp.float32) / head_width
    )
    angles = places.astype(jnp.float32)[:, None] * frequencies[None, :]
    return (jnp.cos(angles)[:, None, :], jnp.sin(angles)[:, None, :])


MESH = pl.DeviceIdType.MESH
HALVES = 2


def bit_orders(reps):
    bits = reps.bit_length() - 1
    first = list(range(bits))
    return (first, first[:1] + first[1:][::-1])


def rep_place(rep_at, order):
    place = 0
    for bit in order:
        place = place * 2 + rep_at // 2**bit % 2
    return place


def partner(rep_at, bit):
    return rep_at + 2**bit * (1 - 2 * (rep_at // 2**bit % 2))


def halves_of(columns):
    tiles = columns // 128
    left = (tiles + 1) // 2 * 128
    return (pl.ds(0, left), pl.ds(left, columns - left))


def meet(rep_at, shard_at, reps, shard_count):
    barrier = pltpu.get_barrier_semaphore()
    bits = reps.bit_length() - 1
    for bit in range(bits):
        pl.semaphore_signal(
            barrier, inc=1, device_id=(partner(rep_at, bit), shard_at), device_id_type=MESH
        )
    for step in range(1, shard_count):
        pl.semaphore_signal(
            barrier,
            inc=1,
            device_id=(rep_at, (shard_at + step) % shard_count),
            device_id_type=MESH,
        )
    pl.semaphore_wait(barrier, bits + shard_count - 1)


def spread(out, orders, columns, rep_at, shard_at, sends, recvs):
    bits = len(orders[0])
    flying = [None] * HALVES
    for at in reversed(range(bits)):
        window = 2 ** (bits - 1 - at)
        for half in range(HALVES):
            order = orders[half]
            place = rep_place(rep_at, order)
            begin = place // window * window
            if flying[half] is not None:
                flying[half].wait()
            block = out.at[:, pl.ds(begin, window), :, columns[half]]
            flying[half] = pltpu.make_async_remote_copy(
                src_ref=block,
                dst_ref=block,
                send_sem=sends.at[half, at],
                recv_sem=recvs.at[half, at],
                device_id=(partner(rep_at, order[at]), shard_at),
                device_id_type=MESH,
            )
            flying[half].start()
    for half in range(HALVES):
        flying[half].wait()


def spread_others(out, orders, columns, rep_at, shard_at, shard_count, sends, recvs):
    bits = len(orders[0])
    flying = [[] for _ in range(HALVES)]
    for at in reversed(range(bits)):
        window = 2 ** (bits - 1 - at)
        for half in range(HALVES):
            order = orders[half]
            place = rep_place(rep_at, order)
            begin = place // window * window
            for copy in flying[half]:
                copy.wait()
            flying[half] = []
            for step in range(1, shard_count):
                block = out.at[
                    (shard_at + step) % shard_count, pl.ds(begin, window), :, columns[half]
                ]
                copy = pltpu.make_async_remote_copy(
                    src_ref=block,
                    dst_ref=block,
                    send_sem=sends.at[half, at, step],
                    recv_sem=recvs.at[half, at, step],
                    device_id=(partner(rep_at, order[at]), shard_at),
                    device_id_type=MESH,
                )
                copy.start()
                flying[half].append(copy)
    for half in range(HALVES):
        for copy in flying[half]:
            copy.wait()


def gather_kernel(reps, shard_count, *refs):
    weights, (dy, routes, out, side, right, left) = refs[:5], refs[5:11]
    piece, z_send, z_recv, sends, recvs, d_send, d_recv = refs[11:]
    rep_at, shard_at = (lax.axis_index("rep"), lax.axis_index("shard"))
    orders = bit_orders(reps)
    columns = halves_of(piece.shape[-1])
    begin = 0
    for ref in weights:
        piece[:, :, begin : begin + ref.shape[-1]] = ref[...]
        begin += ref.shape[-1]
    meet(rep_at, shard_at, reps, shard_count)
    flying = []
    for half in range(HALVES):
        place = rep_place(rep_at, orders[half])
        for step in range(1, shard_count):
            copy = pltpu.make_async_remote_copy(
                src_ref=piece.at[place, :, columns[half]],
                dst_ref=out.at[shard_at, place, :, columns[half]],
                send_sem=z_send.at[half, step - 1],
                recv_sem=z_recv.at[half, step - 1],
                device_id=(rep_at, (shard_at + step) % shard_count),
                device_id_type=MESH,
            )
            copy.start()
            flying.append(copy)

    @pl.loop(0, reps)
    def _(index):
        out[shard_at, index] = piece[index]

    rows, width = dy.shape
    for at in range(0, rows, LANES):
        here = slice(at, at + LANES)
        side[here, :width] = dy[here, :]
        named = routes[here, :]
        lane = lane_of((LANES, PAD))
        mask = lane == named[:, 0:1]
        for k in range(1, named.shape[1]):
            mask = mask | (lane == named[:, k : k + 1])
        side[here, width:] = jnp.where(mask, 1.0, 0.0).astype(side.dtype)
    for copy in flying:
        copy.wait()
    top = shard_count - 1
    neighbours = []
    for number, (step, target) in enumerate(((1, right), (top, left))):
        copy = pltpu.make_async_remote_copy(
            src_ref=side,
            dst_ref=target,
            send_sem=d_send.at[number],
            recv_sem=d_recv.at[number],
            device_id=(rep_at, (shard_at + step) % shard_count),
            device_id_type=MESH,
        )
        neighbours.append(copy)
    sends_right, sends_left = shard_at < top, shard_at > 0

    @pl.when(sends_right)
    def _():
        neighbours[0].start()

    @pl.when(sends_left)
    def _():
        neighbours[1].start()

    @pl.when(shard_at == 0)
    def _():
        right[...] = jnp.zeros_like(right)

    @pl.when(shard_at == top)
    def _():
        left[...] = jnp.zeros_like(left)

    spread_others(out, orders, columns, rep_at, shard_at, shard_count, sends, recvs)

    @pl.when(sends_right)
    def _():
        neighbours[0].wait_send()
        neighbours[1].wait_recv()

    @pl.when(sends_left)
    def _():
        neighbours[1].wait_send()
        neighbours[0].wait_recv()


def gather_all(weights, dy, routes, reps, shard_count, number):
    own = weights[0].shape[0]
    width = sum(w.shape[1] for w in weights)
    rows = own // reps
    bits = reps.bit_length() - 1
    kind = weights[0].dtype
    wide = jax.ShapeDtypeStruct((dy.shape[0], dy.shape[1] + PAD), kind)
    out, side, right, left = pl.pallas_call(
        lambda *refs: gather_kernel(reps, shard_count, *refs),
        out_shape=[jax.ShapeDtypeStruct((shard_count, reps, rows, width), kind), wide, wide, wide],
        in_specs=[pl.BlockSpec(memory_space=pltpu.VMEM)] * (len(weights) + 2),
        out_specs=[pl.BlockSpec(memory_space=pltpu.VMEM)] * 4,
        scratch_shapes=[
            pltpu.VMEM((reps, rows, width), kind),
            pltpu.SemaphoreType.DMA((HALVES, shard_count)),
            pltpu.SemaphoreType.DMA((HALVES, shard_count)),
            pltpu.SemaphoreType.DMA((HALVES, bits, shard_count)),
            pltpu.SemaphoreType.DMA((HALVES, bits, shard_count)),
            pltpu.SemaphoreType.DMA((2,)),
            pltpu.SemaphoreType.DMA((2,)),
        ],
        compiler_params=pltpu.CompilerParams(
            collective_id=number, has_side_effects=True, vmem_limit_bytes=VMEM_BYTES
        ),
        cost_estimate=pl.CostEstimate(
            flops=0, bytes_accessed=shard_count * own * width, transcendentals=0
        ),
    )(*[w.reshape(reps, rows, w.shape[1]) for w in weights], dy, routes)
    return out.reshape(shard_count * own, width), side, right, left


def spread_steps(pieces, outs, orders, rep_at, shard_at, sends, recvs):
    flying = []
    places = [rep_place(rep_at, order) for order in orders]
    for piece, out, place in zip(pieces, outs, places):
        out[place] = piece[...]
    for at in reversed(range(len(orders[0]))):
        window = 2 ** (len(orders[0]) - 1 - at)
        for copy in flying:
            copy.wait()
        flying = []
        for half, (out, place, order) in enumerate(zip(outs, places, orders)):
            block = out.at[pl.ds(place // window * window, window)]
            copy = pltpu.make_async_remote_copy(
                src_ref=block,
                dst_ref=block,
                send_sem=sends.at[half, at],
                recv_sem=recvs.at[half, at],
                device_id=(partner(rep_at, order[at]), shard_at),
                device_id_type=MESH,
            )
            copy.start()
            flying.append(copy)
        yield
    for copy in flying:
        copy.wait()


def reduce_kernel(reps, shard_count, parts, upper, lower, out, upper_out, lower_out, *scratch):
    bits = reps.bit_length() - 1
    f32 = jnp.float32
    landed = [scratch[half * bits : (half + 1) * bits] for half in range(HALVES)]
    rest = scratch[HALVES * bits :]
    if shard_count > 1:
        z_land, (z_send, z_recv) = (rest[:HALVES], rest[HALVES : HALVES + 2])
        rest = rest[HALVES + 2 :]
    r_send, r_recv, sends, recvs, s_send, s_recv = rest
    rep_at, shard_at = (lax.axis_index("rep"), lax.axis_index("shard"))
    orders = bit_orders(reps)
    columns = halves_of(parts.shape[-1])
    meet(rep_at, shard_at, reps, shard_count)
    flying = [None] * HALVES

    def source(half, at):
        return parts.at[:, :, :, columns[half]] if at == 0 else landed[half][at - 1]

    def begin(half, at):
        bit = orders[half][at]
        many = reps // 2 ** (at + 1)
        away = (1 - rep_at // 2**bit % 2) * many
        flying[half] = pltpu.make_async_remote_copy(
            src_ref=source(half, at).at[:, pl.ds(away, many)],
            dst_ref=landed[half][at],
            send_sem=r_send.at[half, at],
            recv_sem=r_recv.at[half, at],
            device_id=(partner(rep_at, bit), shard_at),
            device_id_type=MESH,
        )
        flying[half].start()

    for half in range(HALVES):
        begin(half, 0)
    steps = spread_steps(
        (upper, lower), (upper_out, lower_out), last_orders(bits), rep_at, shard_at, s_send, s_recv
    )
    next(steps, None)
    for at in range(bits):
        many = reps // 2 ** (at + 1)
        for half in range(HALVES):
            flying[half].wait()
            keep = rep_at // 2 ** orders[half][at] % 2 * many
            mine, came = (source(half, at), landed[half][at])

            @pl.loop(0, parts.shape[0] * many)
            def _(index):
                outer, inner = (index // many, index % many)
                came[outer, inner] = (
                    came[outer, inner].astype(f32) + mine[outer, keep + inner].astype(f32)
                ).astype(came.dtype)

            if at + 1 < bits:
                begin(half, at + 1)
        if at > 0 and at + 1 < bits:
            next(steps, None)
    copies = []
    if shard_count > 1:
        for half in range(HALVES):
            for step in range(1, shard_count):
                to = (shard_at + step) % shard_count
                copy = pltpu.make_async_remote_copy(
                    src_ref=landed[half][-1].at[to, 0],
                    dst_ref=z_land[half].at[step - 1],
                    send_sem=z_send.at[half, step - 1],
                    recv_sem=z_recv.at[half, step - 1],
                    device_id=(rep_at, to),
                    device_id_type=MESH,
                )
                copy.start()
                copies.append(copy)
    for copy in copies:
        copy.wait()
    for half in range(HALVES):
        place = rep_place(rep_at, orders[half])
        if shard_count > 1:
            total = landed[half][-1][shard_at, 0].astype(f32)
            for step in range(1, shard_count):
                total = total + z_land[half][step - 1].astype(f32)
            out[0, place, :, columns[half]] = total.astype(out.dtype)
        else:
            out[0, place, :, columns[half]] = landed[half][-1][0, 0]
    spread(out, orders, columns, rep_at, shard_at, sends, recvs)
    for _ in steps:
        pass


def reduce_all(parts, upper, lower, reps, shard_count, number):
    total, width = parts.shape
    rows = total // (reps * shard_count)
    bits = reps.bit_length() - 1
    widths = (halves_of(width)[0].size, halves_of(width)[1].size)
    scratch = []
    for wide in widths:
        for at in range(bits):
            scratch.append(
                pltpu.VMEM((shard_count, reps // 2 ** (at + 1), rows, wide), parts.dtype)
            )
    if shard_count > 1:
        scratch += [pltpu.VMEM((shard_count - 1, rows, wide), parts.dtype) for wide in widths]
        scratch += [pltpu.SemaphoreType.DMA((HALVES, shard_count)) for _ in range(2)]
    scratch += [pltpu.SemaphoreType.DMA((HALVES, bits)) for _ in range(6)]
    out, *wholes = pl.pallas_call(
        lambda *refs: reduce_kernel(reps, shard_count, *refs),
        out_shape=[jax.ShapeDtypeStruct((1, reps, rows, width), parts.dtype)]
        + [jax.ShapeDtypeStruct((reps // 4, *piece.shape), piece.dtype) for piece in (upper, lower)],
        in_specs=[pl.BlockSpec(memory_space=pltpu.VMEM)] * 3,
        out_specs=[pl.BlockSpec(memory_space=pltpu.VMEM)] * 3,
        scratch_shapes=scratch,
        compiler_params=pltpu.CompilerParams(
            collective_id=number, has_side_effects=True, vmem_limit_bytes=VMEM_BYTES
        ),
        cost_estimate=pl.CostEstimate(
            flops=0, bytes_accessed=total * width, transcendentals=0
        ),
    )(parts.reshape(shard_count, reps, rows, width), upper, lower)
    wholes = [whole.reshape(-1, whole.shape[-1]) for whole in wholes]
    return out.reshape(reps * rows, width), wholes


F32, BF16 = jnp.float32, jnp.bfloat16
LANES = 128
TILE = 256
LIGHT = pl.CostEstimate(flops=10**6, bytes_accessed=10**5, transcendentals=0)
GROUP = HEADS // KV_HEADS


def dot(a, b):
    return lax.dot_general(a, b, (((1,), (0,)), ((), ())), preferred_element_type=F32)


def dot_nt(a, b):
    return lax.dot_general(a, b, (((1,), (1,)), ((), ())), preferred_element_type=F32)


def lane_of(shape):
    return lax.broadcasted_iota(jnp.int32, shape, len(shape) - 1)


def swap_halves(values):
    near = lane_of(values.shape) % HEAD_DIM < HEAD_DIM // 2
    up = pltpu.roll(values, LANES - HEAD_DIM // 2, 1)
    down = pltpu.roll(values, HEAD_DIM // 2, 1)
    return jnp.where(near, up, down)


def rope_block(values, ct, st):
    return values * ct + swap_halves(values) * st


def unrope_block(values, ct, st):
    return values * ct - swap_halves(values) * st


def low_high(block, side):
    lane = lane_of(block.shape)
    wide = block.astype(F32)
    kept = jnp.where((lane < HEAD_DIM) if side == 0 else (lane >= HEAD_DIM), wide, 0.0)
    moved = pltpu.roll(kept, HEAD_DIM, 1)
    pair = (kept, moved) if side == 0 else (moved, kept)
    return [item.astype(BF16) for item in pair]


def fill_bias(bias, doc_col, doc_row):
    rows = bias.shape[0]
    keys = lax.broadcasted_iota(jnp.int32, (TILE, rows), 0)
    queries = lax.broadcasted_iota(jnp.int32, (TILE, rows), 1)
    for start in range(0, rows, TILE):
        allowed = (doc_col[start : start + TILE, :] == doc_row[...]) & (keys + start <= queries)
        bias[start : start + TILE, :] = jnp.where(allowed, 0.0, masked_score)


def tile_at(index, width=TILE):
    return pl.ds(pl.multiple_of(index * width, width), width)


def gate_softmax(second, small, mask):
    logits = dot(second, small)
    chosen = jnp.where(mask, logits, masked_score)
    gate_exp = jnp.where(mask, jnp.exp(chosen - jnp.max(chosen, axis=1, keepdims=True)), 0.0)
    return gate_exp / jnp.sum(gate_exp, axis=1, keepdims=True)


def forward_kernel(
    tokens, w, ct, st, doc_col, doc_row,
    second, middle, first_t, q8, keys, values, att_t, lse,
    first, att, bias,
):
    rows, width = tokens.shape
    q_cols, kv_cols = q8.shape[1], keys.shape[1]
    small_at = w.shape[1] - PAD
    gains = w[:, small_at:].astype(F32).T
    gain_in, gain_mid = gains[EXPERTS : EXPERTS + 1], gains[EXPERTS + 1 : EXPERTS + 2]
    for at in range(0, rows, LANES):
        x = tokens[at : at + LANES, :].astype(F32)
        scale = lax.rsqrt(jnp.mean(x * x, axis=-1, keepdims=True) + epsilon)
        low = (x * scale * gain_in).astype(BF16)
        first[at : at + LANES, :] = low
        first_t[:, at : at + LANES] = low.T

    def project(index):
        return dot(first[...], w[:, tile_at(index)])

    def roped(index):
        part = project(index)
        return jnp.concatenate(
            [
                rope_block(part[:, at : at + LANES], ct[...], st[...])
                for at in range(0, TILE, LANES)
            ],
            axis=1,
        )

    @pl.loop(0, q_cols // TILE)
    def _(j):
        q8[:, tile_at(j)] = (roped(j) * HEAD_DIM**-0.5).astype(BF16)

    @pl.loop(0, kv_cols // TILE)
    def _(j):
        keys[:, tile_at(j)] = roped(q_cols // TILE + j).astype(BF16)

    @pl.loop(0, kv_cols // TILE)
    def _(j):
        values[:, tile_at(j)] = project((q_cols + kv_cols) // TILE + j).astype(BF16)

    fill_bias(bias, doc_col, doc_row)

    @pl.loop(0, kv_cols // LANES)
    def _(pair):
        k128, v128 = keys[:, tile_at(pair, LANES)], values[:, tile_at(pair, LANES)]
        v_t = v128.astype(F32).T.astype(BF16)
        for side in range(2):
            low_k = low_high(k128, side)
            q = q8[:, tile_at(pair * 2 + side, LANES)]
            v_s = v_t[side * HEAD_DIM : (side + 1) * HEAD_DIM]
            for h in range(GROUP):
                head = pair * 2 * GROUP + side * GROUP + h
                for begin in range(0, rows, TILE):
                    kr = begin + TILE
                    s = dot_nt(low_k[h][:kr], q[begin:kr]) + bias[:kr, begin:kr]
                    top = jnp.max(s, axis=0, keepdims=True)
                    p = jnp.exp(s - top)
                    total = jnp.sum(p, axis=0, keepdims=True)
                    probs = (p * (1.0 / total)).astype(BF16)
                    lse[head, :, begin:kr] = top + jnp.log(total)
                    att_t[tile_at(head, HEAD_DIM), begin:kr] = dot(v_s[:, :kr], probs).astype(BF16)

    @pl.loop(0, width // TILE)
    def _(j):
        att[:, tile_at(j)] = att_t[tile_at(j), :].astype(F32).T.astype(BF16)

    @pl.loop(0, width // TILE)
    def _(j):
        out_w = w[:, pl.ds(pl.multiple_of(q_cols + 2 * kv_cols + j * TILE, TILE), TILE)]
        middle[:, tile_at(j)] = tokens[:, tile_at(j)].astype(F32) + dot(att[...], out_w)

    for at in range(0, rows, LANES):
        x = middle[at : at + LANES, :]
        scale = lax.rsqrt(jnp.mean(x * x, axis=-1, keepdims=True) + epsilon)
        second[at : at + LANES, :] = (x * scale * gain_mid).astype(BF16)


def split_kernel(joint, *outs):
    begin = 0
    for out in outs:
        out[...] = joint[:, begin : begin + out.shape[1]].astype(F32)
        begin += out.shape[1]


def shape_of(shape, kind):
    return jax.ShapeDtypeStruct(shape, kind)


def local_call(kernel, outs, scratch, *args):
    return pl.pallas_call(
        kernel,
        out_shape=outs,
        in_specs=[pl.BlockSpec(memory_space=pltpu.VMEM)] * len(args),
        out_specs=[pl.BlockSpec(memory_space=pltpu.VMEM)] * len(outs),
        scratch_shapes=scratch,
        compiler_params=pltpu.CompilerParams(vmem_limit_bytes=VMEM_BYTES),
        cost_estimate=LIGHT,
    )(*args)


def forward_block(tokens, w, ct, st, doc_ids, q_cols, kv_cols):
    rows, width = tokens.shape
    outs = [
        shape_of((rows, width), BF16),
        shape_of((rows, width), F32),
        shape_of((width, rows), BF16),
        shape_of((rows, q_cols), BF16),
        shape_of((rows, kv_cols), BF16),
        shape_of((rows, kv_cols), BF16),
        shape_of((q_cols, rows), BF16),
        shape_of((HEADS, 1, rows), F32),
    ]
    scratch = [
        pltpu.VMEM((rows, width), BF16),
        pltpu.VMEM((rows, q_cols), BF16),
        pltpu.VMEM((rows, rows), F32),
    ]
    return local_call(
        forward_kernel, outs, scratch, tokens, w, ct, st, doc_ids[:, None], doc_ids[None, :]
    )


def backward_kernel(
    tokens, side, middle, second, back_own, back_left, back_right, w, ct, st, doc_col, doc_row,
    q8, keys, values, att_t, lse,
    grad_out, rows_t, grad_middle, grad_pre,
    bias, grad_branch, grad_att, dq_t, dk, dv,
):
    rows, width = tokens.shape
    q_cols, kv_cols = q8.shape[1], keys.shape[1]
    qkv_cols = q_cols + 2 * kv_cols
    small_at = w.shape[1] - PAD
    small = w[:, small_at:]
    gains = small.astype(F32).T
    gain_mid = gains[EXPERTS + 1 : EXPERTS + 2]
    tall = back_own.shape[1]
    gain_sum = jnp.zeros((1, width), F32)
    router_t = jnp.zeros((PAD, width), F32)
    for at in range(0, rows, LANES):
        here = slice(at, at + LANES)
        mask = side[here, width:] > 0
        gates = gate_softmax(second[here, :], small, mask)
        came = (
            back_own[here, width:].astype(F32)
            + back_left[here, width:].astype(F32)
            + back_right[here, width:].astype(F32)
        )
        gate_back = jnp.where(
            lane_of(came.shape) < EXPERTS, came + pltpu.roll(came, tall - width - EXPERTS, 1), 0.0
        )
        grad_logits = gates * (gate_back - jnp.sum(gates * gate_back, axis=1, keepdims=True))
        low_logits = grad_logits.astype(BF16)
        router_t += dot(grad_logits.T.astype(BF16), second[here, :])
        grad_second = (
            back_own[here, :width].astype(F32)
            + back_left[here, :width].astype(F32)
            + back_right[here, :width].astype(F32)
            + dot_nt(low_logits, small)
        )
        x = middle[here, :]
        scale = lax.rsqrt(jnp.mean(x * x, axis=-1, keepdims=True) + epsilon)
        normed = x * scale
        gain_sum += jnp.sum(grad_second * normed, axis=0, keepdims=True)
        u = grad_second * gain_mid
        inner = jnp.mean(u * normed, axis=-1, keepdims=True)
        total = side[here, :width].astype(F32) + scale * (u - normed * inner)
        grad_middle[here, :] = total
        grad_branch[here, :] = total.astype(BF16)
    rows_t[...] = router_t
    rows_t[EXPERTS + 1 : EXPERTS + 2, :] = gain_sum

    @pl.loop(0, width // TILE)
    def _(j):
        grad_out[:, tile_at(j)] = dot(att_t[...], grad_branch[:, tile_at(j)]).astype(BF16)
        out_rows = w[tile_at(j), pl.ds(qkv_cols, width)]
        grad_att[:, tile_at(j)] = dot_nt(grad_branch[...], out_rows).astype(BF16)

    fill_bias(bias, doc_col, doc_row)

    @pl.loop(0, kv_cols // LANES)
    def _(pair):
        k128, v128 = keys[:, tile_at(pair, LANES)], values[:, tile_at(pair, LANES)]
        k_t = k128.astype(F32).T.astype(BF16)
        sums = []
        for side_at in range(2):
            low_k, low_v = low_high(k128, side_at), low_high(v128, side_at)
            q = q8[:, tile_at(pair * 2 + side_at, LANES)]
            grad_o = grad_att[:, tile_at(pair * 2 + side_at, LANES)]
            k_s = k_t[side_at * HEAD_DIM : (side_at + 1) * HEAD_DIM]
            for h in range(GROUP):
                head = pair * 2 * GROUP + side_at * GROUP + h
                for begin in reversed(range(0, rows, TILE)):
                    kr = begin + TILE
                    s = dot_nt(low_k[h][:kr], q[begin:kr]) + bias[:kr, begin:kr]
                    p = jnp.exp(s - lse[head, :, begin:kr])
                    dp = dot_nt(low_v[h][:kr], grad_o[begin:kr])
                    inner = jnp.sum(p * dp, axis=0, keepdims=True)
                    ds = (p * (dp - inner)).astype(BF16)
                    dq_t[h * HEAD_DIM : (h + 1) * HEAD_DIM, begin:kr] = dot(k_s[:, :kr], ds)
                    more_k, more_v = dot(ds, q[begin:kr]), dot(p.astype(BF16), grad_o[begin:kr])
                    if kr == rows:
                        dk[h, :, :], dv[h, :, :] = more_k, more_v
                    else:
                        dk[h, :kr, :] += more_k
                        dv[h, :kr, :] += more_v
            grad_q = unrope_block(dq_t[...].T * HEAD_DIM**-0.5, ct[...], st[...])
            grad_pre[:, tile_at(pair * 2 + side_at, LANES)] = grad_q.astype(BF16)
            left = lane_of((rows, LANES)) < HEAD_DIM
            mixed_k = jnp.where(left, dk[0], dk[1])
            mixed_v = jnp.where(left, dv[0], dv[1])
            sums.append(
                (mixed_k + pltpu.roll(mixed_k, HEAD_DIM, 1), mixed_v + pltpu.roll(mixed_v, HEAD_DIM, 1))
            )
        left = lane_of((rows, LANES)) < HEAD_DIM
        grad_k = unrope_block(jnp.where(left, sums[0][0], sums[1][0]), ct[...], st[...])
        grad_v = jnp.where(left, sums[0][1], sums[1][1])
        k_at = pl.multiple_of(q_cols + pair * LANES, LANES)
        v_at = pl.multiple_of(q_cols + kv_cols + pair * LANES, LANES)
        grad_pre[:, pl.ds(k_at, LANES)] = grad_k.astype(BF16)
        grad_pre[:, pl.ds(v_at, LANES)] = grad_v.astype(BF16)


def finish_kernel(
    tokens, w, grad_middle, grad_pre, grad_out, rows_in, first_t,
    joint, grad_tokens,
    grad_first, rows_t,
):
    rows, width = tokens.shape
    qkv_cols = grad_pre.shape[1]
    small_at = w.shape[1] - PAD
    gain_in = w[:, small_at:].astype(F32).T[EXPERTS : EXPERTS + 1]
    joint[:, qkv_cols:small_at] = grad_out[...]
    rows_t[...] = rows_in[...]

    @pl.loop(0, qkv_cols // TILE)
    def _(j):
        joint[:, tile_at(j)] = dot(first_t[...], grad_pre[:, tile_at(j)]).astype(BF16)

    @pl.loop(0, width // TILE)
    def _(j):
        grad_first[:, tile_at(j)] = dot_nt(grad_pre[...], w[tile_at(j), pl.ds(0, qkv_cols)])

    gain_sum = jnp.zeros((1, width), F32)
    for at in range(0, rows, LANES):
        here = slice(at, at + LANES)
        x = tokens[here, :].astype(F32)
        scale = lax.rsqrt(jnp.mean(x * x, axis=-1, keepdims=True) + epsilon)
        normed = x * scale
        columns = grad_first[here, :]
        gain_sum += jnp.sum(columns * normed, axis=0, keepdims=True)
        u = columns * gain_in
        inner = jnp.mean(u * normed, axis=-1, keepdims=True)
        grad_tokens[here, :] = grad_middle[here, :] + scale * (u - normed * inner)
    rows_t[EXPERTS : EXPERTS + 1, :] = gain_sum
    joint[:, pl.ds(small_at, PAD)] = rows_t[...].T.astype(BF16)


def backward_block(tokens, side, middle, second, backs, w, ct, st, doc_ids, kept):
    rows, width = tokens.shape
    q_cols, kv_cols = kept[1].shape[1], kept[2].shape[1]
    outs = [
        shape_of((width, width), BF16),
        shape_of((PAD, width), F32),
        shape_of((rows, width), F32),
        shape_of((rows, q_cols + 2 * kv_cols), BF16),
    ]
    scratch = [
        pltpu.VMEM((rows, rows), F32),
        pltpu.VMEM((rows, width), BF16),
        pltpu.VMEM((rows, q_cols), BF16),
        pltpu.VMEM((LANES, rows), F32),
        pltpu.VMEM((GROUP, rows, LANES), F32),
        pltpu.VMEM((GROUP, rows, LANES), F32),
    ]
    return local_call(
        backward_kernel, outs, scratch,
        tokens, side, middle, second, *backs, w, ct, st, doc_ids[:, None], doc_ids[None, :], *kept[1:],
    )


def finish_block(tokens, w, grad_middle, grad_pre, grad_out, rows_t, first_t):
    rows, width = tokens.shape
    outs = [shape_of((width, w.shape[1]), BF16), shape_of((rows, width), F32)]
    scratch = [pltpu.VMEM((rows, width), F32), pltpu.VMEM((PAD, width), F32)]
    return local_call(
        finish_kernel, outs, scratch, tokens, w, grad_middle, grad_pre, grad_out, rows_t, first_t
    )


def expert_kernel(
    aliased, first_expert, second, side, small, in_w, down_w, *refs
):
    gated_t, grad_both, second_t, dy, comb, back = refs[4 * aliased : 4 * aliased + 6]
    gates, grad_gates, comb_sum, back_sum, gated = refs[4 * aliased + 6 :]
    rows, width = second.shape
    ff = down_w.shape[1]
    at = pl.program_id(0)
    lane = lane_of((rows, PAD))

    @pl.when(at == 0)
    def _():
        gates[...] = gate_softmax(second[...], small[...], side[:, width:] > 0)
        grad_gates[...] = jnp.zeros_like(grad_gates)
        comb_sum[...] = jnp.zeros_like(comb_sum)
        back_sum[...] = jnp.zeros_like(back_sum)
        dy[...] = side[:, :width]
        second_t[...] = second[...].T

    mine = lane == first_expert[0] + at
    gate = jnp.sum(jnp.where(mine, gates[...], 0.0), axis=1, keepdims=True)
    grad_col = jnp.zeros((rows, 1), F32)
    for start in range(0, ff, TILE):
        tile = slice(start, start + TILE)
        up_tile = slice(ff + start, ff + start + TILE)
        gate_part = dot(second[...], in_w[0, :, tile])
        up_part = dot(second[...], in_w[0, :, up_tile])
        came = dot_nt(side[:, :width], down_w[0, tile, :])
        sigmoid_gate = 0.5 * jnp.tanh(0.5 * gate_part) + 0.5
        silu_gate = gate_part * sigmoid_gate
        hidden = (silu_gate * up_part).astype(BF16).astype(F32)
        grad_col += jnp.sum(hidden * came, axis=1, keepdims=True)
        gated[:, tile] = (hidden * gate).astype(BF16)
        gated_t[0, tile, :] = gated[:, tile].T
        grad_hidden = came * gate
        slope = sigmoid_gate + silu_gate * (1.0 - sigmoid_gate)
        grad_both[0, :, tile] = (grad_hidden * up_part * slope).astype(BF16)
        grad_both[0, :, up_tile] = (grad_hidden * silu_gate).astype(BF16)
    grad_gates[...] += jnp.where(mine, grad_col, 0.0)
    for start in range(0, width, TILE):
        tile = slice(start, start + TILE)
        comb_sum[:, tile] += dot(gated[...], down_w[0, :, tile])
        back_sum[:, tile] += dot_nt(grad_both[0], in_w[0, tile, :])

    @pl.when(at == pl.num_programs(0) - 1)
    def _():
        comb[...] = comb_sum[...].astype(BF16)
        back[:, :width] = back_sum[...].astype(BF16)
        high = grad_gates[...].astype(BF16).astype(F32)
        back[:, width:] = (high + pltpu.roll(grad_gates[...] - high, EXPERTS, 1)).astype(BF16)


def expert_block(first_expert, second, side, small, in_w, down_w, place, count, before):
    rows, width = second.shape
    experts, ff = down_w.shape[:2]
    whole = lambda *shape: pl.BlockSpec(shape, lambda e: (0,) * len(shape))
    in_specs = [
        pl.BlockSpec(memory_space=pltpu.SMEM),
        whole(rows, width),
        whole(*side.shape),
        whole(*small.shape),
        pl.BlockSpec((1, width, 2 * ff), lambda e: (e, 0, 0)),
        pl.BlockSpec((1, ff, width), lambda e: (e, 0, 0)),
    ] + [pl.BlockSpec(memory_space=pl.ANY)] * len(before)
    out_specs = [
        pl.BlockSpec((1, ff, rows), lambda e: (e, 0, place)),
        pl.BlockSpec((1, rows, 2 * ff), lambda e: (e, place, 0)),
        pl.BlockSpec((width, rows), lambda e: (0, place)),
        pl.BlockSpec((rows, width), lambda e: (place, 0)),
        whole(rows, width),
        whole(*side.shape),
    ]
    outs = [
        shape_of((experts, ff, count * rows), BF16),
        shape_of((experts, count * rows, 2 * ff), BF16),
        shape_of((width, count * rows), BF16),
        shape_of((count * rows, width), BF16),
        shape_of((rows, width), BF16),
        shape_of(side.shape, BF16),
    ]
    return pl.pallas_call(
        lambda *refs: expert_kernel(bool(before), *refs),
        grid=(experts,),
        out_shape=outs,
        in_specs=in_specs,
        out_specs=out_specs,
        scratch_shapes=[
            pltpu.VMEM((rows, PAD), F32),
            pltpu.VMEM((rows, PAD), F32),
            pltpu.VMEM((rows, width), F32),
            pltpu.VMEM((rows, width), F32),
            pltpu.VMEM((rows, ff), BF16),
        ],
        input_output_aliases={6: 0, 7: 1, 8: 2, 9: 3} if before else {},
        compiler_params=pltpu.CompilerParams(
            vmem_limit_bytes=VMEM_BYTES, dimension_semantics=("arbitrary",)
        ),
        cost_estimate=LIGHT,
    )(first_expert, second, side, small, in_w, down_w, *before)


def weight_kernel(base, second_t, dy, gated_t, grad_both, *outs):
    def fill(grad_in, grad_down):
        for start in range(0, grad_in.shape[1], 2 * TILE):
            tile = slice(start, start + 2 * TILE)
            grad_in[:, tile] = dot(second_t[...], grad_both[0, :, tile]).astype(BF16)
            grad_down[:, tile] = dot(gated_t[0], dy[:, tile]).astype(BF16)

    early = pl.program_id(0) < pl.num_programs(0) // 2
    pl.when(early)(lambda: fill(*outs[:2]))
    pl.when(jnp.logical_not(early))(lambda: fill(*outs[2:]))


def weight_block(base, second_t, dy, gated_t, grad_both):
    width, rows = second_t.shape
    experts, ff = gated_t.shape[:2]
    half = experts // 2
    first = lambda e, at: (jnp.minimum(e, half - 1), 0)
    last = lambda e, at: (jnp.maximum(e - half, 0), 0)
    grid_spec = pltpu.PrefetchScalarGridSpec(
        num_scalar_prefetch=1,
        grid=(experts,),
        in_specs=[
            pl.BlockSpec((width, rows), lambda e, at: (0, 0)),
            pl.BlockSpec((rows, width), lambda e, at: (0, 0)),
            pl.BlockSpec((1, ff, rows), lambda e, at: ((at[0] + e) % experts, 0, 0)),
            pl.BlockSpec((1, rows, 2 * ff), lambda e, at: ((at[0] + e) % experts, 0, 0)),
        ],
        out_specs=[
            pl.BlockSpec((width, 2 * ff), first),
            pl.BlockSpec((ff, width), first),
            pl.BlockSpec((width, 2 * ff), last),
            pl.BlockSpec((ff, width), last),
        ],
    )
    pair = [shape_of((half * width, 2 * ff), BF16), shape_of((half * ff, width), BF16)]
    return pl.pallas_call(
        weight_kernel,
        grid_spec=grid_spec,
        out_shape=pair * 2,
        compiler_params=pltpu.CompilerParams(
            vmem_limit_bytes=VMEM_BYTES, dimension_semantics=("arbitrary",)
        ),
        cost_estimate=LIGHT,
    )(base[None].astype(jnp.int32), second_t, dy, gated_t, grad_both)


def shift(block, count, step):
    return lax.ppermute(block, "shard", [(at, (at + step) % count) for at in range(count)])


def tie(*values):
    return lax.optimization_barrier(values)


def gather_near(piece, count):
    got = {0: piece}
    right = left = piece
    for step in range(1, (count - 1) // 2 + 1):
        right, left = shift(right, count, 1), shift(left, count, -1)
        got[step], got[count - step] = right, left
    return got, right, left


def gather_far(right, left, count):
    half = right.shape[0] // 2
    return shift(right[:half], count, 1), shift(left[half:], count, -1)


def far_first(parts, count):
    half = parts[0].shape[0] // 2
    far = parts[count // 2]
    return shift(far[:half], count, -1), shift(far[half:], count, 1)


def near_rest(parts, left, right, count):
    half = parts[0].shape[0] // 2
    if count == 2:
        return jnp.concatenate([left, right], axis=0), jnp.zeros_like(parts[0])
    for step in reversed(range(1, count // 2)):
        near, far = parts[step], parts[count - step]
        if step == count // 2 - 1:
            left = jnp.concatenate([add_low(near[:half], left), near[half:]], axis=0)
            right = jnp.concatenate([far[:half], add_low(far[half:], right)], axis=0)
        else:
            left, right = add_low(near, left), add_low(far, right)
        left, right = shift(left, count, -1), shift(right, count, 1)
    return left, right


def add_low(a, b):
    return (a.astype(F32) + b.astype(F32)).astype(BF16)


def across(block, reps, bit):
    return lax.ppermute(block, "rep", [(at, at ^ 2**bit) for at in range(reps)])


def part_of(block, index):
    half = block.shape[0] // 2
    return lax.dynamic_slice_in_dim(block, index * half, half, axis=0)


def last_orders(bits):
    return [order[:-1] for order in orders_of(bits)]


def both_halves(mine, other, index):
    first = jnp.where(index == 0, mine, other)
    last = jnp.where(index == 0, other, mine)
    return jnp.concatenate([first, last])


def orders_of(bits):
    return list(range(1, bits)), list(range(1, bits))[::-1]


def sent(block, reps, bit, bit_of):
    return across(part_of(block, 1 - bit_of[bit]), reps, bit)


def kept_sum(block, came, bit, bit_of):
    return add_low(part_of(block, bit_of[bit]), came)


def place_kernel(begin, cut, half, upper, lower, *refs):
    at = begin + pl.program_id(0)

    @pl.when(at < cut)
    def _():
        refs[-1][...] = upper[...].astype(F32)

    @pl.when(at >= cut)
    def _():
        refs[-1][...] = lower[...].astype(F32)


def place_half(upper, lower, begin, rows, target, index):
    step = math.gcd(2 * TILE, upper.shape[0], begin, rows)
    cut, width = upper.shape[0] // step, upper.shape[1]
    first, blocks = begin // step, rows // step
    grid_spec = pltpu.PrefetchScalarGridSpec(
        num_scalar_prefetch=1,
        grid=(blocks,),
        in_specs=[
            pl.BlockSpec((step, width), lambda at, half: (jnp.minimum(first + at, cut - 1), 0)),
            pl.BlockSpec((step, width), lambda at, half: (jnp.maximum(first + at - cut, 0), 0)),
        ]
        + [pl.BlockSpec(memory_space=pl.ANY)] * (target is not None),
        out_specs=pl.BlockSpec((step, width), lambda at, half: (half[0] * blocks + at, 0)),
    )
    return pl.pallas_call(
        lambda *refs: place_kernel(first, cut, *refs),
        grid_spec=grid_spec,
        out_shape=shape_of((2 * rows, width), F32),
        input_output_aliases={} if target is None else {3: 0},
        compiler_params=pltpu.CompilerParams(
            vmem_limit_bytes=VMEM_BYTES, dimension_semantics=("arbitrary",)
        ),
        cost_estimate=LIGHT,
    )(index[None].astype(jnp.int32), upper, lower, *([] if target is None else [target]))


def shards(
    tokens,
    doc_ids,
    routes,
    norm_in_gain,
    w_query,
    w_key,
    w_value,
    w_out,
    norm_mid_gain,
    w_router,
    w_expert_in,
    w_expert_down,
    cotangent,
):
    bf16, f32 = BF16, F32
    row_count, model_width = tokens.shape
    query_cols = w_query.shape[1]
    kv_cols = w_key.shape[1]
    own_rows = w_query.shape[0]
    own_experts, ff = w_expert_down.shape[:2]
    shard_at = lax.axis_index("shard")
    reps, shard_count = (lax.axis_size("rep"), lax.axis_size("shard"))

    small = jnp.concatenate(
        [
            w_router,
            norm_in_gain[:, None],
            norm_mid_gain[:, None],
            jnp.zeros((own_rows, PAD - EXPERTS - 2), bf16),
        ],
        axis=1,
    )
    weights = [w_query, w_key, w_value, w_out, small]
    all_w, side, side_right, side_left = gather_all(
        weights, cotangent, routes, reps, shard_count, 1
    )
    small_at = query_cols + 2 * kv_cols + w_out.shape[1]

    cosine, sine_table = rotary_tables(positions(doc_ids), HEAD_DIM)
    cosine, sine_table = cosine[:, 0, :], sine_table[:, 0, :]
    ct = jnp.concatenate([cosine] * 4, axis=1)
    st = jnp.concatenate([-sine_table, sine_table] * 2, axis=1)
    top = shard_count - 1
    wraps = [lax.ppermute(side, "shard", [pair]) for pair in ((top, 0), (0, top))]
    second_low, middle, *kept = forward_block(
        tokens, all_w, ct, st, doc_ids, query_cols, kv_cols
    )
    second_low, wraps = tie(second_low, wraps)
    far_at = shard_count // 2
    side_parts = {0: side}
    second_parts, *ends = gather_near(second_low, shard_count)
    first_expert = (shard_at * own_experts)[None].astype(jnp.int32)
    order = sorted(range(shard_count), key=lambda k: min(k, shard_count - k))
    small_full = all_w[:, small_at:]
    combs, backs, kept_parts = {}, {}, ()
    for place, k in enumerate(order):
        *kept_parts, combs[k], backs[k] = expert_block(
            first_expert,
            second_parts[k],
            side_parts[k],
            small_full,
            w_expert_in,
            w_expert_down,
            place,
            shard_count,
            kept_parts,
        )
        if k == 0:
            kept_parts, wraps, side_right, side_left = tie(kept_parts, wraps, side_right, side_left)
            side_right = jnp.where(shard_at == 0, wraps[0], side_right)
            side_left = jnp.where(shard_at == top, wraps[1], side_left)
            for step in range(1, (shard_count - 1) // 2 + 1):
                if step > 1:
                    side_right = shift(side_right, shard_count, 1)
                    side_left = shift(side_left, shard_count, -1)
                side_parts[step], side_parts[shard_count - step] = side_right, side_left
            kept_parts, second_parts, ends, side_right, side_left = tie(
                kept_parts, second_parts, ends, side_right, side_left
            )
            second_parts[far_at] = jnp.concatenate(gather_far(*ends, shard_count))
            side_parts[far_at] = jnp.concatenate(gather_far(side_right, side_left, shard_count))
    back_far = far_first(backs, shard_count)
    gated_t, grad_both, second_t, dy_all = kept_parts

    rep_at = lax.axis_index("rep")
    bits = reps.bit_length() - 1
    bit_of = [rep_at // 2**bit % 2 for bit in range(bits)]
    half = own_experts // 2
    grads = (second_t, dy_all, gated_t, grad_both)
    *away, mine_in, mine_down = weight_block((1 - bit_of[0]) * half, *grads)
    mine = (mine_in, mine_down)
    away, back_far, backs = tie(away, back_far, backs)
    back_near = near_rest(backs, *back_far, shard_count)
    core = [across(part, reps, 0) for part in away]
    in_rows, down_rows = [part.shape[0] for part in mine]
    cut = (in_rows + down_rows) // 2
    held_in, held_down = [add_low(a, b) for a, b in zip(mine, core)]
    blocks = [held_in[:cut], jnp.concatenate([held_in[cut:], held_down])]
    block_orders = orders_of(bits)
    steps = bits - 1

    def begin(at, blocks):
        return [sent(b, reps, o[at], bit_of) for b, o in zip(blocks, block_orders)]

    def finish(at, blocks, came):
        return [kept_sum(b, c, o[at], bit_of) for b, c, o in zip(blocks, came, block_orders)]

    came = begin(0, blocks)
    back_near, came, blocks, combs = tie(back_near, came, blocks, combs)
    blocks = finish(0, blocks, came)
    back_near, blocks, combs = tie(back_near, blocks, combs)
    came = begin(1, blocks)
    comb_far = far_first(combs, shard_count)
    middle_back = backward_block(
        tokens, side, middle, second_low, (backs[0], *back_near), all_w, ct, st, doc_ids, kept
    )
    middle_back, came, comb_far, blocks, combs = tie(middle_back, came, comb_far, blocks, combs)
    comb_near = near_rest(combs, *comb_far, shard_count)
    blocks = finish(1, blocks, came)
    for at in range(2, steps):
        blocks = finish(at, blocks, begin(at, blocks))
    middle_back, blocks = tie(middle_back, blocks)
    last_bits = [order[-1] for order in block_orders]
    came = [across(b, reps, bit) for b, bit in zip(blocks, last_bits)]
    grad_out, rows_t, grad_middle, grad_pre = middle_back
    joint, grad_tokens = finish_block(
        tokens, all_w, grad_middle, grad_pre, grad_out, rows_t, kept[0]
    )
    joint, came, blocks = tie(joint, came, blocks)
    blocks = [both_halves(b, c, bit_of[bit]) for b, c, bit in zip(blocks, came, last_bits)]
    joint_own, blocks = reduce_all(joint, *blocks, reps, shard_count, 3)
    joint_own, blocks, comb_near = tie(joint_own, blocks, comb_near)
    mixed = middle + combs[0].astype(f32) + sum(part.astype(f32) for part in comb_near)
    mixed = mixed.astype(bf16)
    others = [across(b, reps, 0) for b in blocks]
    grad_in_own = place_half(*blocks, 0, in_rows, None, bit_of[0])
    grad_down_own = place_half(*blocks, in_rows, down_rows, None, bit_of[0])
    grad_in_own = place_half(*others, 0, in_rows, grad_in_own, 1 - bit_of[0])
    grad_down_own = place_half(*others, in_rows, down_rows, grad_down_own, 1 - bit_of[0])
    widths = (query_cols, kv_cols, kv_cols, w_out.shape[1], PAD)
    query_own, key_own, value_own, out_own, small_own = local_call(
        split_kernel, [shape_of((own_rows, wide), f32) for wide in widths], [], joint_own
    )
    return (
        mixed,
        grad_tokens,
        small_own[:, EXPERTS],
        query_own,
        key_own,
        value_own,
        out_own,
        small_own[:, EXPERTS + 1],
        small_own[:, :EXPERTS],
        grad_in_own.reshape(own_experts, model_width, 2 * ff),
        grad_down_own.reshape(own_experts, ff, model_width),
    )


def solution(mesh):
    in_specs = (
        P(("rep", "shard"), None),
        P(("rep", "shard")),
        P(("rep", "shard"), None),
        P("shard"),
        P("shard", None),
        P("shard", None),
        P("shard", None),
        P("shard", None),
        P("shard"),
        P("shard", None),
        P("shard", None, None),
        P("shard", None, None),
        P(("rep", "shard"), None),
    )
    out_specs = (
        P(("rep", "shard"), None),
        P(("rep", "shard"), None),
        P("shard"),
        P("shard", None),
        P("shard", None),
        P("shard", None),
        P("shard", None),
        P("shard"),
        P("shard", None),
        P("shard", None, None),
        P("shard", None, None),
    )
    return jax.shard_map(shards, mesh=mesh, in_specs=in_specs, out_specs=out_specs, check_vma=False)
```

```python
import math

import jax
import jax.numpy as jnp
from jax import lax
from jax.experimental import pallas as pl
from jax.experimental.pallas import tpu as pltpu
from jax.sharding import PartitionSpec as P

HEADS = 16
KV_HEADS = 8
HEAD_DIM = 64
EXPERTS = 16
PAD = 128
VMEM_BYTES = 54 * 2**20


epsilon = 1e-06
rope_base = 10000.0
masked_score = -1e30


def positions(doc_rows):
    row_count = doc_rows.shape[0]
    places = jnp.arange(row_count, dtype=jnp.int32)
    begins = jnp.sum((doc_rows[None, :] < doc_rows[:, None]).astype(jnp.int32), axis=1)
    return places - begins


def rotary_tables(places, head_width):
    half_width = head_width // 2
    frequencies = jnp.power(
        rope_base, -2.0 * jnp.arange(half_width, dtype=jnp.float32) / head_width
    )
    angles = places.astype(jnp.float32)[:, None] * frequencies[None, :]
    return (jnp.cos(angles)[:, None, :], jnp.sin(angles)[:, None, :])


MESH = pl.DeviceIdType.MESH
HALVES = 2


def bit_orders(reps):
    bits = reps.bit_length() - 1
    first = list(range(bits))
    return (first, first[:1] + first[1:][::-1])


def rep_place(rep_at, order):
    place = 0
    for bit in order:
        place = place * 2 + rep_at // 2**bit % 2
    return place


def partner(rep_at, bit):
    return rep_at + 2**bit * (1 - 2 * (rep_at // 2**bit % 2))


def halves_of(columns):
    tiles = columns // 128
    left = (tiles + 1) // 2 * 128
    return (pl.ds(0, left), pl.ds(left, columns - left))


def meet(rep_at, shard_at, reps, shard_count):
    barrier = pltpu.get_barrier_semaphore()
    bits = reps.bit_length() - 1
    for bit in range(bits):
        pl.semaphore_signal(
            barrier, inc=1, device_id=(partner(rep_at, bit), shard_at), device_id_type=MESH
        )
    for step in range(1, shard_count):
        pl.semaphore_signal(
            barrier,
            inc=1,
            device_id=(rep_at, (shard_at + step) % shard_count),
            device_id_type=MESH,
        )
    pl.semaphore_wait(barrier, bits + shard_count - 1)


def spread(out, orders, columns, rep_at, shard_at, sends, recvs):
    bits = len(orders[0])
    flying = [None] * HALVES
    for at in reversed(range(bits)):
        window = 2 ** (bits - 1 - at)
        for half in range(HALVES):
            order = orders[half]
            place = rep_place(rep_at, order)
            begin = place // window * window
            if flying[half] is not None:
                flying[half].wait()
            block = out.at[:, pl.ds(begin, window), :, columns[half]]
            flying[half] = pltpu.make_async_remote_copy(
                src_ref=block,
                dst_ref=block,
                send_sem=sends.at[half, at],
                recv_sem=recvs.at[half, at],
                device_id=(partner(rep_at, order[at]), shard_at),
                device_id_type=MESH,
            )
            flying[half].start()
    for half in range(HALVES):
        flying[half].wait()


def spread_others(out, orders, columns, rep_at, shard_at, shard_count, sends, recvs):
    bits = len(orders[0])
    flying = [[] for _ in range(HALVES)]
    for at in reversed(range(bits)):
        window = 2 ** (bits - 1 - at)
        for half in range(HALVES):
            order = orders[half]
            place = rep_place(rep_at, order)
            begin = place // window * window
            for copy in flying[half]:
                copy.wait()
            flying[half] = []
            for step in range(1, shard_count):
                block = out.at[
                    (shard_at + step) % shard_count, pl.ds(begin, window), :, columns[half]
                ]
                copy = pltpu.make_async_remote_copy(
                    src_ref=block,
                    dst_ref=block,
                    send_sem=sends.at[half, at, step],
                    recv_sem=recvs.at[half, at, step],
                    device_id=(partner(rep_at, order[at]), shard_at),
                    device_id_type=MESH,
                )
                copy.start()
                flying[half].append(copy)
    for half in range(HALVES):
        for copy in flying[half]:
            copy.wait()


def gather_kernel(reps, shard_count, *refs):
    weights, (dy, routes, out, side, right, left) = refs[:5], refs[5:11]
    piece, z_send, z_recv, sends, recvs, d_send, d_recv = refs[11:]
    rep_at, shard_at = (lax.axis_index("rep"), lax.axis_index("shard"))
    orders = bit_orders(reps)
    columns = halves_of(piece.shape[-1])
    begin = 0
    for ref in weights:
        piece[:, :, begin : begin + ref.shape[-1]] = ref[...]
        begin += ref.shape[-1]
    meet(rep_at, shard_at, reps, shard_count)
    flying = []
    for half in range(HALVES):
        place = rep_place(rep_at, orders[half])
        for step in range(1, shard_count):
            copy = pltpu.make_async_remote_copy(
                src_ref=piece.at[place, :, columns[half]],
                dst_ref=out.at[shard_at, place, :, columns[half]],
                send_sem=z_send.at[half, step - 1],
                recv_sem=z_recv.at[half, step - 1],
                device_id=(rep_at, (shard_at + step) % shard_count),
                device_id_type=MESH,
            )
            copy.start()
            flying.append(copy)

    @pl.loop(0, reps)
    def _(index):
        out[shard_at, index] = piece[index]

    rows, width = dy.shape
    for at in range(0, rows, LANES):
        here = slice(at, at + LANES)
        side[here, :width] = dy[here, :]
        named = routes[here, :]
        lane = lane_of((LANES, PAD))
        mask = lane == named[:, 0:1]
        for k in range(1, named.shape[1]):
            mask = mask | (lane == named[:, k : k + 1])
        side[here, width:] = jnp.where(mask, 1.0, 0.0).astype(side.dtype)
    for copy in flying:
        copy.wait()
    top = shard_count - 1
    neighbours = []
    for number, (step, target) in enumerate(((1, right), (top, left))):
        copy = pltpu.make_async_remote_copy(
            src_ref=side,
            dst_ref=target,
            send_sem=d_send.at[number],
            recv_sem=d_recv.at[number],
            device_id=(rep_at, (shard_at + step) % shard_count),
            device_id_type=MESH,
        )
        neighbours.append(copy)
    sends_right, sends_left = shard_at < top, shard_at > 0

    @pl.when(sends_right)
    def _():
        neighbours[0].start()

    @pl.when(sends_left)
    def _():
        neighbours[1].start()

    @pl.when(shard_at == 0)
    def _():
        right[...] = jnp.zeros_like(right)

    @pl.when(shard_at == top)
    def _():
        left[...] = jnp.zeros_like(left)

    spread_others(out, orders, columns, rep_at, shard_at, shard_count, sends, recvs)

    @pl.when(sends_right)
    def _():
        neighbours[0].wait_send()
        neighbours[1].wait_recv()

    @pl.when(sends_left)
    def _():
        neighbours[1].wait_send()
        neighbours[0].wait_recv()


def gather_all(weights, dy, routes, reps, shard_count, number):
    own = weights[0].shape[0]
    width = sum(w.shape[1] for w in weights)
    rows = own // reps
    bits = reps.bit_length() - 1
    kind = weights[0].dtype
    wide = jax.ShapeDtypeStruct((dy.shape[0], dy.shape[1] + PAD), kind)
    out, side, right, left = pl.pallas_call(
        lambda *refs: gather_kernel(reps, shard_count, *refs),
        out_shape=[jax.ShapeDtypeStruct((shard_count, reps, rows, width), kind), wide, wide, wide],
        in_specs=[pl.BlockSpec(memory_space=pltpu.VMEM)] * (len(weights) + 2),
        out_specs=[pl.BlockSpec(memory_space=pltpu.VMEM)] * 4,
        scratch_shapes=[
            pltpu.VMEM((reps, rows, width), kind),
            pltpu.SemaphoreType.DMA((HALVES, shard_count)),
            pltpu.SemaphoreType.DMA((HALVES, shard_count)),
            pltpu.SemaphoreType.DMA((HALVES, bits, shard_count)),
            pltpu.SemaphoreType.DMA((HALVES, bits, shard_count)),
            pltpu.SemaphoreType.DMA((2,)),
            pltpu.SemaphoreType.DMA((2,)),
        ],
        compiler_params=pltpu.CompilerParams(
            collective_id=number, has_side_effects=True, vmem_limit_bytes=VMEM_BYTES
        ),
        cost_estimate=pl.CostEstimate(
            flops=0, bytes_accessed=shard_count * own * width, transcendentals=0
        ),
    )(*[w.reshape(reps, rows, w.shape[1]) for w in weights], dy, routes)
    return out.reshape(shard_count * own, width), side, right, left


def spread_steps(pieces, outs, orders, rep_at, shard_at, sends, recvs):
    flying = []
    places = [rep_place(rep_at, order) for order in orders]
    for piece, out, place in zip(pieces, outs, places):
        out[place] = piece[...]
    for at in reversed(range(len(orders[0]))):
        window = 2 ** (len(orders[0]) - 1 - at)
        for copy in flying:
            copy.wait()
        flying = []
        for half, (out, place, order) in enumerate(zip(outs, places, orders)):
            block = out.at[pl.ds(place // window * window, window)]
            copy = pltpu.make_async_remote_copy(
                src_ref=block,
                dst_ref=block,
                send_sem=sends.at[half, at],
                recv_sem=recvs.at[half, at],
                device_id=(partner(rep_at, order[at]), shard_at),
                device_id_type=MESH,
            )
            copy.start()
            flying.append(copy)
        yield
    for copy in flying:
        copy.wait()


def reduce_kernel(reps, shard_count, parts, upper, lower, out, upper_out, lower_out, *scratch):
    bits = reps.bit_length() - 1
    f32 = jnp.float32
    landed = [scratch[half * bits : (half + 1) * bits] for half in range(HALVES)]
    rest = scratch[HALVES * bits :]
    if shard_count > 1:
        z_land, (z_send, z_recv) = (rest[:HALVES], rest[HALVES : HALVES + 2])
        rest = rest[HALVES + 2 :]
    r_send, r_recv, sends, recvs, s_send, s_recv = rest
    rep_at, shard_at = (lax.axis_index("rep"), lax.axis_index("shard"))
    orders = bit_orders(reps)
    columns = halves_of(parts.shape[-1])
    meet(rep_at, shard_at, reps, shard_count)
    flying = [None] * HALVES

    def source(half, at):
        return parts.at[:, :, :, columns[half]] if at == 0 else landed[half][at - 1]

    def begin(half, at):
        bit = orders[half][at]
        many = reps // 2 ** (at + 1)
        away = (1 - rep_at // 2**bit % 2) * many
        flying[half] = pltpu.make_async_remote_copy(
            src_ref=source(half, at).at[:, pl.ds(away, many)],
            dst_ref=landed[half][at],
            send_sem=r_send.at[half, at],
            recv_sem=r_recv.at[half, at],
            device_id=(partner(rep_at, bit), shard_at),
            device_id_type=MESH,
        )
        flying[half].start()

    for half in range(HALVES):
        begin(half, 0)
    steps = spread_steps(
        (upper, lower), (upper_out, lower_out), last_orders(bits), rep_at, shard_at, s_send, s_recv
    )
    for at in range(bits):
        many = reps // 2 ** (at + 1)
        for half in range(HALVES):
            flying[half].wait()
            keep = rep_at // 2 ** orders[half][at] % 2 * many
            mine, came = (source(half, at), landed[half][at])

            @pl.loop(0, parts.shape[0] * many)
            def _(index):
                outer, inner = (index // many, index % many)
                came[outer, inner] = (
                    came[outer, inner].astype(f32) + mine[outer, keep + inner].astype(f32)
                ).astype(came.dtype)

            if at + 1 < bits:
                begin(half, at + 1)
        if at > 0 and at + 1 < bits:
            next(steps, None)
    copies = []
    if shard_count > 1:
        for half in range(HALVES):
            for step in range(1, shard_count):
                to = (shard_at + step) % shard_count
                copy = pltpu.make_async_remote_copy(
                    src_ref=landed[half][-1].at[to, 0],
                    dst_ref=z_land[half].at[step - 1],
                    send_sem=z_send.at[half, step - 1],
                    recv_sem=z_recv.at[half, step - 1],
                    device_id=(rep_at, to),
                    device_id_type=MESH,
                )
                copy.start()
                copies.append(copy)
    for copy in copies:
        copy.wait()
    for half in range(HALVES):
        place = rep_place(rep_at, orders[half])
        if shard_count > 1:
            total = landed[half][-1][shard_at, 0].astype(f32)
            for step in range(1, shard_count):
                total = total + z_land[half][step - 1].astype(f32)
            out[0, place, :, columns[half]] = total.astype(out.dtype)
        else:
            out[0, place, :, columns[half]] = landed[half][-1][0, 0]
    spread(out, orders, columns, rep_at, shard_at, sends, recvs)
    for _ in steps:
        pass


def reduce_all(parts, upper, lower, reps, shard_count, number):
    total, width = parts.shape
    rows = total // (reps * shard_count)
    bits = reps.bit_length() - 1
    widths = (halves_of(width)[0].size, halves_of(width)[1].size)
    scratch = []
    for wide in widths:
        for at in range(bits):
            scratch.append(
                pltpu.VMEM((shard_count, reps // 2 ** (at + 1), rows, wide), parts.dtype)
            )
    if shard_count > 1:
        scratch += [pltpu.VMEM((shard_count - 1, rows, wide), parts.dtype) for wide in widths]
        scratch += [pltpu.SemaphoreType.DMA((HALVES, shard_count)) for _ in range(2)]
    scratch += [pltpu.SemaphoreType.DMA((HALVES, bits)) for _ in range(6)]
    out, *wholes = pl.pallas_call(
        lambda *refs: reduce_kernel(reps, shard_count, *refs),
        out_shape=[jax.ShapeDtypeStruct((1, reps, rows, width), parts.dtype)]
        + [jax.ShapeDtypeStruct((reps // 4, *piece.shape), piece.dtype) for piece in (upper, lower)],
        in_specs=[pl.BlockSpec(memory_space=pltpu.VMEM)] * 3,
        out_specs=[pl.BlockSpec(memory_space=pltpu.VMEM)] * 3,
        scratch_shapes=scratch,
        compiler_params=pltpu.CompilerParams(
            collective_id=number, has_side_effects=True, vmem_limit_bytes=VMEM_BYTES
        ),
        cost_estimate=pl.CostEstimate(
            flops=0, bytes_accessed=total * width, transcendentals=0
        ),
    )(parts.reshape(shard_count, reps, rows, width), upper, lower)
    wholes = [whole.reshape(-1, whole.shape[-1]) for whole in wholes]
    return out.reshape(reps * rows, width), wholes


F32, BF16 = jnp.float32, jnp.bfloat16
LANES = 128
TILE = 256
LIGHT = pl.CostEstimate(flops=10**6, bytes_accessed=10**5, transcendentals=0)
GROUP = HEADS // KV_HEADS


def dot(a, b):
    return lax.dot_general(a, b, (((1,), (0,)), ((), ())), preferred_element_type=F32)


def dot_nt(a, b):
    return lax.dot_general(a, b, (((1,), (1,)), ((), ())), preferred_element_type=F32)


def lane_of(shape):
    return lax.broadcasted_iota(jnp.int32, shape, len(shape) - 1)


def swap_halves(values):
    near = lane_of(values.shape) % HEAD_DIM < HEAD_DIM // 2
    up = pltpu.roll(values, LANES - HEAD_DIM // 2, 1)
    down = pltpu.roll(values, HEAD_DIM // 2, 1)
    return jnp.where(near, up, down)


def rope_block(values, ct, st):
    return values * ct + swap_halves(values) * st


def unrope_block(values, ct, st):
    return values * ct - swap_halves(values) * st


def low_high(block, side):
    lane = lane_of(block.shape)
    wide = block.astype(F32)
    kept = jnp.where((lane < HEAD_DIM) if side == 0 else (lane >= HEAD_DIM), wide, 0.0)
    moved = pltpu.roll(kept, HEAD_DIM, 1)
    pair = (kept, moved) if side == 0 else (moved, kept)
    return [item.astype(BF16) for item in pair]


def fill_bias(bias, doc_col, doc_row):
    rows = bias.shape[0]
    keys = lax.broadcasted_iota(jnp.int32, (TILE, rows), 0)
    queries = lax.broadcasted_iota(jnp.int32, (TILE, rows), 1)
    for start in range(0, rows, TILE):
        allowed = (doc_col[start : start + TILE, :] == doc_row[...]) & (keys + start <= queries)
        bias[start : start + TILE, :] = jnp.where(allowed, 0.0, masked_score)


def tile_at(index, width=TILE):
    return pl.ds(pl.multiple_of(index * width, width), width)


def gate_softmax(second, small, mask):
    logits = dot(second, small)
    chosen = jnp.where(mask, logits, masked_score)
    gate_exp = jnp.where(mask, jnp.exp(chosen - jnp.max(chosen, axis=1, keepdims=True)), 0.0)
    return gate_exp / jnp.sum(gate_exp, axis=1, keepdims=True)


def forward_kernel(
    tokens, w, ct, st, doc_col, doc_row,
    second, middle, first_t, q8, keys, values, att_t, lse,
    first, att, bias,
):
    rows, width = tokens.shape
    q_cols, kv_cols = q8.shape[1], keys.shape[1]
    small_at = w.shape[1] - PAD
    gains = w[:, small_at:].astype(F32).T
    gain_in, gain_mid = gains[EXPERTS : EXPERTS + 1], gains[EXPERTS + 1 : EXPERTS + 2]
    for at in range(0, rows, LANES):
        x = tokens[at : at + LANES, :].astype(F32)
        scale = lax.rsqrt(jnp.mean(x * x, axis=-1, keepdims=True) + epsilon)
        low = (x * scale * gain_in).astype(BF16)
        first[at : at + LANES, :] = low
        first_t[:, at : at + LANES] = low.T

    def project(index):
        return dot(first[...], w[:, tile_at(index)])

    def roped(index):
        part = project(index)
        return jnp.concatenate(
            [
                rope_block(part[:, at : at + LANES], ct[...], st[...])
                for at in range(0, TILE, LANES)
            ],
            axis=1,
        )

    @pl.loop(0, q_cols // TILE)
    def _(j):
        q8[:, tile_at(j)] = (roped(j) * HEAD_DIM**-0.5).astype(BF16)

    @pl.loop(0, kv_cols // TILE)
    def _(j):
        keys[:, tile_at(j)] = roped(q_cols // TILE + j).astype(BF16)

    @pl.loop(0, kv_cols // TILE)
    def _(j):
        values[:, tile_at(j)] = project((q_cols + kv_cols) // TILE + j).astype(BF16)

    fill_bias(bias, doc_col, doc_row)

    @pl.loop(0, kv_cols // LANES)
    def _(pair):
        k128, v128 = keys[:, tile_at(pair, LANES)], values[:, tile_at(pair, LANES)]
        v_t = v128.astype(F32).T.astype(BF16)
        for side in range(2):
            low_k = low_high(k128, side)
            q = q8[:, tile_at(pair * 2 + side, LANES)]
            v_s = v_t[side * HEAD_DIM : (side + 1) * HEAD_DIM]
            for h in range(GROUP):
                head = pair * 2 * GROUP + side * GROUP + h
                for begin in range(0, rows, TILE):
                    kr = begin + TILE
                    s = dot_nt(low_k[h][:kr], q[begin:kr]) + bias[:kr, begin:kr]
                    top = jnp.max(s, axis=0, keepdims=True)
                    p = jnp.exp(s - top)
                    total = jnp.sum(p, axis=0, keepdims=True)
                    probs = (p * (1.0 / total)).astype(BF16)
                    lse[head, :, begin:kr] = top + jnp.log(total)
                    att_t[tile_at(head, HEAD_DIM), begin:kr] = dot(v_s[:, :kr], probs).astype(BF16)

    @pl.loop(0, width // TILE)
    def _(j):
        att[:, tile_at(j)] = att_t[tile_at(j), :].astype(F32).T.astype(BF16)

    @pl.loop(0, width // TILE)
    def _(j):
        out_w = w[:, pl.ds(pl.multiple_of(q_cols + 2 * kv_cols + j * TILE, TILE), TILE)]
        middle[:, tile_at(j)] = tokens[:, tile_at(j)].astype(F32) + dot(att[...], out_w)

    for at in range(0, rows, LANES):
        x = middle[at : at + LANES, :]
        scale = lax.rsqrt(jnp.mean(x * x, axis=-1, keepdims=True) + epsilon)
        second[at : at + LANES, :] = (x * scale * gain_mid).astype(BF16)


def split_kernel(joint, *outs):
    begin = 0
    for out in outs:
        out[...] = joint[:, begin : begin + out.shape[1]].astype(F32)
        begin += out.shape[1]


def shape_of(shape, kind):
    return jax.ShapeDtypeStruct(shape, kind)


def local_call(kernel, outs, scratch, *args):
    return pl.pallas_call(
        kernel,
        out_shape=outs,
        in_specs=[pl.BlockSpec(memory_space=pltpu.VMEM)] * len(args),
        out_specs=[pl.BlockSpec(memory_space=pltpu.VMEM)] * len(outs),
        scratch_shapes=scratch,
        compiler_params=pltpu.CompilerParams(vmem_limit_bytes=VMEM_BYTES),
        cost_estimate=LIGHT,
    )(*args)


def forward_block(tokens, w, ct, st, doc_ids, q_cols, kv_cols):
    rows, width = tokens.shape
    outs = [
        shape_of((rows, width), BF16),
        shape_of((rows, width), F32),
        shape_of((width, rows), BF16),
        shape_of((rows, q_cols), BF16),
        shape_of((rows, kv_cols), BF16),
        shape_of((rows, kv_cols), BF16),
        shape_of((q_cols, rows), BF16),
        shape_of((HEADS, 1, rows), F32),
    ]
    scratch = [
        pltpu.VMEM((rows, width), BF16),
        pltpu.VMEM((rows, q_cols), BF16),
        pltpu.VMEM((rows, rows), F32),
    ]
    return local_call(
        forward_kernel, outs, scratch, tokens, w, ct, st, doc_ids[:, None], doc_ids[None, :]
    )


def backward_kernel(
    tokens, side, middle, second, back_own, back_left, back_right, w, ct, st, doc_col, doc_row,
    q8, keys, values, att_t, lse,
    grad_out, rows_t, grad_middle, grad_pre,
    bias, grad_branch, grad_att, dq_t, dk, dv,
):
    rows, width = tokens.shape
    q_cols, kv_cols = q8.shape[1], keys.shape[1]
    qkv_cols = q_cols + 2 * kv_cols
    small_at = w.shape[1] - PAD
    small = w[:, small_at:]
    gains = small.astype(F32).T
    gain_mid = gains[EXPERTS + 1 : EXPERTS + 2]
    tall = back_own.shape[1]
    gain_sum = jnp.zeros((1, width), F32)
    router_t = jnp.zeros((PAD, width), F32)
    for at in range(0, rows, LANES):
        here = slice(at, at + LANES)
        mask = side[here, width:] > 0
        gates = gate_softmax(second[here, :], small, mask)
        came = (
            back_own[here, width:].astype(F32)
            + back_left[here, width:].astype(F32)
            + back_right[here, width:].astype(F32)
        )
        gate_back = jnp.where(
            lane_of(came.shape) < EXPERTS, came + pltpu.roll(came, tall - width - EXPERTS, 1), 0.0
        )
        grad_logits = gates * (gate_back - jnp.sum(gates * gate_back, axis=1, keepdims=True))
        low_logits = grad_logits.astype(BF16)
        router_t += dot(grad_logits.T.astype(BF16), second[here, :])
        grad_second = (
            back_own[here, :width].astype(F32)
            + back_left[here, :width].astype(F32)
            + back_right[here, :width].astype(F32)
            + dot_nt(low_logits, small)
        )
        x = middle[here, :]
        scale = lax.rsqrt(jnp.mean(x * x, axis=-1, keepdims=True) + epsilon)
        normed = x * scale
        gain_sum += jnp.sum(grad_second * normed, axis=0, keepdims=True)
        u = grad_second * gain_mid
        inner = jnp.mean(u * normed, axis=-1, keepdims=True)
        total = side[here, :width].astype(F32) + scale * (u - normed * inner)
        grad_middle[here, :] = total
        grad_branch[here, :] = total.astype(BF16)
    rows_t[...] = router_t
    rows_t[EXPERTS + 1 : EXPERTS + 2, :] = gain_sum

    @pl.loop(0, width // TILE)
    def _(j):
        grad_out[:, tile_at(j)] = dot(att_t[...], grad_branch[:, tile_at(j)]).astype(BF16)
        out_rows = w[tile_at(j), pl.ds(qkv_cols, width)]
        grad_att[:, tile_at(j)] = dot_nt(grad_branch[...], out_rows).astype(BF16)

    fill_bias(bias, doc_col, doc_row)

    @pl.loop(0, kv_cols // LANES)
    def _(pair):
        k128, v128 = keys[:, tile_at(pair, LANES)], values[:, tile_at(pair, LANES)]
        k_t = k128.astype(F32).T.astype(BF16)
        sums = []
        for side_at in range(2):
            low_k, low_v = low_high(k128, side_at), low_high(v128, side_at)
            q = q8[:, tile_at(pair * 2 + side_at, LANES)]
            grad_o = grad_att[:, tile_at(pair * 2 + side_at, LANES)]
            k_s = k_t[side_at * HEAD_DIM : (side_at + 1) * HEAD_DIM]
            for h in range(GROUP):
                head = pair * 2 * GROUP + side_at * GROUP + h
                for begin in reversed(range(0, rows, TILE)):
                    kr = begin + TILE
                    s = dot_nt(low_k[h][:kr], q[begin:kr]) + bias[:kr, begin:kr]
                    p = jnp.exp(s - lse[head, :, begin:kr])
                    dp = dot_nt(low_v[h][:kr], grad_o[begin:kr])
                    inner = jnp.sum(p * dp, axis=0, keepdims=True)
                    ds = (p * (dp - inner)).astype(BF16)
                    dq_t[h * HEAD_DIM : (h + 1) * HEAD_DIM, begin:kr] = dot(k_s[:, :kr], ds)
                    more_k, more_v = dot(ds, q[begin:kr]), dot(p.astype(BF16), grad_o[begin:kr])
                    if kr == rows:
                        dk[h, :, :], dv[h, :, :] = more_k, more_v
                    else:
                        dk[h, :kr, :] += more_k
                        dv[h, :kr, :] += more_v
            grad_q = unrope_block(dq_t[...].T * HEAD_DIM**-0.5, ct[...], st[...])
            grad_pre[:, tile_at(pair * 2 + side_at, LANES)] = grad_q.astype(BF16)
            left = lane_of((rows, LANES)) < HEAD_DIM
            mixed_k = jnp.where(left, dk[0], dk[1])
            mixed_v = jnp.where(left, dv[0], dv[1])
            sums.append(
                (mixed_k + pltpu.roll(mixed_k, HEAD_DIM, 1), mixed_v + pltpu.roll(mixed_v, HEAD_DIM, 1))
            )
        left = lane_of((rows, LANES)) < HEAD_DIM
        grad_k = unrope_block(jnp.where(left, sums[0][0], sums[1][0]), ct[...], st[...])
        grad_v = jnp.where(left, sums[0][1], sums[1][1])
        k_at = pl.multiple_of(q_cols + pair * LANES, LANES)
        v_at = pl.multiple_of(q_cols + kv_cols + pair * LANES, LANES)
        grad_pre[:, pl.ds(k_at, LANES)] = grad_k.astype(BF16)
        grad_pre[:, pl.ds(v_at, LANES)] = grad_v.astype(BF16)


def finish_kernel(
    tokens, w, grad_middle, grad_pre, grad_out, rows_in, first_t,
    joint, grad_tokens,
    grad_first, rows_t,
):
    rows, width = tokens.shape
    qkv_cols = grad_pre.shape[1]
    small_at = w.shape[1] - PAD
    gain_in = w[:, small_at:].astype(F32).T[EXPERTS : EXPERTS + 1]
    joint[:, qkv_cols:small_at] = grad_out[...]
    rows_t[...] = rows_in[...]

    @pl.loop(0, qkv_cols // TILE)
    def _(j):
        joint[:, tile_at(j)] = dot(first_t[...], grad_pre[:, tile_at(j)]).astype(BF16)

    @pl.loop(0, width // TILE)
    def _(j):
        grad_first[:, tile_at(j)] = dot_nt(grad_pre[...], w[tile_at(j), pl.ds(0, qkv_cols)])

    gain_sum = jnp.zeros((1, width), F32)
    for at in range(0, rows, LANES):
        here = slice(at, at + LANES)
        x = tokens[here, :].astype(F32)
        scale = lax.rsqrt(jnp.mean(x * x, axis=-1, keepdims=True) + epsilon)
        normed = x * scale
        columns = grad_first[here, :]
        gain_sum += jnp.sum(columns * normed, axis=0, keepdims=True)
        u = columns * gain_in
        inner = jnp.mean(u * normed, axis=-1, keepdims=True)
        grad_tokens[here, :] = grad_middle[here, :] + scale * (u - normed * inner)
    rows_t[EXPERTS : EXPERTS + 1, :] = gain_sum
    joint[:, pl.ds(small_at, PAD)] = rows_t[...].T.astype(BF16)


def backward_block(tokens, side, middle, second, backs, w, ct, st, doc_ids, kept):
    rows, width = tokens.shape
    q_cols, kv_cols = kept[1].shape[1], kept[2].shape[1]
    outs = [
        shape_of((width, width), BF16),
        shape_of((PAD, width), F32),
        shape_of((rows, width), F32),
        shape_of((rows, q_cols + 2 * kv_cols), BF16),
    ]
    scratch = [
        pltpu.VMEM((rows, rows), F32),
        pltpu.VMEM((rows, width), BF16),
        pltpu.VMEM((rows, q_cols), BF16),
        pltpu.VMEM((LANES, rows), F32),
        pltpu.VMEM((GROUP, rows, LANES), F32),
        pltpu.VMEM((GROUP, rows, LANES), F32),
    ]
    return local_call(
        backward_kernel, outs, scratch,
        tokens, side, middle, second, *backs, w, ct, st, doc_ids[:, None], doc_ids[None, :], *kept[1:],
    )


def finish_block(tokens, w, grad_middle, grad_pre, grad_out, rows_t, first_t):
    rows, width = tokens.shape
    outs = [shape_of((width, w.shape[1]), BF16), shape_of((rows, width), F32)]
    scratch = [pltpu.VMEM((rows, width), F32), pltpu.VMEM((PAD, width), F32)]
    return local_call(
        finish_kernel, outs, scratch, tokens, w, grad_middle, grad_pre, grad_out, rows_t, first_t
    )


def expert_kernel(
    aliased, first_expert, second, side, small, in_w, down_w, *refs
):
    gated_t, grad_both, second_t, dy, comb, back = refs[4 * aliased : 4 * aliased + 6]
    gates, grad_gates, comb_sum, back_sum, gated = refs[4 * aliased + 6 :]
    rows, width = second.shape
    ff = down_w.shape[1]
    at = pl.program_id(0)
    lane = lane_of((rows, PAD))

    @pl.when(at == 0)
    def _():
        gates[...] = gate_softmax(second[...], small[...], side[:, width:] > 0)
        grad_gates[...] = jnp.zeros_like(grad_gates)
        comb_sum[...] = jnp.zeros_like(comb_sum)
        back_sum[...] = jnp.zeros_like(back_sum)
        dy[...] = side[:, :width]
        second_t[...] = second[...].T

    mine = lane == first_expert[0] + at
    gate = jnp.sum(jnp.where(mine, gates[...], 0.0), axis=1, keepdims=True)
    grad_col = jnp.zeros((rows, 1), F32)
    for start in range(0, ff, TILE):
        tile = slice(start, start + TILE)
        up_tile = slice(ff + start, ff + start + TILE)
        gate_part = dot(second[...], in_w[0, :, tile])
        up_part = dot(second[...], in_w[0, :, up_tile])
        came = dot_nt(side[:, :width], down_w[0, tile, :])
        sigmoid_gate = 0.5 * jnp.tanh(0.5 * gate_part) + 0.5
        silu_gate = gate_part * sigmoid_gate
        hidden = (silu_gate * up_part).astype(BF16).astype(F32)
        grad_col += jnp.sum(hidden * came, axis=1, keepdims=True)
        gated[:, tile] = (hidden * gate).astype(BF16)
        gated_t[0, tile, :] = gated[:, tile].T
        grad_hidden = came * gate
        slope = sigmoid_gate + silu_gate * (1.0 - sigmoid_gate)
        grad_both[0, :, tile] = (grad_hidden * up_part * slope).astype(BF16)
        grad_both[0, :, up_tile] = (grad_hidden * silu_gate).astype(BF16)
    grad_gates[...] += jnp.where(mine, grad_col, 0.0)
    for start in range(0, width, TILE):
        tile = slice(start, start + TILE)
        comb_sum[:, tile] += dot(gated[...], down_w[0, :, tile])
        back_sum[:, tile] += dot_nt(grad_both[0], in_w[0, tile, :])

    @pl.when(at == pl.num_programs(0) - 1)
    def _():
        comb[...] = comb_sum[...].astype(BF16)
        back[:, :width] = back_sum[...].astype(BF16)
        high = grad_gates[...].astype(BF16).astype(F32)
        back[:, width:] = (high + pltpu.roll(grad_gates[...] - high, EXPERTS, 1)).astype(BF16)


def expert_block(first_expert, second, side, small, in_w, down_w, place, count, before):
    rows, width = second.shape
    experts, ff = down_w.shape[:2]
    whole = lambda *shape: pl.BlockSpec(shape, lambda e: (0,) * len(shape))
    in_specs = [
        pl.BlockSpec(memory_space=pltpu.SMEM),
        whole(rows, width),
        whole(*side.shape),
        whole(*small.shape),
        pl.BlockSpec((1, width, 2 * ff), lambda e: (e, 0, 0)),
        pl.BlockSpec((1, ff, width), lambda e: (e, 0, 0)),
    ] + [pl.BlockSpec(memory_space=pl.ANY)] * len(before)
    out_specs = [
        pl.BlockSpec((1, ff, rows), lambda e: (e, 0, place)),
        pl.BlockSpec((1, rows, 2 * ff), lambda e: (e, place, 0)),
        pl.BlockSpec((width, rows), lambda e: (0, place)),
        pl.BlockSpec((rows, width), lambda e: (place, 0)),
        whole(rows, width),
        whole(*side.shape),
    ]
    outs = [
        shape_of((experts, ff, count * rows), BF16),
        shape_of((experts, count * rows, 2 * ff), BF16),
        shape_of((width, count * rows), BF16),
        shape_of((count * rows, width), BF16),
        shape_of((rows, width), BF16),
        shape_of(side.shape, BF16),
    ]
    return pl.pallas_call(
        lambda *refs: expert_kernel(bool(before), *refs),
        grid=(experts,),
        out_shape=outs,
        in_specs=in_specs,
        out_specs=out_specs,
        scratch_shapes=[
            pltpu.VMEM((rows, PAD), F32),
            pltpu.VMEM((rows, PAD), F32),
            pltpu.VMEM((rows, width), F32),
            pltpu.VMEM((rows, width), F32),
            pltpu.VMEM((rows, ff), BF16),
        ],
        input_output_aliases={6: 0, 7: 1, 8: 2, 9: 3} if before else {},
        compiler_params=pltpu.CompilerParams(
            vmem_limit_bytes=VMEM_BYTES, dimension_semantics=("arbitrary",)
        ),
        cost_estimate=LIGHT,
    )(first_expert, second, side, small, in_w, down_w, *before)


def weight_kernel(base, second_t, dy, gated_t, grad_both, *outs):
    def fill(grad_in, grad_down):
        for start in range(0, grad_in.shape[1], 2 * TILE):
            tile = slice(start, start + 2 * TILE)
            grad_in[:, tile] = dot(second_t[...], grad_both[0, :, tile]).astype(BF16)
            grad_down[:, tile] = dot(gated_t[0], dy[:, tile]).astype(BF16)

    early = pl.program_id(0) < pl.num_programs(0) // 2
    pl.when(early)(lambda: fill(*outs[:2]))
    pl.when(jnp.logical_not(early))(lambda: fill(*outs[2:]))


def weight_block(base, second_t, dy, gated_t, grad_both):
    width, rows = second_t.shape
    experts, ff = gated_t.shape[:2]
    half = experts // 2
    first = lambda e, at: (jnp.minimum(e, half - 1), 0)
    last = lambda e, at: (jnp.maximum(e - half, 0), 0)
    grid_spec = pltpu.PrefetchScalarGridSpec(
        num_scalar_prefetch=1,
        grid=(experts,),
        in_specs=[
            pl.BlockSpec((width, rows), lambda e, at: (0, 0)),
            pl.BlockSpec((rows, width), lambda e, at: (0, 0)),
            pl.BlockSpec((1, ff, rows), lambda e, at: ((at[0] + e) % experts, 0, 0)),
            pl.BlockSpec((1, rows, 2 * ff), lambda e, at: ((at[0] + e) % experts, 0, 0)),
        ],
        out_specs=[
            pl.BlockSpec((width, 2 * ff), first),
            pl.BlockSpec((ff, width), first),
            pl.BlockSpec((width, 2 * ff), last),
            pl.BlockSpec((ff, width), last),
        ],
    )
    pair = [shape_of((half * width, 2 * ff), BF16), shape_of((half * ff, width), BF16)]
    return pl.pallas_call(
        weight_kernel,
        grid_spec=grid_spec,
        out_shape=pair * 2,
        compiler_params=pltpu.CompilerParams(
            vmem_limit_bytes=VMEM_BYTES, dimension_semantics=("arbitrary",)
        ),
        cost_estimate=LIGHT,
    )(base[None].astype(jnp.int32), second_t, dy, gated_t, grad_both)


def shift(block, count, step):
    return lax.ppermute(block, "shard", [(at, (at + step) % count) for at in range(count)])


def tie(*values):
    return lax.optimization_barrier(values)


def gather_near(piece, count):
    got = {0: piece}
    right = left = piece
    for step in range(1, (count - 1) // 2 + 1):
        right, left = shift(right, count, 1), shift(left, count, -1)
        got[step], got[count - step] = right, left
    return got, right, left


def gather_far(right, left, count):
    half = right.shape[0] // 2
    return shift(right[:half], count, 1), shift(left[half:], count, -1)


def far_first(parts, count):
    half = parts[0].shape[0] // 2
    far = parts[count // 2]
    return shift(far[:half], count, -1), shift(far[half:], count, 1)


def near_rest(parts, left, right, count):
    half = parts[0].shape[0] // 2
    if count == 2:
        return jnp.concatenate([left, right], axis=0), jnp.zeros_like(parts[0])
    for step in reversed(range(1, count // 2)):
        near, far = parts[step], parts[count - step]
        if step == count // 2 - 1:
            left = jnp.concatenate([add_low(near[:half], left), near[half:]], axis=0)
            right = jnp.concatenate([far[:half], add_low(far[half:], right)], axis=0)
        else:
            left, right = add_low(near, left), add_low(far, right)
        left, right = shift(left, count, -1), shift(right, count, 1)
    return left, right


def add_low(a, b):
    return (a.astype(F32) + b.astype(F32)).astype(BF16)


def across(block, reps, bit):
    return lax.ppermute(block, "rep", [(at, at ^ 2**bit) for at in range(reps)])


def part_of(block, index):
    half = block.shape[0] // 2
    return lax.dynamic_slice_in_dim(block, index * half, half, axis=0)


def last_orders(bits):
    return [order[:-1] for order in orders_of(bits)]


def both_halves(mine, other, index):
    first = jnp.where(index == 0, mine, other)
    last = jnp.where(index == 0, other, mine)
    return jnp.concatenate([first, last])


def orders_of(bits):
    return list(range(1, bits)), list(range(1, bits))[::-1]


def sent(block, reps, bit, bit_of):
    return across(part_of(block, 1 - bit_of[bit]), reps, bit)


def kept_sum(block, came, bit, bit_of):
    return add_low(part_of(block, bit_of[bit]), came)


def place_kernel(begin, cut, half, upper, lower, *refs):
    at = begin + pl.program_id(0)

    @pl.when(at < cut)
    def _():
        refs[-1][...] = upper[...].astype(F32)

    @pl.when(at >= cut)
    def _():
        refs[-1][...] = lower[...].astype(F32)


def place_half(upper, lower, begin, rows, target, index):
    step = math.gcd(2 * TILE, upper.shape[0], begin, rows)
    cut, width = upper.shape[0] // step, upper.shape[1]
    first, blocks = begin // step, rows // step
    grid_spec = pltpu.PrefetchScalarGridSpec(
        num_scalar_prefetch=1,
        grid=(blocks,),
        in_specs=[
            pl.BlockSpec((step, width), lambda at, half: (jnp.minimum(first + at, cut - 1), 0)),
            pl.BlockSpec((step, width), lambda at, half: (jnp.maximum(first + at - cut, 0), 0)),
        ]
        + [pl.BlockSpec(memory_space=pl.ANY)] * (target is not None),
        out_specs=pl.BlockSpec((step, width), lambda at, half: (half[0] * blocks + at, 0)),
    )
    return pl.pallas_call(
        lambda *refs: place_kernel(first, cut, *refs),
        grid_spec=grid_spec,
        out_shape=shape_of((2 * rows, width), F32),
        input_output_aliases={} if target is None else {3: 0},
        compiler_params=pltpu.CompilerParams(
            vmem_limit_bytes=VMEM_BYTES, dimension_semantics=("arbitrary",)
        ),
        cost_estimate=LIGHT,
    )(index[None].astype(jnp.int32), upper, lower, *([] if target is None else [target]))


def shards(
    tokens,
    doc_ids,
    routes,
    norm_in_gain,
    w_query,
    w_key,
    w_value,
    w_out,
    norm_mid_gain,
    w_router,
    w_expert_in,
    w_expert_down,
    cotangent,
):
    bf16, f32 = BF16, F32
    row_count, model_width = tokens.shape
    query_cols = w_query.shape[1]
    kv_cols = w_key.shape[1]
    own_rows = w_query.shape[0]
    own_experts, ff = w_expert_down.shape[:2]
    shard_at = lax.axis_index("shard")
    reps, shard_count = (lax.axis_size("rep"), lax.axis_size("shard"))

    small = jnp.concatenate(
        [
            w_router,
            norm_in_gain[:, None],
            norm_mid_gain[:, None],
            jnp.zeros((own_rows, PAD - EXPERTS - 2), bf16),
        ],
        axis=1,
    )
    weights = [w_query, w_key, w_value, w_out, small]
    all_w, side, side_right, side_left = gather_all(
        weights, cotangent, routes, reps, shard_count, 1
    )
    small_at = query_cols + 2 * kv_cols + w_out.shape[1]

    cosine, sine_table = rotary_tables(positions(doc_ids), HEAD_DIM)
    cosine, sine_table = cosine[:, 0, :], sine_table[:, 0, :]
    ct = jnp.concatenate([cosine] * 4, axis=1)
    st = jnp.concatenate([-sine_table, sine_table] * 2, axis=1)
    top = shard_count - 1
    wraps = [lax.ppermute(side, "shard", [pair]) for pair in ((top, 0), (0, top))]
    second_low, middle, *kept = forward_block(
        tokens, all_w, ct, st, doc_ids, query_cols, kv_cols
    )
    second_low, wraps = tie(second_low, wraps)
    far_at = shard_count // 2
    side_parts = {0: side}
    second_parts, *ends = gather_near(second_low, shard_count)
    first_expert = (shard_at * own_experts)[None].astype(jnp.int32)
    order = sorted(range(shard_count), key=lambda k: min(k, shard_count - k))
    small_full = all_w[:, small_at:]
    combs, backs, kept_parts = {}, {}, ()
    for place, k in enumerate(order):
        *kept_parts, combs[k], backs[k] = expert_block(
            first_expert,
            second_parts[k],
            side_parts[k],
            small_full,
            w_expert_in,
            w_expert_down,
            place,
            shard_count,
            kept_parts,
        )
        if k == 0:
            kept_parts, wraps, side_right, side_left = tie(kept_parts, wraps, side_right, side_left)
            side_right = jnp.where(shard_at == 0, wraps[0], side_right)
            side_left = jnp.where(shard_at == top, wraps[1], side_left)
            for step in range(1, (shard_count - 1) // 2 + 1):
                if step > 1:
                    side_right = shift(side_right, shard_count, 1)
                    side_left = shift(side_left, shard_count, -1)
                side_parts[step], side_parts[shard_count - step] = side_right, side_left
            kept_parts, second_parts, ends, side_right, side_left = tie(
                kept_parts, second_parts, ends, side_right, side_left
            )
            second_parts[far_at] = jnp.concatenate(gather_far(*ends, shard_count))
            side_parts[far_at] = jnp.concatenate(gather_far(side_right, side_left, shard_count))
    back_far = far_first(backs, shard_count)
    gated_t, grad_both, second_t, dy_all = kept_parts

    rep_at = lax.axis_index("rep")
    bits = reps.bit_length() - 1
    bit_of = [rep_at // 2**bit % 2 for bit in range(bits)]
    half = own_experts // 2
    grads = (second_t, dy_all, gated_t, grad_both)
    *away, mine_in, mine_down = weight_block((1 - bit_of[0]) * half, *grads)
    mine = (mine_in, mine_down)
    away, back_far, backs = tie(away, back_far, backs)
    back_near = near_rest(backs, *back_far, shard_count)
    core = [across(part, reps, 0) for part in away]
    in_rows, down_rows = [part.shape[0] for part in mine]
    cut = (in_rows + down_rows) // 2
    held_in, held_down = [add_low(a, b) for a, b in zip(mine, core)]
    blocks = [held_in[:cut], jnp.concatenate([held_in[cut:], held_down])]
    block_orders = orders_of(bits)
    steps = bits - 1

    def begin(at, blocks):
        return [sent(b, reps, o[at], bit_of) for b, o in zip(blocks, block_orders)]

    def finish(at, blocks, came):
        return [kept_sum(b, c, o[at], bit_of) for b, c, o in zip(blocks, came, block_orders)]

    came = begin(0, blocks)
    back_near, came, blocks, combs = tie(back_near, came, blocks, combs)
    blocks = finish(0, blocks, came)
    back_near, blocks, combs = tie(back_near, blocks, combs)
    came = begin(1, blocks)
    comb_far = far_first(combs, shard_count)
    middle_back = backward_block(
        tokens, side, middle, second_low, (backs[0], *back_near), all_w, ct, st, doc_ids, kept
    )
    middle_back, came, comb_far, blocks, combs = tie(middle_back, came, comb_far, blocks, combs)
    comb_near = near_rest(combs, *comb_far, shard_count)
    blocks = finish(1, blocks, came)
    for at in range(2, steps):
        blocks = finish(at, blocks, begin(at, blocks))
    middle_back, blocks = tie(middle_back, blocks)
    last_bits = [order[-1] for order in block_orders]
    came = [across(b, reps, bit) for b, bit in zip(blocks, last_bits)]
    grad_out, rows_t, grad_middle, grad_pre = middle_back
    joint, grad_tokens = finish_block(
        tokens, all_w, grad_middle, grad_pre, grad_out, rows_t, kept[0]
    )
    joint, came, blocks = tie(joint, came, blocks)
    blocks = [both_halves(b, c, bit_of[bit]) for b, c, bit in zip(blocks, came, last_bits)]
    joint_own, blocks = reduce_all(joint, *blocks, reps, shard_count, 3)
    joint_own, blocks, comb_near = tie(joint_own, blocks, comb_near)
    mixed = middle + combs[0].astype(f32) + sum(part.astype(f32) for part in comb_near)
    mixed = mixed.astype(bf16)
    others = [across(b, reps, 0) for b in blocks]
    grad_in_own = place_half(*blocks, 0, in_rows, None, bit_of[0])
    grad_down_own = place_half(*blocks, in_rows, down_rows, None, bit_of[0])
    grad_in_own = place_half(*others, 0, in_rows, grad_in_own, 1 - bit_of[0])
    grad_down_own = place_half(*others, in_rows, down_rows, grad_down_own, 1 - bit_of[0])
    widths = (query_cols, kv_cols, kv_cols, w_out.shape[1], PAD)
    query_own, key_own, value_own, out_own, small_own = local_call(
        split_kernel, [shape_of((own_rows, wide), f32) for wide in widths], [], joint_own
    )
    return (
        mixed,
        grad_tokens,
        small_own[:, EXPERTS],
        query_own,
        key_own,
        value_own,
        out_own,
        small_own[:, EXPERTS + 1],
        small_own[:, :EXPERTS],
        grad_in_own.reshape(own_experts, model_width, 2 * ff),
        grad_down_own.reshape(own_experts, ff, model_width),
    )


def solution(mesh):
    in_specs = (
        P(("rep", "shard"), None),
        P(("rep", "shard")),
        P(("rep", "shard"), None),
        P("shard"),
        P("shard", None),
        P("shard", None),
        P("shard", None),
        P("shard", None),
        P("shard"),
        P("shard", None),
        P("shard", None, None),
        P("shard", None, None),
        P(("rep", "shard"), None),
    )
    out_specs = (
        P(("rep", "shard"), None),
        P(("rep", "shard"), None),
        P("shard"),
        P("shard", None),
        P("shard", None),
        P("shard", None),
        P("shard", None),
        P("shard"),
        P("shard", None),
        P("shard", None, None),
        P("shard", None, None),
    )
    return jax.shard_map(shards, mesh=mesh, in_specs=in_specs, out_specs=out_specs, check_vma=False)
```
